32 devices in a mesh: dp: 4 (over y, x), fsdp: 8 (over z, core).
Axes of the slice: x: 2, y: 2, z: 4, core: 2. Of those that a mesh axis runs over, the one named last changes fastest.
Arguments:
- hidden: bfloat16 [50176, 768], P(('dp', 'fsdp')), may hold values from -6 to 6
- cotangent: bfloat16 [50176, 768], P(('dp', 'fsdp')), may hold values from -6 to 6
- drive_weight: bfloat16 [4608, 128], P(('dp', 'fsdp')), may hold values from -0.21875 to 0.21875
- forget_weight: bfloat16 [2304, 128], P(('dp', 'fsdp')), may hold values from -0.21875 to 0.21875
- outgate_weight: bfloat16 [4608, 128], P(('dp', 'fsdp')), may hold values from -0.21875 to 0.21875
- mixout_weight: bfloat16 [4608, 128], P(('dp', 'fsdp')), may hold values from -0.4375 to 0.4375
- gate_weight: bfloat16 [9216, 128], P(('dp', 'fsdp')), may hold values from -0.21875 to 0.21875
- up_weight: bfloat16 [9216, 128], P(('dp', 'fsdp')), may hold values from -0.21875 to 0.21875
- down_weight: bfloat16 [9216, 128], P(('dp', 'fsdp')), may hold values from -0.21875 to 0.21875
- first_gain: bfloat16 [768], P(('dp', 'fsdp')), may hold values from 0.099609375 to 1.8984375
- second_gain: bfloat16 [768], P(('dp', 'fsdp')), may hold values from 0.099609375 to 1.8984375
- group_gain: bfloat16 [768], P(('dp', 'fsdp')), may hold values from 0.099609375 to 1.8984375
- forget_bias: bfloat16 [384], P(('dp', 'fsdp')), may hold values from -1 to 6
- phase_angle: bfloat16 [384], P(('dp', 'fsdp')), may hold values from -3.140625 to 3.140625
Outputs:
- layer_out: bfloat16 [50176, 768], P(('dp', 'fsdp'))
- hidden_grad: float32 [50176, 768], P(('dp', 'fsdp'))
- drive_grad: float32 [4608, 128], P(('dp', 'fsdp'))
- forget_grad: float32 [2304, 128], P(('dp', 'fsdp'))
- outgate_grad: float32 [4608, 128], P(('dp', 'fsdp'))
- mixout_grad: float32 [4608, 128], P(('dp', 'fsdp'))
- gate_grad: float32 [9216, 128], P(('dp', 'fsdp'))
- up_grad: float32 [9216, 128], P(('dp', 'fsdp'))
- down_grad: float32 [9216, 128], P(('dp', 'fsdp'))
- firstgain_grad: float32 [768], P(('dp', 'fsdp'))
- secondgain_grad: float32 [768], P(('dp', 'fsdp'))
- groupgain_grad: float32 [768], P(('dp', 'fsdp'))
- bias_grad: float32 [384], P(('dp', 'fsdp'))
- phase_grad: float32 [384], P(('dp', 'fsdp'))
The draws below stay inside these ranges and needn't reach their ends.
All inputs are finite; a program needn't handle non-finite values.
Results may differ from the reference program's by a relative error of at most 0.013.
Values may be sent and summed in bfloat16 or wider, within the bound.
A program may use at most 256 MiB of HBM per device.

```python
import jax
import jax.numpy as jnp
from jax import lax

D = 768
C = 384
FF = 1536
SEQ = 1568
SPAN = 56
GROUPS = 8
TOKENS = 50176


def block_levels(rng, extent, cuts, low, top_value):
    loudness = 1.0
    for axis_at, blocks in cuts:
        steps = jax.random.uniform(jax.random.fold_in(jax.random.fold_in(rng, 6), axis_at), (blocks,), jnp.float32, low / len(cuts), top_value / len(cuts))
        loudness = loudness * jnp.repeat(jnp.exp(steps), extent[axis_at] // blocks).reshape((-1,) + (1,) * (len(extent) - 1 - axis_at))
    return loudness


def centred(rng, dims, spread, bound, split=(), kind=jnp.bfloat16):
    values = jax.random.normal(rng, dims, jnp.float32) * spread
    if len(split) > 0:
        values = block_levels(rng, dims, split, -0.22, 0.18) * values
    return jnp.clip(values, min=-bound, max=bound).astype(kind)


def setup_inputs(seed: int = 0) -> dict:
    seeds = jax.random.split(jax.random.key(seed), 15)
    hidden = centred(seeds[0], (TOKENS, D), 1.0, 6.0, ((0, 32),))
    cotangent = centred(seeds[1], (TOKENS, D), 1.0, 6.0, ((0, 32),))
    drive_weight = centred(seeds[2], (D * D // 128, 128), D ** -0.5, 0.21875, ((0, 32),))
    forget_weight = centred(seeds[3], (D * C // 128, 128), D ** -0.5, 0.21875, ((0, 32),))
    outgate_weight = centred(seeds[4], (D * D // 128, 128), D ** -0.5, 0.21875, ((0, 32),))
    mixout_weight = centred(seeds[5], (D * D // 128, 128), (D // 4) ** -0.5, 0.4375, ((0, 32),))
    gate_weight = centred(seeds[6], (D * FF // 128, 128), D ** -0.5, 0.21875, ((0, 32),))
    up_weight = centred(seeds[7], (D * FF // 128, 128), D ** -0.5, 0.21875, ((0, 32),))
    down_weight = centred(seeds[8], (FF * D // 128, 128), (FF // 2) ** -0.5, 0.21875, ((0, 32),))
    first_gain = jnp.clip(1.0 + 0.18 * jax.random.normal(seeds[9], (D,), jnp.float32), 0.099609375, 1.8984375).astype(jnp.bfloat16)
    second_gain = jnp.clip(1.0 + 0.18 * jax.random.normal(seeds[10], (D,), jnp.float32), 0.099609375, 1.8984375).astype(jnp.bfloat16)
    group_gain = jnp.clip(1.0 + 0.18 * jax.random.normal(seeds[11], (D,), jnp.float32), 0.099609375, 1.8984375).astype(jnp.bfloat16)
    forget_bias = jnp.clip(-1.0 + 7.0 * jax.random.uniform(seeds[12], (C,), jnp.float32) ** block_levels(seeds[12], (C,), ((0, 32),), -0.2, 0.2), -1.0, 6.0).astype(jnp.bfloat16)
    phase_angle = jnp.clip(jax.random.uniform(seeds[13], (C,), jnp.float32, -3.140625, 3.140625), -3.140625, 3.140625).astype(jnp.bfloat16)
    return dict(hidden=hidden, cotangent=cotangent, drive_weight=drive_weight, forget_weight=forget_weight, outgate_weight=outgate_weight, mixout_weight=mixout_weight, gate_weight=gate_weight, up_weight=up_weight, down_weight=down_weight, first_gain=first_gain, second_gain=second_gain, group_gain=group_gain, forget_bias=forget_bias, phase_angle=phase_angle)


lower_bound = 0.25
norm_eps = 1e-06
group_eps = 1e-05

@jax.custom_vjp
def low(v):
    return lax.optimization_barrier(v.astype(jnp.bfloat16)).astype(jnp.float32)

@jax.custom_vjp
def low_back(v):
    return v

def low_keep(v):
    return (low(v), None)

def low_pass(kept, grad):
    return (grad,)

def back_keep(v):
    return (v, None)

def back_low(kept, grad):
    return (low(grad),)
low.defvjp(low_keep, low_pass)
low_back.defvjp(back_keep, back_low)

def exact_dot(left, right):
    return jnp.dot(left, right, precision=lax.Precision.HIGHEST)

def rms_scale(values, gain_vec):
    return values * lax.rsqrt(lax.optimization_barrier(jnp.mean(values * values, axis=1, keepdims=True)) + norm_eps) * gain_vec

def combine(earlier, later_term):
    return (later_term[0] * earlier[0] - later_term[1] * earlier[1], later_term[0] * earlier[1] + later_term[1] * earlier[0], later_term[0] * earlier[2] - later_term[1] * earlier[3] + later_term[2], later_term[0] * earlier[3] + later_term[1] * earlier[2] + later_term[3])

def mixer_core(drive_pre, forget_pre, outgate_pre, phase_angle, forget_bias, group_gain):
    length = drive_pre.shape[0]
    features = drive_pre.shape[1]
    channels = features // 2
    blocks = length // SPAN
    driven = jax.nn.silu(drive_pre)
    retain = lower_bound + (1.0 - lower_bound) * jax.nn.sigmoid(forget_pre + forget_bias)
    rotate_re = retain * jnp.cos(phase_angle)
    rotate_im = retain * jnp.sin(phase_angle)
    inflow = 1.0 - retain
    source_re = inflow * driven[:, :channels]
    source_im = inflow * driven[:, channels:]
    pieces = tuple((member.reshape(blocks, SPAN, channels) for member in (rotate_re, rotate_im, source_re, source_im)))

    def advance(carried, block_terms):
        summed = lax.associative_scan(combine, block_terms, axis=0)
        state_re = summed[0] * carried[0] - summed[1] * carried[1] + summed[2]
        state_im = summed[0] * carried[1] + summed[1] * carried[0] + summed[3]
        return ((state_re[-1], state_im[-1]), (state_re, state_im))
    initial = (jnp.zeros((channels,), jnp.float32), jnp.zeros((channels,), jnp.float32))
    _, (states_re, states_im) = lax.scan(jax.checkpoint(advance), initial, pieces)
    joined = jnp.concatenate([states_re.reshape(length, channels), states_im.reshape(length, channels)], axis=1)
    grouped = joined.reshape(length, GROUPS, features // GROUPS)
    centered = grouped - lax.optimization_barrier(jnp.mean(grouped, axis=2, keepdims=True))
    normed = centered * lax.rsqrt(lax.optimization_barrier(jnp.mean(centered * centered, axis=2, keepdims=True)) + group_eps)
    return normed.reshape(length, features) * group_gain * jax.nn.sigmoid(outgate_pre)

def layer_forward(inputs, params):
    drive_matrix, forget_matrix, outgate_matrix, mixout_matrix, gate_matrix, up_matrix, down_matrix, first_gain, second_gain, group_gain, forget_bias, phase_angle = params
    normed_one = low(rms_scale(inputs, first_gain))
    drive_pre = low_back(exact_dot(normed_one, drive_matrix))
    forget_pre = low_back(exact_dot(normed_one, forget_matrix))
    outgate_pre = low_back(exact_dot(normed_one, outgate_matrix))
    mixed = low(mixer_core(drive_pre, forget_pre, outgate_pre, phase_angle, forget_bias, group_gain))
    middle = inputs + low_back(exact_dot(mixed, mixout_matrix))
    normed_two = low(rms_scale(middle, second_gain))
    gate_pre = low_back(exact_dot(normed_two, gate_matrix))
    up_pre = low_back(exact_dot(normed_two, up_matrix))
    hidden_units = low(jax.nn.silu(gate_pre) * up_pre)
    return middle + exact_dot(hidden_units, down_matrix)

def reference(hidden, cotangent, drive_weight, forget_weight, outgate_weight, mixout_weight, gate_weight, up_weight, down_weight, first_gain, second_gain, group_gain, forget_bias, phase_angle):
    targets = ((D, D), (D, C), (D, D), (D, D), (D, FF), (D, FF), (FF, D))
    weights = (drive_weight, forget_weight, outgate_weight, mixout_weight, gate_weight, up_weight, down_weight)
    matrices = tuple((weight.astype(jnp.float32).reshape(target) for weight, target in zip(weights, targets)))
    vectors = tuple((member.astype(jnp.float32) for member in (first_gain, second_gain, group_gain, forget_bias, phase_angle)))
    params = matrices + vectors
    seq_count = hidden.shape[0] // SEQ
    inputs_all = hidden.astype(jnp.float32).reshape(seq_count, SEQ, D)
    tangents_all = cotangent.astype(jnp.float32).reshape(seq_count, SEQ, D)

    def one_sequence(totals, seq_pair):
        result, pullback = jax.vjp(layer_forward, seq_pair[0], params)
        input_grad, param_grads = pullback(seq_pair[1])
        return (jax.tree.map(jnp.add, totals, param_grads), (result.astype(jnp.bfloat16), input_grad))
    zero_grads = jax.tree.map(jnp.zeros_like, params)
    totals, (outputs, input_grads) = lax.scan(one_sequence, zero_grads, (inputs_all, tangents_all))
    return (outputs.reshape(-1, D), input_grads.reshape(-1, D), totals[0].reshape(-1, 128), totals[1].reshape(-1, 128), totals[2].reshape(-1, 128), totals[3].reshape(-1, 128), totals[4].reshape(-1, 128), totals[5].reshape(-1, 128), totals[6].reshape(-1, 128), totals[7], totals[8], totals[9], totals[10], totals[11])
```

```python
import functools

import jax
import jax.numpy as jnp
from jax import lax
from jax.experimental import pallas as pl
from jax.experimental.pallas import tpu as pltpu
from jax.sharding import PartitionSpec as P

D = 768
C = 384
FF = 1536
GROUPS = 8
NB = D // 128
CB = C // 128

lower_bound = 0.25
norm_eps = 1e-06
group_eps = 1e-05

F32 = jnp.float32
BF16 = jnp.bfloat16
MESH = pl.DeviceIdType.MESH
MIB = 2**20

DRIVE = (0, 24, 6)
OUTGATE = (144, 24, 6)
FORGET = (288, 24, 3)
VECTORS = 360
MIXOUT = (368, 24, 6)
GATE = (512, 24, 12)
UP = (800, 24, 12)
DOWN = (1088, 48, 6)
ROWS = 1376
VECTOR_PARTS = ((0, 24), (24, 24), (48, 24), (72, 12), (84, 12))
WDFG = 2 * D + C

TILE = 224
SEGMENTS = 16


def sigmoid(t):
    return 0.5 * jnp.tanh(0.5 * t) + 0.5


def product(left, right):
    return jnp.dot(left, right, preferred_element_type=F32)


def back_product(left, right):
    return lax.dot_general(left, right, (((1,), (1,)), ((), ())), preferred_element_type=F32)


def outer_sum(left, right):
    return lax.dot_general(left, right, (((0,), (0,)), ((), ())), preferred_element_type=F32)


def coords():
    dp = lax.axis_index("dp")
    fsdp = lax.axis_index("fsdp")
    return dp // 2, dp % 2, fsdp // 2, fsdp % 2


def device(y, x, z, core):
    return (y * 2 + x, z * 2 + core)


class Places:
    def __init__(self):
        y, x, z, c = coords()
        self.z, self.core = z, c
        fy = jnp.where(c == 0, 1 - y, y)
        fx = jnp.where(c == 0, x, 1 - x)
        sy = jnp.where(c == 0, y, 1 - y)
        sx = jnp.where(c == 0, 1 - x, x)
        self.first = device(fy, fx, z, c)
        self.second = device(sy, sx, z, c)
        self.sibling = device(y, x, z, 1 - c)
        self.pair = device(y, x, z ^ 1, c)
        self.along = [device(y, x, (z + d) % 4, c) for d in (1, 2, 3)]
        self.col = (y * 2 + x) * 4
        self.fcol = (fy * 2 + fx) * 4
        self.scol = (sy * 2 + sx) * 4
        self.dcol = ((1 - y) * 2 + (1 - x)) * 4
        self.half = (z % 2) * 2
        self.chip = self.col + z

    def barrier(self):
        bar = pltpu.get_barrier_semaphore()
        for partner in [self.first, self.second, self.sibling] + self.along:
            pl.semaphore_signal(bar, inc=1, device_id=partner, device_id_type=MESH)
        pl.semaphore_wait(bar, 6)


class Gather:
    def __init__(self, places, raw, cuts, sems):
        self.at, self.raw, self.cuts = places, raw, cuts
        self.zs, self.zr, self.fs, self.fr, self.ss, self.sr, self.ps, self.pr, self.cs, self.cr = sems
        self.ops = {}

    @staticmethod
    def semaphores(k):
        dma = pltpu.SemaphoreType.DMA
        return [dma((k, 3)), dma((k, 3)), dma((k,)), dma((k,)), dma((k, 2)), dma((k, 2)), dma((k,)), dma((k,)), dma((k, 5)), dma((k, 5))]

    def send(self, key, first, count, k, send_sem, recv_sem, target):
        low, high = self.cuts[k]
        ref = self.raw.at[self.at.core, pl.ds(first, count), low:high]
        copy = pltpu.make_async_remote_copy(
            src_ref=ref, dst_ref=ref, send_sem=send_sem, recv_sem=recv_sem, device_id=target, device_id_type=MESH
        )
        copy.start()
        self.ops[(key, k)] = copy

    def along(self, k):
        for d in range(3):
            self.send(f"z{d}", self.at.chip, 1, k, self.zs.at[k, d], self.zr.at[k, d], self.at.along[d])

    def column(self, k):
        for d in range(3):
            self.ops[(f"z{d}", k)].wait_recv()
        at = self.at
        self.send("f", at.col, 4, k, self.fs.at[k], self.fr.at[k], at.first)
        self.send("s", at.col, 4, k, self.ss.at[k, 0], self.sr.at[k, 0], at.second)
        self.send("c0", at.col, 4, k, self.cs.at[k, 0], self.cr.at[k, 0], at.sibling)

    def plane(self, k):
        at = self.at
        self.ops[("f", k)].wait_recv()
        self.send("s2", at.fcol + at.half, 2, k, self.ss.at[k, 1], self.sr.at[k, 1], at.second)
        self.send("c1", at.fcol, 4, k, self.cs.at[k, 1], self.cr.at[k, 1], at.sibling)
        self.ops[("s", k)].wait_recv()
        self.send("c2", at.scol, 4, k, self.cs.at[k, 2], self.cr.at[k, 2], at.sibling)

    def diagonal(self, k):
        at = self.at
        self.ops[("s2", k)].wait_recv()
        self.send("p", at.dcol + at.half, 2, k, self.ps.at[k], self.pr.at[k], at.pair)
        self.send("c3", at.dcol + at.half, 2, k, self.cs.at[k, 3], self.cr.at[k, 3], at.sibling)

    def rest(self, k):
        at = self.at
        self.ops[("p", k)].wait_recv()
        self.send("c4", at.dcol + 2 - at.half, 2, k, self.cs.at[k, 4], self.cr.at[k, 4], at.sibling)

    def whole(self, k):
        for i in range(5):
            self.ops[(f"c{i}", k)].wait_recv()

    def finish(self):
        for copy in self.ops.values():
            copy.wait_send()


GATHER_SIZES = (144, 144, 80, 144, 144, 144, 144, 144, 144, 144)


def cuts_of(sizes):
    cuts, start = [], 0
    for size in sizes:
        cuts.append((start, start + size))
        start += size
    return cuts


def pack(weight_ref, stage, blocks):
    rows = weight_ref.shape[0]
    stage[0:rows] = weight_ref[...].astype(F32)
    each = rows // blocks
    return jnp.concatenate([stage[pl.ds(j, each, stride=blocks)] for j in range(blocks)], axis=0)


def assemble(raw, part, target, column):
    first, rows, blocks = part
    total = -(-rows * blocks // 16) * 16

    def one(chip, _):
        pair = [raw[core, chip, first : first + total].astype(F32) for core in (0, 1)]
        for j in range(blocks):
            block = jnp.concatenate([member[j * rows : (j + 1) * rows] for member in pair], axis=0)
            target[pl.ds(pl.multiple_of(chip * (2 * rows), 16), 2 * rows), column + j * 128 : column + (j + 1) * 128] = (
                block.astype(BF16)
            )
        return 0

    lax.fori_loop(0, 16, one, 0)


def spread(lane, width, total, by_row):
    col = lax.broadcasted_iota(jnp.int32, (128, total), 1).astype(F32)
    row = lax.broadcasted_iota(jnp.int32, (128, total), 0).astype(F32)
    within = col - width * jnp.floor((col + 0.5) * (1.0 / width))
    return jnp.where(row == within + lane, 1.0, 0.0).astype(BF16)


def own_columns(width, total):
    col = lax.broadcasted_iota(jnp.int32, (32, total), 1)
    low = lax.broadcasted_iota(jnp.int32, (32, total), 0) * width
    return jnp.logical_and(col >= low, col < low + width)


def vector_of(rows, lane, width):
    total = 32 * width
    placed = product(rows, spread(lane, width, total, True))
    return jnp.sum(jnp.where(own_columns(width, total), placed, 0.0), axis=0, keepdims=True)


def col(c):
    return slice(c * 128, (c + 1) * 128)


def scan_forward(length, lam, src, out, cos, sin, carry):
    steps = length // SEGMENTS
    zero = jnp.zeros((SEGMENTS, 128), F32)

    def rows(j):
        return pl.ds(j, SEGMENTS, stride=steps)

    def first(j, kept):
        prod, re, im = kept
        new_p, new_re, new_im = [], [], []
        for c in range(CB):
            gate = lam[c, rows(j)]
            a, b = gate * cos[:, col(c)], gate * sin[:, col(c)]
            new_p.append(prod[c] * gate)
            new_re.append(a * re[c] - b * im[c] + src[c, rows(j)])
            new_im.append(a * im[c] + b * re[c] + src[CB + c, rows(j)])
        return tuple(new_p), tuple(new_re), tuple(new_im)

    ones = (jnp.ones((SEGMENTS, 128), F32),) * CB
    prod, re, im = lax.fori_loop(0, steps, first, (ones, (zero,) * CB, (zero,) * CB))
    turn_re, turn_im = turned(cos, sin, steps)
    for c in range(CB):
        p_re, p_im = prod[c] * turn_re[:, col(c)], prod[c] * turn_im[:, col(c)]
        at_re = at_im = jnp.zeros((1, 128), F32)
        for k in range(SEGMENTS):
            carry[c, k : k + 1] = at_re
            carry[CB + c, k : k + 1] = at_im
            row = slice(k, k + 1)
            at_re, at_im = (
                p_re[row] * at_re - p_im[row] * at_im + re[c][row],
                p_re[row] * at_im + p_im[row] * at_re + im[c][row],
            )

    def second(j, kept):
        re, im = kept
        new_re, new_im = [], []
        for c in range(CB):
            gate = lam[c, rows(j)]
            a, b = gate * cos[:, col(c)], gate * sin[:, col(c)]
            new_re.append(a * re[c] - b * im[c] + src[c, rows(j)])
            new_im.append(a * im[c] + b * re[c] + src[CB + c, rows(j)])
            out[c, rows(j)] = new_re[c]
            out[CB + c, rows(j)] = new_im[c]
        return tuple(new_re), tuple(new_im)

    start = tuple(carry[c] for c in range(CB)), tuple(carry[CB + c] for c in range(CB))
    lax.fori_loop(0, steps, second, start)


def turned(cos, sin, power):
    re, im = jnp.ones_like(cos), jnp.zeros_like(sin)
    base_re, base_im = cos, sin
    while power:
        if power % 2:
            re, im = re * base_re - im * base_im, re * base_im + im * base_re
        power //= 2
        if power:
            base_re, base_im = base_re * base_re - base_im * base_im, 2.0 * base_re * base_im
    return re, im


def opening_kernel(
    length, cuts,
    hidden, drive, forget, outgate, mixout, gate, up, down, vectors,
    n1_out, pd_out, pg_out, lam_out, s_out, wdfg_out, wo_out, wau_out, wb_out, vec_out,
    raw, stage, wdfg, wo, wau, wb, vec_rows, vec, n1, pd_low, pg_low, lam, src, states, carry,
    out_sems, *sems,
):
    at = Places()
    gather = Gather(at, raw, cuts, sems)
    own = raw.at[at.core, at.chip]
    for ref, part in ((drive, DRIVE), (outgate, OUTGATE), (mixout, MIXOUT), (gate, GATE), (up, UP), (down, DOWN)):
        own[part[0] : part[0] + ref.shape[0]] = pack(ref, stage, part[2]).astype(BF16)
    own[FORGET[0] : FORGET[0] + 80] = jnp.concatenate([pack(forget, stage, 3), vectors[...].astype(F32)], axis=0).astype(BF16)
    at.barrier()

    copies = []

    def give(index, source, target):
        copy = pltpu.make_async_copy(source, target, out_sems.at[index])
        copy.start()
        copies.append(copy)

    def compute_first():
        assemble(raw, DRIVE, wdfg, 0)
        assemble(raw, FORGET, wdfg, D)
        assemble(raw, OUTGATE, wdfg, D + C)
        for chip in range(16):
            for core in range(2):
                block = raw[core, chip, FORGET[0] + 64 : FORGET[0] + 80].astype(F32)
                vec_rows[2 * chip + core : 2 * chip + core + 1] = block[8:9]
        rows = vec_rows[...].astype(BF16)
        for index, (lane, width) in enumerate(VECTOR_PARTS):
            vec[index : index + 1, 0 : 32 * width] = vector_of(rows, lane, width)
        phase = vec[4:5, 0:C]
        vec[5:6, 0:C] = jnp.cos(phase)
        vec[6:7, 0:C] = jnp.sin(phase)
        gain = vec[0:1]
        bias = vec[3:4, 0:C]

        def tile(t, _):
            at_rows = pl.ds(pl.multiple_of(t * TILE, TILE), TILE)
            x = hidden[at_rows].astype(F32)
            normed = (x * lax.rsqrt(jnp.mean(x * x, axis=1, keepdims=True) + norm_eps) * gain).astype(BF16)
            n1[at_rows] = normed
            pre = product(normed, wdfg[...])
            pd, pf, pg = pre[:, :D], pre[:, D : D + C], pre[:, D + C :]
            pd_low[at_rows] = pd.astype(BF16)
            pg_low[at_rows] = pg.astype(BF16)
            keep = lower_bound + (1.0 - lower_bound) * sigmoid(pf + bias)
            driven = pd * sigmoid(pd)
            inflow = 1.0 - keep
            for c in range(CB):
                lam[c, at_rows] = keep[:, col(c)]
                src[c, at_rows] = inflow[:, col(c)] * driven[:, col(c)]
                src[CB + c, at_rows] = inflow[:, col(c)] * driven[:, col(CB + c)]
            return 0

        lax.fori_loop(0, length // TILE, tile, 0)
        give(0, n1, n1_out)
        give(1, pd_low, pd_out)
        give(2, pg_low, pg_out)
        give(3, lam, lam_out)
        give(4, wdfg, wdfg_out)
        give(5, vec, vec_out)

    def compute_scan():
        scan_forward(length, lam, src, states, vec[5:6, 0:C], vec[6:7, 0:C], carry)
        give(6, states, s_out)

    todo = {2: [compute_first, compute_scan], 3: [lambda: assemble(raw, MIXOUT, wo, 0), lambda: give(7, wo, wo_out)]}
    todo[5] = [lambda: assemble(raw, GATE, wau, 0)]
    todo[7] = [lambda: assemble(raw, UP, wau, FF), lambda: give(8, wau, wau_out)]
    todo[9] = [lambda: assemble(raw, DOWN, wb, 0), lambda: give(9, wb, wb_out)]
    count = len(cuts)
    ahead = 2
    for k in range(ahead):
        gather.along(k)
    for t in range(count + 5):
        if t < count:
            gather.column(t)
            if t + ahead < count:
                gather.along(t + ahead)
        if 0 <= t - 1 < count:
            gather.plane(t - 1)
        if 0 <= t - 3 < count:
            gather.diagonal(t - 3)
        if 0 <= t - 4 < count:
            gather.rest(t - 4)
        if 0 <= t - 5 < count:
            gather.whole(t - 5)
            for work in todo.get(t - 5, ()):
                work()
    gather.finish()
    for copy in copies:
        copy.wait()


def opening(hidden, weights, vectors):
    length = hidden.shape[0]
    cuts = cuts_of(GATHER_SIZES)
    vmem = pl.BlockSpec(memory_space=pltpu.VMEM)
    hbm = pl.BlockSpec(memory_space=pl.ANY)
    shapes = [
        ((length, D), BF16), ((length, D), BF16), ((length, D), BF16), ((CB, length, 128), F32), ((NB, length, 128), F32),
        ((D, WDFG), BF16), ((D, D), BF16), ((D, 2 * FF), BF16), ((FF, D), BF16), ((8, D), F32),
    ]
    return pl.pallas_call(
        functools.partial(opening_kernel, length, cuts),
        out_shape=[jax.ShapeDtypeStruct(*s) for s in shapes],
        in_specs=[vmem] * 9,
        out_specs=[hbm] * len(shapes),
        scratch_shapes=[
            pltpu.VMEM((2, 16, ROWS, 128), BF16), pltpu.VMEM((288, 128), F32),
            pltpu.VMEM((D, WDFG), BF16), pltpu.VMEM((D, D), BF16), pltpu.VMEM((D, 2 * FF), BF16), pltpu.VMEM((FF, D), BF16),
            pltpu.VMEM((32, 128), F32), pltpu.VMEM((8, D), F32),
            pltpu.VMEM((length, D), BF16), pltpu.VMEM((length, D), BF16), pltpu.VMEM((length, D), BF16),
            pltpu.VMEM((CB, length, 128), F32), pltpu.VMEM((NB, length, 128), F32), pltpu.VMEM((NB, length, 128), F32),
            pltpu.VMEM((NB, SEGMENTS, 128), F32),
            pltpu.SemaphoreType.DMA((10,)),
        ] + Gather.semaphores(len(cuts)),
        compiler_params=pltpu.CompilerParams(collective_id=0, has_side_effects=True, vmem_limit_bytes=60 * MIB),
    )(hidden, *weights, vectors)


MID = 224


def group_sum(values, ones, exact):
    high = values.astype(BF16)
    total = product(high, ones)
    if exact:
        total += product((values - high.astype(F32)).astype(BF16), ones)
    return total


def group_spread(values, wide):
    high = values.astype(BF16)
    low = (values - high.astype(F32)).astype(BF16)
    return product(jnp.concatenate([high, low], axis=1), wide)


def group_matrices():
    feature = lax.broadcasted_iota(jnp.int32, (D, 128), 0)
    group = lax.broadcasted_iota(jnp.int32, (D, 128), 1) * (D // GROUPS)
    ones = jnp.where(jnp.logical_and(feature >= group, feature < group + D // GROUPS), 1.0, 0.0)
    feature = lax.broadcasted_iota(jnp.int32, (256, D), 1)
    row = lax.broadcasted_iota(jnp.int32, (256, D), 0)
    group = jnp.where(row >= 128, row - 128, row) * (D // GROUPS)
    wide = jnp.where(jnp.logical_and(feature >= group, feature < group + D // GROUPS), 1.0, 0.0)
    return ones.astype(BF16), wide.astype(BF16)


def middle_kernel(
    x_ref, g_ref, s_ref, pg_ref, wo, wau, wb, vec,
    out_ref, n2_ref, mixed_ref, units_ref, dpau_ref, dm_ref, dmiddle_ref, ds_ref, dpg_ref, sums_ref,
    ones_ref, wide_ref,
):
    @pl.when(pl.program_id(0) == 0)
    def _():
        ones_ref[...], wide_ref[...] = group_matrices()
        sums_ref[...] = jnp.zeros_like(sums_ref)

    ones, wide = ones_ref[...], wide_ref[...]
    share = 1.0 / (D // GROUPS)
    second_gain, group_gain = vec[1:2], vec[2:3]
    x = x_ref[...].astype(F32)
    g = g_ref[...]
    y = jnp.concatenate([s_ref[c] for c in range(NB)], axis=1)
    centered = y - group_spread(group_sum(y, ones, True) * share, wide)
    spread_var = group_sum(centered * centered, ones, False) * share
    rstd = group_spread(lax.rsqrt(spread_var + group_eps), wide)
    normed = centered * rstd
    sg = sigmoid(pg_ref[...].astype(F32))
    gated = group_gain * sg
    mixed = (normed * gated).astype(BF16)
    mixed_ref[...] = mixed
    middle = x + product(mixed, wo[...])
    q = lax.rsqrt(jnp.mean(middle * middle, axis=1, keepdims=True) + norm_eps)
    scaled = middle * q
    n2 = (scaled * second_gain).astype(BF16)
    n2_ref[...] = n2
    pre = product(n2, wau[...])
    pa, pu = pre[:, :FF], pre[:, FF:]
    sa = sigmoid(pa)
    silu = pa * sa
    units = (silu * pu).astype(BF16)
    units_ref[...] = units
    out_ref[...] = (middle + product(units, wb[...])).astype(BF16)
    dunits = back_product(g, wb[...])
    dpa = (dunits * pu * (sa * (1.0 + pa * (1.0 - sa)))).astype(BF16)
    dpu = (dunits * silu).astype(BF16)
    dpau = jnp.concatenate([dpa, dpu], axis=1)
    dpau_ref[...] = dpau
    dn2 = back_product(dpau, wau[...])
    along = dn2 * scaled
    h_mean = jnp.mean(along * second_gain, axis=1, keepdims=True)
    dmiddle = g.astype(F32) + q * (second_gain * dn2 - scaled * h_mean)
    dmiddle_ref[...] = dmiddle
    dm = dmiddle.astype(BF16)
    dm_ref[...] = dm
    dmixed = back_product(dm, wo[...])
    dnormed = dmixed * gated
    both = dmixed * normed * sg
    dpg_ref[...] = (both * group_gain * (1.0 - sg)).astype(BF16)
    mean_one = group_spread(group_sum(dnormed, ones, False) * share, wide)
    mean_two = group_spread(group_sum(dnormed * normed, ones, False) * share, wide)
    ds = rstd * (dnormed - mean_one - normed * mean_two)
    for c in range(NB):
        ds_ref[c] = ds[:, col(c)]
    sums_ref[0:1] += jnp.sum(along, axis=0, keepdims=True)
    sums_ref[1:2] += jnp.sum(both, axis=0, keepdims=True)


def middle_part(hidden, cotangent, states, pg, wo, wau, wb, vec):
    length = hidden.shape[0]
    rows = lambda width: pl.BlockSpec((MID, width), lambda t: (t, 0))
    cols = pl.BlockSpec((NB, MID, 128), lambda t: (0, t, 0))
    whole = lambda a: pl.BlockSpec(a.shape, lambda t: (0, 0), pipeline_mode=pl.Buffered(1))
    outs = [(D, BF16), (D, BF16), (D, BF16), (FF, BF16), (2 * FF, BF16), (D, BF16), (D, F32)]
    return pl.pallas_call(
        middle_kernel,
        grid=(length // MID,),
        out_shape=[jax.ShapeDtypeStruct((length, w), t) for w, t in outs]
        + [jax.ShapeDtypeStruct((NB, length, 128), F32), jax.ShapeDtypeStruct((length, D), BF16), jax.ShapeDtypeStruct((8, D), F32)],
        in_specs=[rows(D), rows(D), cols, rows(D), whole(wo), whole(wau), whole(wb), whole(vec)],
        out_specs=[rows(w) for w, _ in outs] + [cols, rows(D), pl.BlockSpec((8, D), lambda t: (0, 0))],
        scratch_shapes=[pltpu.VMEM((D, 128), BF16), pltpu.VMEM((256, D), BF16)],
        compiler_params=pltpu.CompilerParams(vmem_limit_bytes=60 * MIB),
    )(hidden, cotangent, states, pg, wo, wau, wb, vec)


CHUNKS = ((1088, 144), (1232, 144), (512, 144), (656, 144), (800, 144), (944, 144), (368, 144), (0, 144), (144, 144), (288, 80))


class Scatter:
    def __init__(self, places, stage, recv1, recv2, recv3, recvz, outs, sems):
        self.at, self.stage = places, stage
        self.recv1, self.recv2, self.recv3, self.recvz, self.outs = recv1, recv2, recv3, recvz, outs
        self.s1, self.r1, self.s2, self.r2, self.s3, self.r3, self.s4, self.r4 = sems
        self.ops = {}

    @staticmethod
    def semaphores(k):
        dma = pltpu.SemaphoreType.DMA
        return [dma((k,)), dma((k,)), dma((k, 2)), dma((k, 2)), dma((k,)), dma((k,)), dma((k, 3)), dma((k, 3))]

    def send(self, key, source, target, send_sem, recv_sem, partner):
        copy = pltpu.make_async_remote_copy(
            src_ref=source, dst_ref=target, send_sem=send_sem, recv_sem=recv_sem, device_id=partner, device_id_type=MESH
        )
        copy.start()
        self.ops[key] = copy

    def rows(self, k):
        return slice(CHUNKS[k][0], CHUNKS[k][0] + CHUNKS[k][1])

    def add(self, k, first, received, slot):
        rows, core = self.rows(k), self.at.core

        def one(i, _):
            mine = self.stage[core, first + i, rows].astype(F32)
            self.stage[core, first + i, rows] = (mine + received[slot + i, rows].astype(F32)).astype(BF16)
            return 0

        lax.fori_loop(0, 4, one, 0)

    def cores(self, k):
        rows = self.rows(k)
        self.send(("1", k), self.stage.at[1 - self.at.core, :, rows], self.recv1.at[:, rows], self.s1.at[k], self.r1.at[k], self.at.sibling)

    def second(self, k):
        rows, at = self.rows(k), self.at
        self.ops[("1", k)].wait_recv()
        for i, first in enumerate((at.dcol, at.scol)):
            self.add(k, first, self.recv1, first)
            self.send(
                (f"2{i}", k), self.stage.at[at.core, pl.ds(first, 4), rows], self.recv2.at[pl.ds(4 * i, 4), rows],
                self.s2.at[k, i], self.r2.at[k, i], at.second,
            )
        self.add(k, at.fcol, self.recv1, at.fcol)
        self.add(k, at.col, self.recv1, at.col)

    def first(self, k):
        rows, at = self.rows(k), self.at
        self.ops[("20", k)].wait_recv()
        self.add(k, at.fcol, self.recv2, 0)
        self.send(("3", k), self.stage.at[at.core, pl.ds(at.fcol, 4), rows], self.recv3.at[:, rows], self.s3.at[k], self.r3.at[k], at.first)
        self.ops[("21", k)].wait_recv()
        self.add(k, at.col, self.recv2, 4)

    def along(self, k):
        rows, at = self.rows(k), self.at
        self.ops[("3", k)].wait_recv()
        self.add(k, at.col, self.recv3, 0)
        for d in (1, 2, 3):
            self.send(
                (f"4{d}", k), self.stage.at[at.core, at.col + (at.z + d) % 4, rows], self.recvz.at[d - 1, rows],
                self.s4.at[k, d - 1], self.r4.at[k, d - 1], at.along[d - 1],
            )

    def last(self, k):
        rows, at = self.rows(k), self.at
        total = self.stage[at.core, at.chip, rows].astype(F32)
        for d in (1, 2, 3):
            self.ops[(f"4{d}", k)].wait_recv()
            total += self.recvz[d - 1, rows].astype(F32)
        self.outs(k, total)

    def finish(self):
        for copy in self.ops.values():
            copy.wait_send()


def closing_kernel(
    length,
    units, g, n2, dpau, mixed, dm, n1, dpg, states, ds, lam, pd, hidden, dmiddle, wdfg, vec, sums,
    hidden_grad, drive_out, forget_out, outgate_out, mixout_out, gate_out, up_out, down_out, vec_out,
    left, right, left2, right2, s_buf, ds_buf, lam_buf, wdfg_buf, x_tile, dm_tile, hg_tile, carry, vec_rows, vec_sums,
    stage, recv1, recv2, recv3, recvz, load_sems, tile_sems, *sems,
):
    at = Places()

    def unpack(ref, total, rows, blocks, first_block):
        for j in range(total.shape[0] // rows):
            ref[pl.ds(first_block + j, rows, stride=blocks)] = total[j * rows : (j + 1) * rows]

    def deliver(k, total):
        if k < 2:
            unpack(down_out, total, 48, 6, 3 * k)
        elif k < 4:
            unpack(gate_out, total, 24, 12, 6 * (k - 2))
        elif k < 6:
            unpack(up_out, total, 24, 12, 6 * (k - 4))
        elif k < 9:
            unpack((mixout_out, drive_out, outgate_out)[k - 6], total, 24, 6, 0)
        else:
            unpack(forget_out, total[:72], 24, 3, 0)
            vec_out[...] = total[72:80]

    scatter = Scatter(at, stage, recv1, recv2, recv3, recvz, deliver, sems)
    loads = {}

    def load(key, source, target):
        copy = pltpu.make_async_copy(source, target, load_sems.at[len(loads)])
        copy.start()
        loads[key] = copy

    def need(*keys):
        for key in keys:
            loads[key].wait()

    load("units", units, left)
    load("g", g, right)
    load("n2", n2, left2)
    load("dpau", dpau, right2)
    load("s", states, s_buf.at[:, pl.ds(8, length)])
    load("ds", ds, ds_buf)
    load("lam", lam, lam_buf)
    load("wdfg", wdfg, wdfg_buf)
    at.barrier()

    def weight_chunk(source, source_col, rows, per, other, other_col, blocks, start, tail=None):
        for m in range(rows // 384):
            value = outer_sum(
                source[:, source_col + 384 * m : source_col + 384 * (m + 1)], other[:, other_col : other_col + 128 * blocks]
            )
            for i in range(384 // per):
                index = m * (384 // per) + i
                core, chip = index % 2, index // 2
                parts = [value[i * per : (i + 1) * per, col(j)] for j in range(blocks)]
                if tail is not None:
                    row = tail[index : index + 1]
                    parts += [row, jnp.zeros((7, 128), F32)]
                block = jnp.concatenate(parts, axis=0)
                stage[core, chip, start : start + block.shape[0]] = block.astype(BF16)

    def down(i):
        if i == 0:
            need("units", "g")
        weight_chunk(left, 0, FF, 48, right, 384 * i, 3, DOWN[0] + 144 * i)
        if i == 1:
            load("mixed", mixed, left.at[:, 0:D])
            load("n1", n1, left.at[:, D : 2 * D])
            load("dm", dm, right)

    def gate_up(i):
        if i == 0:
            need("n2", "dpau")
        weight_chunk(left2, 0, D, 24, right2, D * i, 6, GATE[0] + 144 * i)
        if i == 3:
            load("dpg", dpg, right2.at[:, D + C : WDFG])
            load("pd", pd, left2)

    def mixout():
        need("mixed", "dm")
        weight_chunk(left, 0, D, 24, right, 0, 6, MIXOUT[0])

    def reverse():
        need("s", "ds", "lam", "pd")
        vec_sums[0:1] = jnp.zeros((1, D), F32)
        scan_backward(length, lam_buf, s_buf, ds_buf, vec[5:6, 0:C], vec[6:7, 0:C], carry, vec_sums)

        def tile(t, _):
            rows = pl.ds(pl.multiple_of(t * TILE, TILE), TILE)
            pre = left2[rows].astype(F32)
            sig = sigmoid(pre)
            driven = pre * sig
            slope = sig * (1.0 + pre * (1.0 - sig))
            for c in range(CB):
                gate = lam_buf[c, rows]
                inflow = 1.0 - gate
                dgate = s_buf[c, pl.ds(pl.multiple_of(t * TILE + 8, 8), TILE)]
                for half in (c, CB + c):
                    grad = ds_buf[half, rows]
                    dgate -= grad * driven[:, col(half)]
                    right2[rows, col(half)] = (inflow * grad * slope[:, col(half)]).astype(BF16)
                dpf = dgate * ((gate - lower_bound) * inflow * (1.0 / (1.0 - lower_bound)))
                vec_sums[0:1, col(c)] += jnp.sum(dpf, axis=0, keepdims=True)
                right2[rows, col(NB + c)] = dpf.astype(BF16)
            return 0

        lax.fori_loop(0, length // TILE, tile, 0)

    def drive():
        need("n1", "dpg")
        weight_chunk(left, D, D, 24, right2, 0, 6, DRIVE[0])

    def outgate():
        weight_chunk(left, D, D, 24, right2, D + C, 6, OUTGATE[0])

    def inputs():
        need("wdfg")
        vec_sums[2:3] = jnp.zeros((1, D), F32)
        first_gain = vec[0:1]
        count = length // TILE
        back = {}

        def fetch(t):
            rows = slice(t * TILE, (t + 1) * TILE)
            a = pltpu.make_async_copy(hidden.at[rows], x_tile.at[t % 2], tile_sems.at[0, t % 2])
            b = pltpu.make_async_copy(dmiddle.at[rows], dm_tile.at[t % 2], tile_sems.at[1, t % 2])
            a.start()
            b.start()
            back[t] = (a, b)

        fetch(0)
        outgoing = {}
        for t in range(count):
            if t + 1 < count:
                fetch(t + 1)
            for copy in back[t]:
                copy.wait()
            rows = slice(t * TILE, (t + 1) * TILE)
            x = x_tile[t % 2].astype(F32)
            dn1 = back_product(right2[rows, 0:WDFG], wdfg_buf[...])
            p = lax.rsqrt(jnp.mean(x * x, axis=1, keepdims=True) + norm_eps)
            scaled = x * p
            terms = dn1 * scaled
            vec_sums[2:3] += jnp.sum(terms, axis=0, keepdims=True)
            if t >= 2:
                outgoing[t - 2].wait()
            mean = jnp.mean(terms * first_gain, axis=1, keepdims=True)
            hg_tile[t % 2] = dm_tile[t % 2] + p * (first_gain * dn1 - scaled * mean)
            copy = pltpu.make_async_copy(hg_tile.at[t % 2], hidden_grad.at[rows], tile_sems.at[2, t % 2])
            copy.start()
            outgoing[t] = copy
        for t in (count - 2, count - 1):
            outgoing[t].wait()

    def forget():
        rows = jnp.zeros((32, 128), F32)
        sources = (vec_sums[2:3], sums[0:1], sums[1:2], vec_sums[0:1, 0:C], vec_sums[1:2, 0:C])
        for (lane, width), source in zip(VECTOR_PARTS, sources):
            total = 32 * width
            mine = jnp.where(own_columns(width, total), jnp.broadcast_to(source, (32, total)), 0.0).astype(BF16)
            rows += back_product(mine, spread(lane, width, total, True))
        vec_rows[...] = rows
        weight_chunk(left, D, D, 24, right2, D, 3, FORGET[0], vec_rows)

    work = [
        lambda: down(0), lambda: down(1), lambda: gate_up(0), lambda: gate_up(1), lambda: gate_up(2), lambda: gate_up(3), mixout,
        lambda: (reverse(), drive()), outgate, lambda: (inputs(), forget()),
    ]
    count = len(work)
    for t in range(count + 4):
        if t < count:
            work[t]()
            scatter.cores(t)
        if 0 <= t - 1 < count:
            scatter.second(t - 1)
        if 0 <= t - 2 < count:
            scatter.first(t - 2)
        if 0 <= t - 3 < count:
            scatter.along(t - 3)
        if 0 <= t - 4 < count:
            scatter.last(t - 4)
    scatter.finish()


def scan_backward(length, lam, states, ds, cos, sin, carry, vec_sums):
    steps = length // SEGMENTS
    zero = jnp.zeros((SEGMENTS, 128), F32)

    def rows(j):
        return pl.ds(j, SEGMENTS, stride=steps)

    def first(i, kept):
        j = steps - 1 - i
        prod, re, im = kept
        new_p, new_re, new_im = [], [], []
        for c in range(CB):
            gate = lam[c, rows(j)]
            g_re, g_im = ds[c, rows(j)] + re[c], ds[CB + c, rows(j)] + im[c]
            new_p.append(prod[c] * gate)
            new_re.append(gate * (cos[:, col(c)] * g_re + sin[:, col(c)] * g_im))
            new_im.append(gate * (cos[:, col(c)] * g_im - sin[:, col(c)] * g_re))
        return tuple(new_p), tuple(new_re), tuple(new_im)

    ones = (jnp.ones((SEGMENTS, 128), F32),) * CB
    prod, re, im = lax.fori_loop(0, steps, first, (ones, (zero,) * CB, (zero,) * CB))
    turn_re, turn_im = turned(cos, -sin, steps)
    for c in range(CB):
        p_re, p_im = prod[c] * turn_re[:, col(c)], prod[c] * turn_im[:, col(c)]
        at_re = at_im = jnp.zeros((1, 128), F32)
        for k in reversed(range(SEGMENTS)):
            carry[c, k : k + 1] = at_re
            carry[CB + c, k : k + 1] = at_im
            row = slice(k, k + 1)
            at_re, at_im = (
                p_re[row] * at_re - p_im[row] * at_im + re[c][row],
                p_re[row] * at_im + p_im[row] * at_re + im[c][row],
            )
    for c in range(NB):
        states[c, 0:8] = jnp.zeros((8, 128), F32)

    def step(at_rows, before, kept):
        re, im, phase = kept
        new_re, new_im, new_phase = [], [], []
        for c in range(CB):
            gate = lam[c, at_rows]
            g_re, g_im = ds[c, at_rows] + re[c], ds[CB + c, at_rows] + im[c]
            w_re = cos[:, col(c)] * g_re + sin[:, col(c)] * g_im
            w_im = cos[:, col(c)] * g_im - sin[:, col(c)] * g_re
            new_re.append(gate * w_re)
            new_im.append(gate * w_im)
            s_re, s_im = before(c), before(CB + c)
            new_phase.append(phase[c] + gate * (w_im * s_re - w_re * s_im))
            ds[c, at_rows] = g_re
            ds[CB + c, at_rows] = g_im
            yield c, w_re * s_re + w_im * s_im
        kept[:] = [tuple(new_re), tuple(new_im), tuple(new_phase)]

    opening_rows = [states[c, pl.ds(7, SEGMENTS, stride=steps)] for c in range(NB)]

    def second(i, kept):
        j = steps - 1 - i
        kept = list(kept)
        for c, dgate in step(rows(j), lambda c: states[c, pl.ds(j + 7, SEGMENTS, stride=steps)], kept):
            states[c, pl.ds(j + 8, SEGMENTS, stride=steps)] = dgate
        return tuple(kept)

    start = (tuple(carry[c] for c in range(CB)), tuple(carry[CB + c] for c in range(CB)), (zero,) * CB)
    kept = list(lax.fori_loop(0, steps - 1, second, start))
    for c, dgate in step(rows(0), lambda c: opening_rows[c], kept):
        states[c, pl.ds(8, SEGMENTS, stride=steps)] = dgate
    for c in range(CB):
        vec_sums[1:2, col(c)] = jnp.sum(kept[2][c], axis=0, keepdims=True)


def closing(length, shards, arrays, hidden, dmiddle, wdfg, vec, sums):
    vmem = pl.BlockSpec(memory_space=pltpu.VMEM)
    hbm = pl.BlockSpec(memory_space=pl.ANY)
    shapes = [(length, D)] + [w.shape for w in shards] + [(8, 128)]
    return pl.pallas_call(
        functools.partial(closing_kernel, length),
        out_shape=[jax.ShapeDtypeStruct(s, F32) for s in shapes],
        in_specs=[hbm] * 15 + [vmem] * 2,
        out_specs=[hbm] + [vmem] * 8,
        scratch_shapes=[
            pltpu.VMEM((length, FF), BF16), pltpu.VMEM((length, D), BF16), pltpu.VMEM((length, D), BF16), pltpu.VMEM((length, 2 * FF), BF16),
            pltpu.VMEM((NB, length + 8, 128), F32), pltpu.VMEM((NB, length, 128), F32), pltpu.VMEM((CB, length, 128), F32),
            pltpu.VMEM((D, WDFG), BF16), pltpu.VMEM((2, TILE, D), BF16), pltpu.VMEM((2, TILE, D), F32), pltpu.VMEM((2, TILE, D), F32),
            pltpu.VMEM((NB, SEGMENTS, 128), F32), pltpu.VMEM((32, 128), F32), pltpu.VMEM((8, D), F32),
            pltpu.VMEM((2, 16, ROWS, 128), BF16), pltpu.VMEM((16, ROWS, 128), BF16), pltpu.VMEM((8, ROWS, 128), BF16),
            pltpu.VMEM((4, ROWS, 128), BF16), pltpu.VMEM((3, ROWS, 128), BF16),
            pltpu.SemaphoreType.DMA((16,)), pltpu.SemaphoreType.DMA((3, 2)),
        ] + Scatter.semaphores(len(CHUNKS)),
        compiler_params=pltpu.CompilerParams(collective_id=1, has_side_effects=True, vmem_limit_bytes=62 * MIB),
    )(*arrays, hidden, dmiddle, wdfg, vec, sums)


def fast(hidden, cotangent, *params):
    weights, parts = params[:7], params[7:]
    vectors = jnp.zeros((8, 128), BF16).at[0, :96].set(jnp.concatenate(parts))
    n1, pd, pg, lam, states, wdfg, wo, wau, wb, vec = opening(hidden, weights, vectors)
    out, n2, mixed, units, dpau, dm, dmiddle, ds, dpg, sums = middle_part(hidden, cotangent, states, pg, wo, wau, wb, vec)
    hidden_grad, *grads, row = closing(
        hidden.shape[0], weights, (units, cotangent, n2, dpau, mixed, dm, n1, dpg, states, ds, lam, pd), hidden, dmiddle, wdfg, vec, sums
    )
    return (out, hidden_grad, *grads) + tuple(row[0, lane : lane + width] for lane, width in VECTOR_PARTS)


SPAN = 56


def rms_scale(values, gain_vec):
    return (
        values * lax.rsqrt(jnp.mean(values * values, axis=1, keepdims=True) + norm_eps) * gain_vec
    )


def combine(earlier, later_term):
    return (
        later_term[0] * earlier[0] - later_term[1] * earlier[1],
        later_term[0] * earlier[1] + later_term[1] * earlier[0],
        later_term[0] * earlier[2] - later_term[1] * earlier[3] + later_term[2],
        later_term[0] * earlier[3] + later_term[1] * earlier[2] + later_term[3],
    )


def block_prefix(block_terms):
    length = block_terms[0].shape[0]
    width = block_terms[0].shape[1]
    current = block_terms
    offset = 1
    while offset < length:
        filler = (
            jnp.ones((offset, width), jnp.float32),
            jnp.zeros((offset, width), jnp.float32),
            jnp.zeros((offset, width), jnp.float32),
            jnp.zeros((offset, width), jnp.float32),
        )
        earlier = tuple(
            (
                jnp.concatenate([front, member[: length - offset]], axis=0)
                for front, member in zip(filler, current)
            )
        )
        current = combine(earlier, current)
        offset = offset * 2
    return current


def mixer_core(drive_pre, forget_pre, outgate_pre, phase_angle, forget_bias, group_gain):
    length = drive_pre.shape[0]
    features = drive_pre.shape[1]
    channels = features // 2
    blocks = length // SPAN
    driven = jax.nn.silu(drive_pre)
    retain = lower_bound + (1.0 - lower_bound) * jax.nn.sigmoid(forget_pre + forget_bias)
    rotate_re = retain * jnp.cos(phase_angle)
    rotate_im = retain * jnp.sin(phase_angle)
    inflow = 1.0 - retain
    source_re = inflow * driven[:, :channels]
    source_im = inflow * driven[:, channels:]
    pieces = tuple(
        (
            member.reshape(blocks, SPAN, channels)
            for member in (rotate_re, rotate_im, source_re, source_im)
        )
    )

    def advance(carried, block_terms):
        summed = block_prefix(block_terms)
        state_re = summed[0] * carried[0] - summed[1] * carried[1] + summed[2]
        state_im = summed[0] * carried[1] + summed[1] * carried[0] + summed[3]
        return ((state_re[-1], state_im[-1]), (state_re, state_im))

    initial = (jnp.zeros((channels,), jnp.float32), jnp.zeros((channels,), jnp.float32))
    _, (states_re, states_im) = lax.scan(jax.checkpoint(advance), initial, pieces)
    joined = jnp.concatenate(
        [states_re.reshape(length, channels), states_im.reshape(length, channels)], axis=1
    )
    grouped = joined.reshape(length, GROUPS, features // GROUPS)
    centered = grouped - jnp.mean(grouped, axis=2, keepdims=True)
    normed = centered * lax.rsqrt(jnp.mean(centered * centered, axis=2, keepdims=True) + group_eps)
    return normed.reshape(length, features) * group_gain * jax.nn.sigmoid(outgate_pre)


def unpack(gathered):
    targets = ((D, D), (D, C), (D, D), (D, D), (D, FF), (D, FF), (FF, D))
    matrices = tuple(
        (gathered[position].reshape(target) for position, target in enumerate(targets))
    )
    vectors = tuple((member.astype(jnp.float32) for member in gathered[7:]))
    return matrices + vectors


def local(
    hidden,
    cotangent,
    drive_weight,
    forget_weight,
    outgate_weight,
    mixout_weight,
    gate_weight,
    up_weight,
    down_weight,
    first_gain,
    second_gain,
    group_gain,
    forget_bias,
    phase_angle,
):
    params = unpack(
        (
            lax.all_gather(drive_weight, ("dp", "fsdp"), axis=0, tiled=True),
            lax.all_gather(forget_weight, ("dp", "fsdp"), axis=0, tiled=True),
            lax.all_gather(outgate_weight, ("dp", "fsdp"), axis=0, tiled=True),
            lax.all_gather(mixout_weight, ("dp", "fsdp"), axis=0, tiled=True),
            lax.all_gather(gate_weight, ("dp", "fsdp"), axis=0, tiled=True),
            lax.all_gather(up_weight, ("dp", "fsdp"), axis=0, tiled=True),
            lax.all_gather(down_weight, ("dp", "fsdp"), axis=0, tiled=True),
            lax.all_gather(first_gain, ("dp", "fsdp"), axis=0, tiled=True),
            lax.all_gather(second_gain, ("dp", "fsdp"), axis=0, tiled=True),
            lax.all_gather(group_gain, ("dp", "fsdp"), axis=0, tiled=True),
            lax.all_gather(forget_bias, ("dp", "fsdp"), axis=0, tiled=True),
            lax.all_gather(phase_angle, ("dp", "fsdp"), axis=0, tiled=True),
        )
    )
    inputs = hidden.astype(jnp.float32)
    normed_float, pull_first = jax.vjp(rms_scale, inputs, params[7])
    normed_one = normed_float.astype(jnp.bfloat16)
    drive_pre = product(normed_one, params[0])
    forget_pre = product(normed_one, params[1])
    outgate_pre = product(normed_one, params[2])
    mixed_float, pull_mixer = jax.vjp(
        mixer_core, drive_pre, forget_pre, outgate_pre, params[11], params[10], params[9]
    )
    mixed = mixed_float.astype(jnp.bfloat16)
    middle = inputs + product(mixed, params[3])
    second_float, pull_second = jax.vjp(rms_scale, middle, params[8])
    normed_two = second_float.astype(jnp.bfloat16)
    gate_pre = product(normed_two, params[4])
    up_pre = product(normed_two, params[5])
    gate_sig = jax.nn.sigmoid(gate_pre)
    silu_gate = gate_pre * gate_sig
    hidden_units = (silu_gate * up_pre).astype(jnp.bfloat16)
    layer_out = (middle + product(hidden_units, params[6])).astype(jnp.bfloat16)
    back_params = unpack(
        (
            lax.all_gather(drive_weight, ("dp", "fsdp"), axis=0, tiled=True),
            lax.all_gather(forget_weight, ("dp", "fsdp"), axis=0, tiled=True),
            lax.all_gather(outgate_weight, ("dp", "fsdp"), axis=0, tiled=True),
            lax.all_gather(mixout_weight, ("dp", "fsdp"), axis=0, tiled=True),
            lax.all_gather(gate_weight, ("dp", "fsdp"), axis=0, tiled=True),
            lax.all_gather(up_weight, ("dp", "fsdp"), axis=0, tiled=True),
            lax.all_gather(down_weight, ("dp", "fsdp"), axis=0, tiled=True),
            lax.all_gather(first_gain, ("dp", "fsdp"), axis=0, tiled=True),
            lax.all_gather(second_gain, ("dp", "fsdp"), axis=0, tiled=True),
            lax.all_gather(group_gain, ("dp", "fsdp"), axis=0, tiled=True),
            lax.all_gather(forget_bias, ("dp", "fsdp"), axis=0, tiled=True),
            lax.all_gather(phase_angle, ("dp", "fsdp"), axis=0, tiled=True),
        )
    )
    units_back = back_product(cotangent, back_params[6])
    down_grad = outer_sum(hidden_units, cotangent)
    slope = gate_sig * (1.0 + gate_pre * (1.0 - gate_sig))
    gate_back = (units_back * up_pre * slope).astype(jnp.bfloat16)
    up_back = (units_back * silu_gate).astype(jnp.bfloat16)
    gate_grad = outer_sum(normed_two, gate_back)
    up_grad = outer_sum(normed_two, up_back)
    second_back = back_product(gate_back, back_params[4]) + back_product(up_back, back_params[5])
    middle_part, secondgain_grad = pull_second(second_back)
    middle_back = cotangent.astype(jnp.float32) + middle_part
    middle_low = middle_back.astype(jnp.bfloat16)
    mixout_grad = outer_sum(mixed, middle_low)
    mixed_back = back_product(middle_low, back_params[3])
    drive_back, forget_back, outgate_back, phase_grad, bias_grad, groupgain_grad = pull_mixer(
        mixed_back
    )
    drive_low = drive_back.astype(jnp.bfloat16)
    forget_low = forget_back.astype(jnp.bfloat16)
    outgate_low = outgate_back.astype(jnp.bfloat16)
    drive_grad = outer_sum(normed_one, drive_low)
    forget_grad = outer_sum(normed_one, forget_low)
    outgate_grad = outer_sum(normed_one, outgate_low)
    first_back = (
        back_product(drive_low, back_params[0])
        + back_product(forget_low, back_params[1])
        + back_product(outgate_low, back_params[2])
    )
    input_part, firstgain_grad = pull_first(first_back)
    hidden_grad = middle_back + input_part
    all_terms = (
        drive_grad.reshape(-1, 128),
        forget_grad.reshape(-1, 128),
        outgate_grad.reshape(-1, 128),
        mixout_grad.reshape(-1, 128),
        gate_grad.reshape(-1, 128),
        up_grad.reshape(-1, 128),
        down_grad.reshape(-1, 128),
        firstgain_grad,
        secondgain_grad,
        groupgain_grad,
        bias_grad,
        phase_grad,
    )
    sums = (
        lax.psum_scatter(all_terms[0], ("dp", "fsdp"), scatter_dimension=0, tiled=True),
        lax.psum_scatter(all_terms[1], ("dp", "fsdp"), scatter_dimension=0, tiled=True),
        lax.psum_scatter(all_terms[2], ("dp", "fsdp"), scatter_dimension=0, tiled=True),
        lax.psum_scatter(all_terms[3], ("dp", "fsdp"), scatter_dimension=0, tiled=True),
        lax.psum_scatter(all_terms[4], ("dp", "fsdp"), scatter_dimension=0, tiled=True),
        lax.psum_scatter(all_terms[5], ("dp", "fsdp"), scatter_dimension=0, tiled=True),
        lax.psum_scatter(all_terms[6], ("dp", "fsdp"), scatter_dimension=0, tiled=True),
        lax.psum_scatter(all_terms[7], ("dp", "fsdp"), scatter_dimension=0, tiled=True),
        lax.psum_scatter(all_terms[8], ("dp", "fsdp"), scatter_dimension=0, tiled=True),
        lax.psum_scatter(all_terms[9], ("dp", "fsdp"), scatter_dimension=0, tiled=True),
        lax.psum_scatter(all_terms[10], ("dp", "fsdp"), scatter_dimension=0, tiled=True),
        lax.psum_scatter(all_terms[11], ("dp", "fsdp"), scatter_dimension=0, tiled=True),
    )
    return (
        layer_out,
        hidden_grad,
        sums[0],
        sums[1],
        sums[2],
        sums[3],
        sums[4],
        sums[5],
        sums[6],
        sums[7],
        sums[8],
        sums[9],
        sums[10],
        sums[11],
    )


def solution(mesh):
    rows, flat = P(("dp", "fsdp"), None), P(("dp", "fsdp"))
    step = fast if dict(mesh.shape) == {"dp": 4, "fsdp": 8} else local
    return jax.shard_map(
        step, mesh=mesh, in_specs=(rows,) * 9 + (flat,) * 5, out_specs=(rows,) * 9 + (flat,) * 5, check_vma=False
    )
```

```python
import functools

import jax
import jax.numpy as jnp
from jax import lax
from jax.experimental import pallas as pl
from jax.experimental.pallas import tpu as pltpu
from jax.sharding import PartitionSpec as P

D = 768
C = 384
FF = 1536
GROUPS = 8
NB = D // 128
CB = C // 128

lower_bound = 0.25
norm_eps = 1e-06
group_eps = 1e-05

F32 = jnp.float32
BF16 = jnp.bfloat16
MESH = pl.DeviceIdType.MESH
MIB = 2**20
AXES = "dp", "fsdp"

DRIVE = (0, 24, 6)
OUTGATE = (144, 24, 6)
FORGET = (288, 24, 3)
VECTORS = 360
MIXOUT = (368, 24, 6)
GATE = (512, 24, 12)
UP = (800, 24, 12)
DOWN = (1088, 48, 6)
ROWS = 1376
VECTOR_PARTS = ((0, 24), (24, 24), (48, 24), (72, 12), (84, 12))
WDFG = 2 * D + C

TILE = 224
SEGMENTS = 16


def sigmoid(t):
    return 0.5 * jnp.tanh(0.5 * t) + 0.5


def product(left, right):
    return jnp.dot(left, right, preferred_element_type=F32)


def back_product(left, right):
    return lax.dot_general(left, right, (((1,), (1,)), ((), ())), preferred_element_type=F32)


def outer_sum(left, right):
    return lax.dot_general(left, right, (((0,), (0,)), ((), ())), preferred_element_type=F32)


def coords():
    dp = lax.axis_index(AXES[0])
    fsdp = lax.axis_index(AXES[1])
    return dp // 2, dp % 2, fsdp // 2, fsdp % 2


def device(y, x, z, core):
    return (y * 2 + x, z * 2 + core)


CORE_LINK = 550e3
CORE_HOP = 1.5
GATHER_RATES = 75e3, 8.0
SCATTER_RATES = 92e3, 2.5
WINDOW = 4


Z_LINK, MID_LINK, PLANE_LINK, CORE_LINKS = range(4)


class Steps:
    def __init__(self):
        self.steps = []

    def add(self, run, needs, cost, transfers=(), rank=None):
        number = len(self.steps)
        self.steps.append((run, needs, cost, transfers, rank or (1, number)))
        return number

    def run(self, width, link_rate, hop):
        ready_at, free, now = {}, {}, 0.0
        pending = list(range(len(self.steps)))
        while pending:
            at = {n: max([ready_at[d] for d in self.steps[n][1]], default=0.0) for n in pending if all(d in ready_at for d in self.steps[n][1])}
            able = [n for n, t in at.items() if t <= now]
            if not able:
                now = min(at.values())
                continue
            chosen = min(able, key=lambda n: self.steps[n][4])
            pending.remove(chosen)
            run, _, cost, transfers, _ = self.steps[chosen]
            run()
            now += cost
            for index, (link, size) in enumerate(transfers):
                rate, wait = (CORE_LINK, CORE_HOP) if link == CORE_LINKS else (link_rate, hop)
                free[link] = max(now, free.get(link, 0.0)) + size * width / rate
                ready_at[chosen, index] = free[link] + wait
            ready_at[chosen] = now


class Places:
    def __init__(self):
        y, x, z, c = coords()
        self.z, self.core = z, c
        fy = jnp.where(c == 0, 1 - y, y)
        fx = jnp.where(c == 0, x, 1 - x)
        sy = jnp.where(c == 0, y, 1 - y)
        sx = jnp.where(c == 0, 1 - x, x)
        self.first = device(fy, fx, z, c)
        self.second = device(sy, sx, z, c)
        self.sibling = device(y, x, z, 1 - c)
        self.mate = device(y, x, z ^ 1, c)
        self.other = device(y, x, 3 - z, c)
        self.inner = jnp.logical_or(z == 1, z == 2)
        self.outer = jnp.logical_not(self.inner)
        self.along = [device(y, x, (z + d) % 4, c) for d in (1, 2, 3)]
        self.col = (y * 2 + x) * 4
        self.fcol = (fy * 2 + fx) * 4
        self.scol = (sy * 2 + sx) * 4
        self.dcol = ((1 - y) * 2 + (1 - x)) * 4
        self.half = (z % 2) * 2
        self.chip = self.col + z
        self.near = self.col + (z // 2) * 2
        self.far = self.col + 2 - (z // 2) * 2

    def barrier(self):
        bar = pltpu.get_barrier_semaphore()
        for partner in [self.first, self.second, self.sibling] + self.along:
            pl.semaphore_signal(bar, inc=1, device_id=partner, device_id_type=MESH)
        pl.semaphore_wait(bar, 6)


class Sends:
    def __init__(self, names, send_sems, recv_sems):
        self.index = {name: i for i, name in enumerate(names)}
        self.send_sems, self.recv_sems, self.copies = send_sems, recv_sems, {}

    def start(self, name, k, source, target, partner, when=None, lands=None):
        copy = pltpu.make_async_remote_copy(
            src_ref=source, dst_ref=target, send_sem=self.send_sems.at[k, self.index[name]],
            recv_sem=self.recv_sems.at[k, self.index[lands or name]], device_id=partner, device_id_type=MESH,
        )
        if when is None:
            copy.start()
        else:
            pl.when(when)(copy.start)
        self.copies[name, k] = copy, when

    def arrived(self, name, k):
        self.copies[name, k][0].wait_recv()

    def finish(self):
        for copy, when in self.copies.values():
            if when is None:
                copy.wait_send()
            else:
                pl.when(when)(copy.wait_send)


GATHER_NAMES = ("z1", "z2", "z3", "f0", "f1", "s0", "s1", "s2", "p", "c0", "c1", "c2", "c3", "c4")


class Gather:
    def __init__(self, places, raw, cuts, send_sems, recv_sems):
        self.at, self.raw, self.cuts = places, raw, cuts
        self.sends = Sends(GATHER_NAMES, send_sems, recv_sems)

    def send(self, name, first, count, k, partner, when=None, lands=None):
        low, high = self.cuts[k]
        ref = self.raw.at[self.at.core, pl.ds(first, count), low:high]
        self.sends.start(name, k, ref, ref, partner, when, lands)

    def own(self, k):
        self.send("z1", self.at.chip, 1, k, self.at.mate)

    def near(self, k):
        at = self.at
        self.sends.arrived("z1", k)
        self.send("z2", at.near, 2, k, at.other, at.inner)
        self.send("f0", at.near, 2, k, at.first)
        self.send("s0", at.near, 2, k, at.second)

    def far(self, k):
        at = self.at
        self.sends.arrived("z2", k)
        self.send("z3", at.far, 2, k, at.mate, at.inner, "z2")
        self.send("f1", at.far, 2, k, at.first)
        self.send("s1", at.far, 2, k, at.second)
        self.send("c0", at.col, 4, k, at.sibling)

    def first(self, k):
        at = self.at
        self.sends.arrived("f0", k)
        self.sends.arrived("f1", k)
        self.send("s2", at.fcol + at.half, 2, k, at.second)
        self.send("c1", at.fcol, 4, k, at.sibling)

    def second(self, k):
        at = self.at
        self.sends.arrived("s0", k)
        self.sends.arrived("s1", k)
        self.send("c2", at.scol, 4, k, at.sibling)

    def diagonal(self, k):
        at = self.at
        self.sends.arrived("s2", k)
        self.send("p", at.dcol + at.half, 2, k, at.mate)
        self.send("c3", at.dcol + at.half, 2, k, at.sibling)

    def rest(self, k):
        at = self.at
        self.sends.arrived("p", k)
        self.send("c4", at.dcol + 2 - at.half, 2, k, at.sibling)

    def whole(self, k):
        for name in ("c0", "c1", "c2", "c3", "c4"):
            self.sends.arrived(name, k)

    def schedule(self, steps, cost=0.3):
        done, far = [], []
        for k, (low, high) in enumerate(self.cuts):
            n = 2 * (high - low)

            def step(run, needs, transfers, stage):
                return steps.add(functools.partial(run, k), needs, cost, transfers, (0, k, -stage))

            own = step(self.own, far[k - WINDOW : k - WINDOW + 1] if k >= WINDOW else [], [(Z_LINK, n)], 0)
            near = step(self.near, [(own, 0)], [(MID_LINK, 2 * n), (PLANE_LINK, 2 * n)], 1)
            far.append(step(self.far, [(near, 0)], [(Z_LINK, 2 * n), (PLANE_LINK, 2 * n), (CORE_LINKS, 2 * n)], 2))
            first = step(self.first, [(near, 1), (far[k], 0), (far[k], 1)], [(PLANE_LINK, n), (CORE_LINKS, 2 * n)], 3)
            second = step(self.second, [first], [(CORE_LINKS, 2 * n)], 4)
            diagonal = step(self.diagonal, [second, (first, 0)], [(Z_LINK, 2 * n), (CORE_LINKS, n)], 5)
            rest = step(self.rest, [(diagonal, 0)], [(CORE_LINKS, n)], 6)
            done.append(step(self.whole, [(rest, 0), (diagonal, 1), (second, 0), (first, 1), (far[k], 2)], [], 7))
        return done


GATHER_SIZES = (144, 144, 80, 144, 288, 288, 288)


def cuts_of(sizes):
    cuts, start = [], 0
    for size in sizes:
        cuts.append((start, start + size))
        start += size
    return cuts


def pack(weight_ref, stage, blocks):
    rows = weight_ref.shape[0]
    stage[0:rows] = weight_ref[...].astype(F32)
    each = rows // blocks
    return jnp.concatenate([stage[pl.ds(j, each, stride=blocks)] for j in range(blocks)], axis=0)


def assemble(raw, part, target, column):
    first, rows, blocks = part
    total = -(-rows * blocks // 16) * 16

    def one(chip, _):
        pair = [raw[core, chip, first : first + total].astype(F32) for core in (0, 1)]
        for j in range(blocks):
            block = jnp.concatenate([member[j * rows : (j + 1) * rows] for member in pair], axis=0)
            target[pl.ds(pl.multiple_of(chip * (2 * rows), 16), 2 * rows), column + j * 128 : column + (j + 1) * 128] = (
                block.astype(BF16)
            )
        return 0

    lax.fori_loop(0, 16, one, 0)


def spread(lane, width, total, by_row):
    col = lax.broadcasted_iota(jnp.int32, (128, total), 1).astype(F32)
    row = lax.broadcasted_iota(jnp.int32, (128, total), 0).astype(F32)
    within = col - width * jnp.floor((col + 0.5) * (1.0 / width))
    return jnp.where(row == within + lane, 1.0, 0.0).astype(BF16)


def own_columns(width, total):
    col = lax.broadcasted_iota(jnp.int32, (32, total), 1)
    low = lax.broadcasted_iota(jnp.int32, (32, total), 0) * width
    return jnp.logical_and(col >= low, col < low + width)


def vector_of(rows, lane, width):
    total = 32 * width
    placed = product(rows, spread(lane, width, total, True))
    return jnp.sum(jnp.where(own_columns(width, total), placed, 0.0), axis=0, keepdims=True)


def col(c):
    return slice(c * 128, (c + 1) * 128)


def scan_forward(length, lam, src, out, cos, sin, carry):
    steps = length // SEGMENTS
    zero = jnp.zeros((SEGMENTS, 128), F32)

    def rows(j):
        return pl.ds(j, SEGMENTS, stride=steps)

    def first(j, kept):
        prod, re, im = kept
        new_p, new_re, new_im = [], [], []
        for c in range(CB):
            gate = lam[c, rows(j)]
            a, b = gate * cos[:, col(c)], gate * sin[:, col(c)]
            new_p.append(prod[c] * gate)
            new_re.append(a * re[c] - b * im[c] + src[c, rows(j)])
            new_im.append(a * im[c] + b * re[c] + src[CB + c, rows(j)])
        return tuple(new_p), tuple(new_re), tuple(new_im)

    ones = (jnp.ones((SEGMENTS, 128), F32),) * CB
    prod, re, im = lax.fori_loop(0, steps, first, (ones, (zero,) * CB, (zero,) * CB))
    turn_re, turn_im = turned(cos, sin, steps)
    for c in range(CB):
        p_re, p_im = prod[c] * turn_re[:, col(c)], prod[c] * turn_im[:, col(c)]
        at_re = at_im = jnp.zeros((1, 128), F32)
        for k in range(SEGMENTS):
            carry[c, k : k + 1] = at_re
            carry[CB + c, k : k + 1] = at_im
            row = slice(k, k + 1)
            at_re, at_im = (
                p_re[row] * at_re - p_im[row] * at_im + re[c][row],
                p_re[row] * at_im + p_im[row] * at_re + im[c][row],
            )

    def second(j, kept):
        re, im = kept
        new_re, new_im = [], []
        for c in range(CB):
            gate = lam[c, rows(j)]
            a, b = gate * cos[:, col(c)], gate * sin[:, col(c)]
            new_re.append(a * re[c] - b * im[c] + src[c, rows(j)])
            new_im.append(a * im[c] + b * re[c] + src[CB + c, rows(j)])
            out[c, rows(j)] = new_re[c]
            out[CB + c, rows(j)] = new_im[c]
        return tuple(new_re), tuple(new_im)

    start = tuple(carry[c] for c in range(CB)), tuple(carry[CB + c] for c in range(CB))
    lax.fori_loop(0, steps, second, start)


def turned(cos, sin, power):
    re, im = jnp.ones_like(cos), jnp.zeros_like(sin)
    base_re, base_im = cos, sin
    while power:
        if power % 2:
            re, im = re * base_re - im * base_im, re * base_im + im * base_re
        power //= 2
        if power:
            base_re, base_im = base_re * base_re - base_im * base_im, 2.0 * base_re * base_im
    return re, im


def group_sum(values, ones, exact):
    high = values.astype(BF16)
    total = product(high, ones)
    if exact:
        total += product((values - high.astype(F32)).astype(BF16), ones)
    return total


def split(values):
    high = values.astype(BF16)
    return jnp.concatenate([high, (values - high.astype(F32)).astype(BF16)], axis=1)


def group_spread(values, wide):
    return product(split(values), wide)


def group_matrices():
    feature = lax.broadcasted_iota(jnp.int32, (D, 128), 0)
    group = lax.broadcasted_iota(jnp.int32, (D, 128), 1) * (D // GROUPS)
    ones = jnp.where(jnp.logical_and(feature >= group, feature < group + D // GROUPS), 1.0, 0.0)
    feature = lax.broadcasted_iota(jnp.int32, (256, D), 1)
    row = lax.broadcasted_iota(jnp.int32, (256, D), 0)
    group = jnp.where(row >= 128, row - 128, row) * (D // GROUPS)
    wide = jnp.where(jnp.logical_and(feature >= group, feature < group + D // GROUPS), 1.0, 0.0)
    return ones.astype(BF16), wide.astype(BF16)


SHARE = 1.0 / (D // GROUPS)


def opening_kernel(
    length, cuts,
    hidden_in, drive, forget, outgate, mixout, gate, up, down, part0, part1, part2, part3, part4,
    n1_out, pd_out, pg_out, lam_out, s_out, mixed_out, normed_out, rstd_out, middle_out, n2_out, wdfg_out, wo_out, wau_out, wb_out, vec_out,
    raw, stage, wdfg, wo, wau, wb, vec_rows, vec, n1, pd_low, pg_low, lam, src, states, carry, mixed, normed, rstd, n2,
    ones_ref, wide_ref, hidden, out_sems, in_sem, send_sems, recv_sems,
):
    at = Places()
    coming = pltpu.make_async_copy(hidden_in, hidden, in_sem)
    coming.start()
    gather = Gather(at, raw, cuts, send_sems, recv_sems)
    own = raw.at[at.core, at.chip]
    vec_rows[0:8] = jnp.zeros((8, 128), F32)
    for ref, (lane, width) in zip((part0, part1, part2, part3, part4), VECTOR_PARTS):
        vec_rows[0:1, lane : lane + width] = ref[...].astype(F32)
    for ref, part in ((drive, DRIVE), (outgate, OUTGATE), (mixout, MIXOUT), (gate, GATE), (up, UP), (down, DOWN)):
        own[part[0] : part[0] + ref.shape[0]] = pack(ref, stage, part[2]).astype(BF16)
    own[FORGET[0] : FORGET[0] + 80] = jnp.concatenate([pack(forget, stage, 3), vec_rows[0:8]], axis=0).astype(BF16)
    at.barrier()

    copies = []

    def give(index, source, target):
        copy = pltpu.make_async_copy(source, target, out_sems.at[index])
        copy.start()
        copies.append(copy)

    def prepare():
        ones_ref[...], wide_ref[...] = group_matrices()

    def vectors():
        for chip in range(16):
            for core in range(2):
                block = raw[core, chip, FORGET[0] + 64 : FORGET[0] + 80].astype(F32)
                vec_rows[2 * chip + core : 2 * chip + core + 1] = block[8:9]
        rows = vec_rows[...].astype(BF16)
        for index, (lane, width) in enumerate(VECTOR_PARTS):
            vec[index : index + 1, 0 : 32 * width] = vector_of(rows, lane, width)
        phase = vec[4:5, 0:C]
        vec[5:6, 0:C] = jnp.cos(phase)
        vec[6:7, 0:C] = jnp.sin(phase)
        vec[7:8] = jnp.zeros((1, D), F32)
        give(0, vec, vec_out)
        give(1, wdfg, wdfg_out)
        coming.wait()

    def project(t):
        rows = slice(t * TILE, (t + 1) * TILE)
        x = hidden[rows].astype(F32)
        unit = (x * lax.rsqrt(jnp.mean(x * x, axis=1, keepdims=True) + norm_eps) * vec[0:1]).astype(BF16)
        n1[rows] = unit
        pre = product(unit, wdfg[...])
        pd, pf, pg = pre[:, :D], pre[:, D : D + C], pre[:, D + C :]
        pd_low[rows] = pd.astype(BF16)
        pg_low[rows] = pg.astype(BF16)
        keep = lower_bound + (1.0 - lower_bound) * sigmoid(pf + vec[3:4, 0:C])
        driven = pd * sigmoid(pd)
        inflow = 1.0 - keep
        for c in range(CB):
            lam[c, rows] = keep[:, col(c)]
            src[c, rows] = inflow[:, col(c)] * driven[:, col(c)]
            src[CB + c, rows] = inflow[:, col(c)] * driven[:, col(CB + c)]

    def projected():
        give(2, n1, n1_out)
        give(3, pd_low, pd_out)
        give(4, pg_low, pg_out)
        give(5, lam, lam_out)

    def scan():
        scan_forward(length, lam, src, states, vec[5:6, 0:C], vec[6:7, 0:C], carry)
        give(6, states, s_out)

    def mix(t):
        rows = slice(t * TILE, (t + 1) * TILE)
        ones, wide = ones_ref[...], wide_ref[...]
        y = jnp.concatenate([states[c, rows] for c in range(NB)], axis=1)
        centered = y - group_spread(group_sum(y, ones, True) * SHARE, wide)
        scale = split(lax.rsqrt(group_sum(centered * centered, ones, False) * SHARE + group_eps))
        rstd[rows] = scale
        unit = centered * product(scale, wide)
        normed[rows] = unit.astype(BF16)
        low = (unit * vec[2:3] * sigmoid(pg_low[rows].astype(F32))).astype(BF16)
        mixed[rows] = low
        middle = hidden[rows].astype(F32) + product(low, wo[...])
        for c in range(NB):
            src[c, rows] = middle[:, col(c)]
        q = lax.rsqrt(jnp.mean(middle * middle, axis=1, keepdims=True) + norm_eps)
        n2[rows] = (middle * q * vec[1:2]).astype(BF16)

    def mixed_rows(low, high, index):
        rows = pl.ds(low * TILE, (high - low) * TILE)
        for source, target in ((mixed, mixed_out), (normed, normed_out), (rstd, rstd_out), (n2, n2_out)):
            give(index, source.at[rows], target.at[rows])
            index += 1
        give(index, src.at[:, rows], middle_out.at[:, rows])

    tiles = length // TILE
    steps = Steps()
    whole = gather.schedule(steps)

    def place(k, part, target, column, cost):
        return steps.add(lambda: assemble(raw, part, target, column), whole[k : k + 1], cost)

    ready = steps.add(prepare, [], 0.3)
    first = [place(0, DRIVE, wdfg, 0, 0.4), place(1, OUTGATE, wdfg, D + C, 0.4), place(2, FORGET, wdfg, D, 0.3)]
    last = steps.add(vectors, first, 1.0)
    for t in range(tiles):
        last = steps.add(functools.partial(project, t), [last], 0.9)
    steps.add(projected, [last], 0.2)
    last = steps.add(scan, [last], 3.4)
    wo_ready = place(3, MIXOUT, wo, 0, 0.4)
    for t in range(tiles):
        last = steps.add(functools.partial(mix, t), [last, wo_ready, ready], 1.1)
        if t == tiles // 2:
            steps.add(functools.partial(mixed_rows, 0, t + 1, 7), [last], 0.3)
    steps.add(functools.partial(mixed_rows, tiles // 2 + 1, tiles, 12), [last], 0.3)
    wa_ready, wu_ready, wb_ready = place(4, GATE, wau, 0, 0.8), place(5, UP, wau, FF, 0.8), place(6, DOWN, wb, 0, 0.8)
    for index, source, target, needs in ((17, wo, wo_out, [wo_ready]), (18, wau, wau_out, [wa_ready, wu_ready]), (19, wb, wb_out, [wb_ready])):
        steps.add(functools.partial(give, index, source, target), needs, 0.1)
    steps.run(256, *GATHER_RATES)
    gather.sends.finish()
    for copy in copies:
        copy.wait()


def opening(hidden, weights, parts):
    length = hidden.shape[0]
    cuts = cuts_of(GATHER_SIZES)
    vmem = pl.BlockSpec(memory_space=pltpu.VMEM)
    hbm = pl.BlockSpec(memory_space=pl.ANY)
    low, wide = ((length, D), BF16), ((NB, length, 128), F32)
    shapes = [
        low, low, low, ((CB, length, 128), F32), wide, low, low, ((length, 256), BF16), wide, low,
        ((D, WDFG), BF16), ((D, D), BF16), ((D, 2 * FF), BF16), ((FF, D), BF16), ((8, D), F32),
    ]
    scratch = [
        ((2, 16, ROWS, 128), BF16), ((288, 128), F32), ((D, WDFG), BF16), ((D, D), BF16), ((D, 2 * FF), BF16), ((FF, D), BF16),
        ((32, 128), F32), ((8, D), F32), low, low, low, ((CB, length, 128), F32), wide, wide, ((NB, SEGMENTS, 128), F32),
        low, low, ((length, 256), BF16), low, ((D, 128), BF16), ((256, D), BF16), low,
    ]
    dma = pltpu.SemaphoreType.DMA
    count = len(cuts), len(GATHER_NAMES)
    return pl.pallas_call(
        functools.partial(opening_kernel, length, cuts),
        out_shape=[jax.ShapeDtypeStruct(*s) for s in shapes],
        in_specs=[hbm] + [vmem] * 12,
        out_specs=[hbm] * len(shapes),
        scratch_shapes=[pltpu.VMEM(*s) for s in scratch] + [dma((20,)), dma, dma(count), dma(count)],
        compiler_params=pltpu.CompilerParams(collective_id=0, has_side_effects=True, vmem_limit_bytes=63 * MIB),
    )(hidden, *weights, *(part[None] for part in parts))


MID = 224


def feed_kernel(g_ref, n2_ref, middle_ref, wau, wb, vec, out_ref, units_ref, dpau_ref, dm_ref, dmiddle_ref, sums_ref):
    @pl.when(pl.program_id(0) == 0)
    def _():
        sums_ref[...] = jnp.zeros_like(sums_ref)

    second_gain = vec[1:2]
    g = g_ref[...]
    middle = jnp.concatenate([middle_ref[c] for c in range(NB)], axis=1)
    pre = product(n2_ref[...], wau[...])
    pa, pu = pre[:, :FF], pre[:, FF:]
    sa = sigmoid(pa)
    silu = pa * sa
    units = (silu * pu).astype(BF16)
    units_ref[...] = units
    out_ref[...] = (middle + product(units, wb[...])).astype(BF16)
    dunits = back_product(g, wb[...])
    dpa = (dunits * pu * (sa * (1.0 + pa * (1.0 - sa)))).astype(BF16)
    dpu = (dunits * silu).astype(BF16)
    dpau = jnp.concatenate([dpa, dpu], axis=1)
    dpau_ref[...] = dpau
    dn2 = back_product(dpau, wau[...])
    q = lax.rsqrt(jnp.mean(middle * middle, axis=1, keepdims=True) + norm_eps)
    scaled = middle * q
    along = dn2 * scaled
    mean = jnp.mean(along * second_gain, axis=1, keepdims=True)
    dmiddle = g.astype(F32) + q * (second_gain * dn2 - scaled * mean)
    dmiddle_ref[...] = dmiddle
    dm_ref[...] = dmiddle.astype(BF16)
    sums_ref[0:1] += jnp.sum(along, axis=0, keepdims=True)


def feed(cotangent, n2, middle, wau, wb, vec):
    length = n2.shape[0]
    rows = lambda width: pl.BlockSpec((MID, width), lambda t: (t, 0))
    cols = pl.BlockSpec((NB, MID, 128), lambda t: (0, t, 0))
    whole = lambda a: pl.BlockSpec(a.shape, lambda t: (0, 0), pipeline_mode=pl.Buffered(1))
    outs = [(D, BF16), (FF, BF16), (2 * FF, BF16), (D, BF16), (D, F32)]
    return pl.pallas_call(
        feed_kernel,
        grid=(length // MID,),
        out_shape=[jax.ShapeDtypeStruct((length, w), t) for w, t in outs] + [jax.ShapeDtypeStruct((8, D), F32)],
        in_specs=[rows(D), rows(D), cols, whole(wau), whole(wb), whole(vec)],
        out_specs=[rows(w) for w, _ in outs] + [pl.BlockSpec((8, D), lambda t: (0, 0))],
        compiler_params=pltpu.CompilerParams(vmem_limit_bytes=63 * MIB),
    )(cotangent, n2, middle, wau, wb, vec)


CHUNKS = ((1088, 144), (1232, 144), (512, 144), (656, 144), (800, 144), (944, 144), (368, 144), (0, 144), (144, 144), (288, 80))
PARTS = tuple(part + (part[2] // split, i * (part[2] // split)) for part, split in ((DOWN, 2), (GATE, 2), (UP, 2)) for i in range(2)) + tuple(
    part + (part[2], 0) for part in (MIXOUT, DRIVE, OUTGATE, FORGET)
)
SCATTER_NAMES = ("c", "p", "s", "t", "f", "z3", "z2", "z1", "d1", "d2", "d3")
DIRECT = 7


class Scatter:
    SLOTS = {"p": 0, "t": 2, "s": 4, "f": 8, "z3": 12, "z2": 14, "z1": 16, "d1": 12, "d2": 13, "d3": 14}

    def __init__(self, places, stage, wide, narrow, deliver, send_sems, recv_sems):
        self.at, self.stage, self.wide, self.narrow, self.deliver = places, stage, wide, narrow, deliver
        self.sends = Sends(SCATTER_NAMES, send_sems, recv_sems)

    def rows(self, k):
        return slice(CHUNKS[k][0], CHUNKS[k][0] + CHUNKS[k][1])

    def add(self, k, first, count, received, slot):
        rows, core = self.rows(k), self.at.core

        def one(i, _):
            self.stage[core, first + i, rows] += received[slot + i, rows]
            return 0

        lax.fori_loop(0, count, one, 0, unroll=2)

    def slot(self, name, k):
        return 0 if name == "t" and k >= DIRECT else self.SLOTS[name]

    def send(self, name, k, first, count, partner, when=None):
        rows = self.rows(k)
        slot = self.slot(name, k)
        self.sends.start(
            name, k, self.stage.at[self.at.core, pl.ds(first, count), rows], self.narrow.at[slot : slot + count, rows], partner, when
        )

    def merge(self, name, k, first, count):
        self.sends.arrived(name, k)
        self.add(k, first, count, self.narrow, self.slot(name, k))

    def cores(self, k):
        rows = self.rows(k)
        self.sends.start("c", k, self.stage.at[1 - self.at.core, :, rows], self.wide.at[:, rows], self.at.sibling)

    def pair(self, k):
        at = self.at
        self.sends.arrived("c", k)
        if k < DIRECT:
            away = at.dcol + 2 - at.half
            self.add(k, away, 2, self.wide, away)
            self.send("p", k, away, 2, at.mate)
        else:
            self.add(k, at.dcol, 4, self.wide, at.dcol)
            self.send("t", k, at.dcol, 4, at.second)
        self.add(k, at.scol, 4, self.wide, at.scol)
        self.send("s", k, at.scol, 4, at.second)
        if k < DIRECT:
            self.add(k, at.dcol + at.half, 2, self.wide, at.dcol + at.half)
        self.add(k, at.fcol, 4, self.wide, at.fcol)
        self.add(k, at.col, 4, self.wide, at.col)

    def diagonal(self, k):
        at = self.at
        self.merge("p", k, at.dcol + at.half, 2)
        self.send("t", k, at.dcol + at.half, 2, at.second)

    def second(self, k):
        at = self.at
        if k < DIRECT:
            self.merge("t", k, at.fcol + at.half, 2)
        else:
            self.merge("t", k, at.fcol, 4)
        self.send("f", k, at.fcol, 4, at.first)
        self.merge("s", k, at.col, 4)

    def first(self, k):
        at = self.at
        self.merge("f", k, at.col, 4)
        if k < DIRECT:
            self.send("z3", k, at.far, 2, at.mate, at.outer)
        else:
            for d, name in enumerate(("d1", "d2", "d3")):
                self.send(name, k, at.col + (at.z + d + 1) % 4, 1, at.along[d])

    def relay(self, k):
        at = self.at

        @pl.when(at.inner)
        def _():
            self.merge("z3", k, at.far, 2)

        self.send("z2", k, at.far, 2, at.other, at.inner)

    def near(self, k):
        at = self.at

        @pl.when(at.inner)
        def _():
            self.merge("z2", k, at.near, 2)

        self.send("z1", k, at.col + (at.z ^ 1), 1, at.mate)

    def last(self, k):
        rows, at = self.rows(k), self.at
        total = self.stage[at.core, at.chip, rows].astype(F32)
        for name in ("z1",) if k < DIRECT else ("d1", "d2", "d3"):
            self.sends.arrived(name, k)
            total += self.narrow[self.SLOTS[name], rows].astype(F32)
        self.deliver(k, total)

    def schedule(self, steps, k, made):
        n = 2 * CHUNKS[k][1]

        def step(run, needs, cost, transfers, stage):
            return steps.add(functools.partial(run, k), needs, cost, transfers, (0, k, -stage))

        cores = step(self.cores, [made], 0.2, [(CORE_LINKS, 8 * n)], 0)
        if k < DIRECT:
            pair = step(self.pair, [(cores, 0)], 0.8, [(Z_LINK, 2 * n), (PLANE_LINK, 4 * n)], 1)
            diagonal = step(self.diagonal, [(pair, 0)], 0.3, [(PLANE_LINK, 2 * n)], 2)
            second = step(self.second, [(diagonal, 0), (pair, 1)], 0.4, [(PLANE_LINK, 4 * n)], 3)
            first = step(self.first, [(second, 0)], 0.4, [(Z_LINK, 2 * n)], 4)
            relay = step(self.relay, [(first, 0)], 0.3, [(MID_LINK, 2 * n)], 5)
            near = step(self.near, [(relay, 0)], 0.3, [(Z_LINK, n)], 6)
            step(self.last, [(near, 0)], 0.3, [], 7)
        else:
            pair = step(self.pair, [(cores, 0)], 0.8, [(PLANE_LINK, 4 * n), (PLANE_LINK, 4 * n)], 1)
            second = step(self.second, [(pair, 0), (pair, 1)], 0.4, [(PLANE_LINK, 4 * n)], 3)
            first = step(self.first, [(second, 0)], 0.4, [(MID_LINK, 4 * n)], 4)
            step(self.last, [(first, 0)], 0.3, [], 7)


def closing_kernel(
    length,
    units, g, n2, dpau, mixed, dm, n1, pg, normed, rstd, states, lam, pd, hidden, dmiddle, wdfg, wo, vec, sums,
    hidden_grad, packed_out,
    left, right, left2, right2, s_buf, ds_buf, lam_buf, wdfg_buf, wo_buf, x_tile, dm_tile, carry, vec_rows, vec_sums, gain_rows, wide_ref, ones_ref,
    stage, from_core, from_links, load_sems, tile_sems, send_sems, recv_sems,
):
    at = Places()

    def unpack(total, start, rows, blocks, here, first):
        for j in range(here):
            packed_out[pl.ds(start + first + j, rows, stride=blocks)] = total[j * rows : (j + 1) * rows]

    def deliver(k, total):
        unpack(total, *PARTS[k])
        if k == 9:
            packed_out[VECTORS : VECTORS + 8] = total[72:80]

    scatter = Scatter(at, stage, from_core, from_links, deliver, send_sems, recv_sems)
    loads = {}

    def load(key, source, target):
        copy = pltpu.make_async_copy(source, target, load_sems.at[len(loads)])
        copy.start()
        loads[key] = copy

    def need(*keys):
        for key in keys:
            loads[key].wait()

    load("units", units, left)
    load("g", g, right)
    load("n2", n2, left2)
    load("dpau", dpau, right2)
    load("s", states, s_buf.at[:, pl.ds(8, length)])
    load("lam", lam, lam_buf)
    load("wo", wo, wo_buf)
    load("wdfg", wdfg, wdfg_buf)
    at.barrier()

    def weight_chunk(source, source_col, rows, per, other, other_col, blocks, start, tail=None, by=None):
        for m in range(rows // 384):
            value = outer_sum(
                source[:, source_col + 384 * m : source_col + 384 * (m + 1)], other[:, other_col : other_col + 128 * blocks]
            )
            if by is not None:
                own = slice(384 * m, 384 * (m + 1))
                total = value[:, col(0)] * by[own, other_col : other_col + 128].astype(F32)
                for j in range(1, blocks):
                    total += value[:, col(j)] * by[own, other_col + 128 * j : other_col + 128 * (j + 1)].astype(F32)
                if other_col == 0:
                    gain_rows[own] = total
                else:
                    gain_rows[own] += total
            for i in range(384 // per):
                index = m * (384 // per) + i
                core, chip = index % 2, index // 2
                parts = [value[i * per : (i + 1) * per, col(j)] for j in range(blocks)]
                if tail is not None:
                    parts += [tail[index : index + 1], jnp.zeros((7, 128), F32)]
                block = jnp.concatenate(parts, axis=0)
                stage[core, chip, start : start + block.shape[0]] = block.astype(BF16)

    def down(i):
        if i == 0:
            need("units", "g")
        weight_chunk(left, 0, FF, 48, right, 384 * i, 3, DOWN[0] + 144 * i)
        if i == 1:
            load("mixed", mixed, left.at[:, 0:D])
            load("n1", n1, left.at[:, D : 2 * D])
            load("dm", dm, right)

    def gate_up(i):
        if i == 0:
            need("n2", "dpau")
        weight_chunk(left2, 0, D, 24, right2, D * i, 6, GATE[0] + 144 * i)
        if i == 3:
            load("pg", pg, right2.at[:, D + C : WDFG])
            load("normed", normed, right2.at[:, WDFG : WDFG + D])
            load("rstd", rstd, right2.at[:, WDFG + D : WDFG + D + 256])
            load("pd", pd, left2)
            ones_ref[...], wide_ref[...] = group_matrices()
            vec_sums[...] = jnp.zeros_like(vec_sums)

    def mixout():
        need("mixed", "dm")
        weight_chunk(left, 0, D, 24, right, 0, 6, MIXOUT[0])

    def unmix(t):
        if t == 0:
            need("pg", "normed", "rstd", "wo")
        rows = slice(t * TILE, (t + 1) * TILE)
        ones, wide = ones_ref[...], wide_ref[...]
        group_gain = vec[2:3]
        unit = right2[rows, WDFG : WDFG + D].astype(F32)
        scale = product(right2[rows, WDFG + D : WDFG + D + 256], wide)
        sg = sigmoid(right2[rows, D + C : WDFG].astype(F32))
        dmixed = back_product(right[rows], wo_buf[...])
        both = dmixed * sg
        dunit = both * group_gain
        both = both * unit
        right2[rows, D + C : WDFG] = (both * group_gain * (1.0 - sg)).astype(BF16)
        mean_one = group_spread(group_sum(dunit, ones, False) * SHARE, wide)
        mean_two = group_spread(group_sum(dunit * unit, ones, False) * SHARE, wide)
        ds = scale * (dunit - mean_one - unit * mean_two)
        for c in range(NB):
            ds_buf[c, rows] = ds[:, col(c)]
        vec_sums[3:4] += jnp.sum(both, axis=0, keepdims=True)

    def reverse():
        need("s", "lam")
        scan_backward(length, lam_buf, s_buf, ds_buf, vec[5:6, 0:C], vec[6:7, 0:C], carry, vec_sums)

    def gates(t):
        if t == 0:
            need("pd")
        rows = slice(t * TILE, (t + 1) * TILE)
        pre = left2[rows].astype(F32)
        sig = sigmoid(pre)
        driven = pre * sig
        slope = sig * (1.0 + pre * (1.0 - sig))
        for c in range(CB):
            gate = lam_buf[c, rows]
            inflow = 1.0 - gate
            dgate = s_buf[c, t * TILE + 8 : (t + 1) * TILE + 8]
            for half in (c, CB + c):
                grad = ds_buf[half, rows]
                dgate -= grad * driven[:, col(half)]
                right2[rows, col(half)] = (inflow * grad * slope[:, col(half)]).astype(BF16)
            dpf = dgate * ((gate - lower_bound) * inflow * (1.0 / (1.0 - lower_bound)))
            vec_sums[0:1, col(c)] += jnp.sum(dpf, axis=0, keepdims=True)
            right2[rows, col(NB + c)] = dpf.astype(BF16)

    def drive():
        need("n1", "wdfg")
        weight_chunk(left, D, D, 24, right2, 0, 6, DRIVE[0], None, wdfg_buf)

    def outgate():
        weight_chunk(left, D, D, 24, right2, D + C, 6, OUTGATE[0], None, wdfg_buf)

    def forget():
        value = outer_sum(left[:, D : 2 * D], right2[:, D : D + C])
        for c in range(CB):
            gain_rows[...] += value[:, col(c)] * wdfg_buf[:, col(NB + c)].astype(F32)
        high = gain_rows[...].astype(BF16)
        low = (gain_rows[...] - high.astype(F32)).astype(BF16)
        ones = jnp.ones((8, 128), BF16)
        vec_sums[2:3] = (back_product(ones, high) + back_product(ones, low))[0:1] / vec[0:1]
        rows = jnp.zeros((32, 128), F32)
        sources = (vec_sums[2:3], sums[0:1], vec_sums[3:4], vec_sums[0:1, 0:C], vec_sums[1:2, 0:C])
        for (lane, width), source in zip(VECTOR_PARTS, sources):
            total = 32 * width
            mine = jnp.where(own_columns(width, total), jnp.broadcast_to(source, (32, total)), 0.0).astype(BF16)
            rows += back_product(mine, spread(lane, width, total, True))
        vec_rows[...] = rows
        for index in range(32):
            parts = [value[index * 24 : (index + 1) * 24, col(j)] for j in range(3)]
            parts += [vec_rows[index : index + 1], jnp.zeros((7, 128), F32)]
            stage[index % 2, index // 2, FORGET[0] : FORGET[0] + 80] = jnp.concatenate(parts, axis=0).astype(BF16)

    count = length // TILE
    fetched, outgoing = {}, {}

    def fetch(t):
        rows = slice(t * TILE, (t + 1) * TILE)
        a = pltpu.make_async_copy(hidden.at[rows], x_tile.at[t % 2], tile_sems.at[0, t % 2])
        b = pltpu.make_async_copy(dmiddle.at[rows], dm_tile.at[t % 3], tile_sems.at[1, t % 3])
        a.start()
        b.start()
        fetched[t] = (a, b)

    def inputs(t):
        if t == 0:
            fetch(0)
        if t >= 2:
            outgoing[t - 2].wait()
        if t + 1 < count:
            fetch(t + 1)
        for copy in fetched[t]:
            copy.wait()
        rows = slice(t * TILE, (t + 1) * TILE)
        first_gain = vec[0:1]
        x = x_tile[t % 2].astype(F32)
        dn1 = back_product(right2[rows, 0:WDFG], wdfg_buf[...])
        p = lax.rsqrt(jnp.mean(x * x, axis=1, keepdims=True) + norm_eps)
        scaled = x * p
        mean = jnp.mean(dn1 * scaled * first_gain, axis=1, keepdims=True)
        dm_tile[t % 3] += p * (first_gain * dn1 - scaled * mean)
        copy = pltpu.make_async_copy(dm_tile.at[t % 3], hidden_grad.at[rows], tile_sems.at[2, t % 3])
        copy.start()
        outgoing[t] = copy

    steps = Steps()
    last = None

    def job(run, cost, k=None):
        nonlocal last
        last = steps.add(run, [] if last is None else [last], cost)
        if k is not None:
            scatter.schedule(steps, k, last)

    def tiled(run, cost):
        for t in range(count):
            job(functools.partial(run, t), cost)

    for i in range(2):
        job(functools.partial(down, i), 2.5, i)
    for i in range(4):
        job(functools.partial(gate_up, i), 2.5, 2 + i)
    job(mixout, 2.5, 6)
    tiled(unmix, 1.1)
    job(reverse, 4.5)
    tiled(gates, 0.4)
    job(drive, 2.5, 7)
    job(outgate, 2.5, 8)
    job(forget, 2.5, 9)
    tiled(inputs, 1.1)
    steps.run(256, *SCATTER_RATES)
    for t in (count - 2, count - 1):
        outgoing[t].wait()
    scatter.sends.finish()


def scan_backward(length, lam, states, ds, cos, sin, carry, vec_sums):
    steps = length // SEGMENTS
    zero = jnp.zeros((SEGMENTS, 128), F32)

    def rows(j):
        return pl.ds(j, SEGMENTS, stride=steps)

    def first(i, kept):
        j = steps - 1 - i
        prod, re, im = kept
        new_p, new_re, new_im = [], [], []
        for c in range(CB):
            gate = lam[c, rows(j)]
            g_re, g_im = ds[c, rows(j)] + re[c], ds[CB + c, rows(j)] + im[c]
            new_p.append(prod[c] * gate)
            new_re.append(gate * (cos[:, col(c)] * g_re + sin[:, col(c)] * g_im))
            new_im.append(gate * (cos[:, col(c)] * g_im - sin[:, col(c)] * g_re))
        return tuple(new_p), tuple(new_re), tuple(new_im)

    ones = (jnp.ones((SEGMENTS, 128), F32),) * CB
    prod, re, im = lax.fori_loop(0, steps, first, (ones, (zero,) * CB, (zero,) * CB))
    turn_re, turn_im = turned(cos, -sin, steps)
    for c in range(CB):
        p_re, p_im = prod[c] * turn_re[:, col(c)], prod[c] * turn_im[:, col(c)]
        at_re = at_im = jnp.zeros((1, 128), F32)
        for k in reversed(range(SEGMENTS)):
            carry[c, k : k + 1] = at_re
            carry[CB + c, k : k + 1] = at_im
            row = slice(k, k + 1)
            at_re, at_im = (
                p_re[row] * at_re - p_im[row] * at_im + re[c][row],
                p_re[row] * at_im + p_im[row] * at_re + im[c][row],
            )
    for c in range(NB):
        states[c, 0:8] = jnp.zeros((8, 128), F32)

    def step(at_rows, before, kept):
        re, im, phase = kept
        new_re, new_im, new_phase = [], [], []
        for c in range(CB):
            gate = lam[c, at_rows]
            g_re, g_im = ds[c, at_rows] + re[c], ds[CB + c, at_rows] + im[c]
            w_re = cos[:, col(c)] * g_re + sin[:, col(c)] * g_im
            w_im = cos[:, col(c)] * g_im - sin[:, col(c)] * g_re
            new_re.append(gate * w_re)
            new_im.append(gate * w_im)
            s_re, s_im = before(c), before(CB + c)
            new_phase.append(phase[c] + gate * (w_im * s_re - w_re * s_im))
            ds[c, at_rows] = g_re
            ds[CB + c, at_rows] = g_im
            yield c, w_re * s_re + w_im * s_im
        kept[:] = [tuple(new_re), tuple(new_im), tuple(new_phase)]

    opening_rows = [states[c, pl.ds(7, SEGMENTS, stride=steps)] for c in range(NB)]

    def second(i, kept):
        j = steps - 1 - i
        kept = list(kept)
        for c, dgate in step(rows(j), lambda c: states[c, pl.ds(j + 7, SEGMENTS, stride=steps)], kept):
            states[c, pl.ds(j + 8, SEGMENTS, stride=steps)] = dgate
        return tuple(kept)

    start = (tuple(carry[c] for c in range(CB)), tuple(carry[CB + c] for c in range(CB)), (zero,) * CB)
    kept = list(lax.fori_loop(0, steps - 1, second, start))
    for c, dgate in step(rows(0), lambda c: opening_rows[c], kept):
        states[c, pl.ds(8, SEGMENTS, stride=steps)] = dgate
    for c in range(CB):
        vec_sums[1:2, col(c)] = jnp.sum(kept[2][c], axis=0, keepdims=True)


def closing(length, arrays, hidden, dmiddle, wdfg, wo, vec, sums):
    vmem = pl.BlockSpec(memory_space=pltpu.VMEM)
    hbm = pl.BlockSpec(memory_space=pl.ANY)
    dma = pltpu.SemaphoreType.DMA
    scratch = [
        ((length, FF), BF16), ((length, D), BF16), ((length, D), BF16), ((length, 2 * FF), BF16),
        ((NB, length + 8, 128), F32), ((NB, length, 128), F32), ((CB, length, 128), F32), ((D, WDFG), BF16), ((D, D), BF16),
        ((2, TILE, D), BF16), ((3, TILE, D), F32), ((NB, SEGMENTS, 128), F32), ((32, 128), F32), ((8, D), F32),
        ((D, 128), F32), ((256, D), BF16), ((D, 128), BF16),
        ((2, 16, ROWS, 128), BF16), ((16, ROWS, 128), BF16), ((17, ROWS, 128), BF16),
    ]
    sems = len(CHUNKS), len(SCATTER_NAMES)
    return pl.pallas_call(
        functools.partial(closing_kernel, length),
        out_shape=[jax.ShapeDtypeStruct((length, D), F32), jax.ShapeDtypeStruct((ROWS, 128), F32)],
        in_specs=[hbm] * 17 + [vmem] * 2,
        out_specs=[hbm, vmem],
        scratch_shapes=[pltpu.VMEM(*s) for s in scratch] + [dma((17,)), dma((3, 3)), dma(sems), dma(sems)],
        compiler_params=pltpu.CompilerParams(collective_id=1, has_side_effects=True, vmem_limit_bytes=63 * MIB),
    )(*arrays, hidden, dmiddle, wdfg, wo, vec, sums)


PIECES = 7


def handing_kernel(grad, packed, grad_out, drive_out, forget_out, outgate_out, mixout_out, gate_out, up_out, down_out, vec_out, held, sems):
    rows = grad.shape[0] // PIECES
    part = lambda ref, i: ref.at[pl.ds(i * rows, rows)]
    copies = [pltpu.make_async_copy(part(grad, i), part(held, i), sems.at[0, i]) for i in range(PIECES)]
    for copy in copies:
        copy.start()
    for ref, place in (
        (drive_out, DRIVE), (forget_out, FORGET), (outgate_out, OUTGATE), (mixout_out, MIXOUT), (gate_out, GATE), (up_out, UP), (down_out, DOWN)
    ):
        ref[...] = packed[place[0] : place[0] + ref.shape[0]]
    vec_out[...] = packed[VECTORS : VECTORS + 8]
    away = [pltpu.make_async_copy(part(held, i), part(grad_out, i), sems.at[1, i]) for i in range(PIECES)]
    for copy, out in zip(copies, away):
        copy.wait()
        out.start()
    for out in away:
        out.wait()


def handing(grad, packed, shards):
    vmem = pl.BlockSpec(memory_space=pltpu.VMEM)
    hbm = pl.BlockSpec(memory_space=pl.ANY)
    shapes = [grad.shape] + [w.shape for w in shards] + [(8, 128)]
    return pl.pallas_call(
        handing_kernel,
        out_shape=[jax.ShapeDtypeStruct(s, F32) for s in shapes],
        in_specs=[hbm, vmem],
        out_specs=[hbm] + [vmem] * 8,
        scratch_shapes=[pltpu.VMEM(grad.shape, F32), pltpu.SemaphoreType.DMA((2, PIECES))],
        compiler_params=pltpu.CompilerParams(vmem_limit_bytes=63 * MIB),
    )(grad, packed)


def fast(hidden, cotangent, *params):
    weights, parts = params[:7], params[7:]
    n1, pd, pg, lam, states, mixed, normed, rstd, middle, n2, wdfg, wo, wau, wb, vec = opening(hidden, weights, parts)
    out, units, dpau, dm, dmiddle, sums = feed(cotangent, n2, middle, wau, wb, vec)
    arrays = (units, cotangent, n2, dpau, mixed, dm, n1, pg, normed, rstd, states, lam, pd)
    grad, packed = closing(hidden.shape[0], arrays, hidden, dmiddle, wdfg, wo, vec, sums)
    hidden_grad, *grads, row = handing(grad, packed, weights)
    return (out, hidden_grad, *grads) + tuple(row[0, lane : lane + width] for lane, width in VECTOR_PARTS)


SPAN = 56


def rms_scale(values, gain_vec):
    return (
        values * lax.rsqrt(jnp.mean(values * values, axis=1, keepdims=True) + norm_eps) * gain_vec
    )


def combine(earlier, later_term):
    return (
        later_term[0] * earlier[0] - later_term[1] * earlier[1],
        later_term[0] * earlier[1] + later_term[1] * earlier[0],
        later_term[0] * earlier[2] - later_term[1] * earlier[3] + later_term[2],
        later_term[0] * earlier[3] + later_term[1] * earlier[2] + later_term[3],
    )


def block_prefix(block_terms):
    length = block_terms[0].shape[0]
    width = block_terms[0].shape[1]
    current = block_terms
    offset = 1
    while offset < length:
        filler = (
            jnp.ones((offset, width), jnp.float32),
            jnp.zeros((offset, width), jnp.float32),
            jnp.zeros((offset, width), jnp.float32),
            jnp.zeros((offset, width), jnp.float32),
        )
        earlier = tuple(
            (
                jnp.concatenate([front, member[: length - offset]], axis=0)
                for front, member in zip(filler, current)
            )
        )
        current = combine(earlier, current)
        offset = offset * 2
    return current


def mixer_core(drive_pre, forget_pre, outgate_pre, phase_angle, forget_bias, group_gain):
    length = drive_pre.shape[0]
    features = drive_pre.shape[1]
    channels = features // 2
    blocks = length // SPAN
    driven = jax.nn.silu(drive_pre)
    retain = lower_bound + (1.0 - lower_bound) * jax.nn.sigmoid(forget_pre + forget_bias)
    rotate_re = retain * jnp.cos(phase_angle)
    rotate_im = retain * jnp.sin(phase_angle)
    inflow = 1.0 - retain
    source_re = inflow * driven[:, :channels]
    source_im = inflow * driven[:, channels:]
    pieces = tuple(
        (
            member.reshape(blocks, SPAN, channels)
            for member in (rotate_re, rotate_im, source_re, source_im)
        )
    )

    def advance(carried, block_terms):
        summed = block_prefix(block_terms)
        state_re = summed[0] * carried[0] - summed[1] * carried[1] + summed[2]
        state_im = summed[0] * carried[1] + summed[1] * carried[0] + summed[3]
        return ((state_re[-1], state_im[-1]), (state_re, state_im))

    initial = (jnp.zeros((channels,), jnp.float32), jnp.zeros((channels,), jnp.float32))
    _, (states_re, states_im) = lax.scan(jax.checkpoint(advance), initial, pieces)
    joined = jnp.concatenate(
        [states_re.reshape(length, channels), states_im.reshape(length, channels)], axis=1
    )
    grouped = joined.reshape(length, GROUPS, features // GROUPS)
    centered = grouped - jnp.mean(grouped, axis=2, keepdims=True)
    normed = centered * lax.rsqrt(jnp.mean(centered * centered, axis=2, keepdims=True) + group_eps)
    return normed.reshape(length, features) * group_gain * jax.nn.sigmoid(outgate_pre)


def unpack(gathered):
    targets = ((D, D), (D, C), (D, D), (D, D), (D, FF), (D, FF), (FF, D))
    matrices = tuple(
        (gathered[position].reshape(target) for position, target in enumerate(targets))
    )
    vectors = tuple((member.astype(jnp.float32) for member in gathered[7:]))
    return matrices + vectors


def local(
    hidden,
    cotangent,
    drive_weight,
    forget_weight,
    outgate_weight,
    mixout_weight,
    gate_weight,
    up_weight,
    down_weight,
    first_gain,
    second_gain,
    group_gain,
    forget_bias,
    phase_angle,
):
    params = unpack(
        (
            lax.all_gather(drive_weight, AXES, axis=0, tiled=True),
            lax.all_gather(forget_weight, AXES, axis=0, tiled=True),
            lax.all_gather(outgate_weight, AXES, axis=0, tiled=True),
            lax.all_gather(mixout_weight, AXES, axis=0, tiled=True),
            lax.all_gather(gate_weight, AXES, axis=0, tiled=True),
            lax.all_gather(up_weight, AXES, axis=0, tiled=True),
            lax.all_gather(down_weight, AXES, axis=0, tiled=True),
            lax.all_gather(first_gain, AXES, axis=0, tiled=True),
            lax.all_gather(second_gain, AXES, axis=0, tiled=True),
            lax.all_gather(group_gain, AXES, axis=0, tiled=True),
            lax.all_gather(forget_bias, AXES, axis=0, tiled=True),
            lax.all_gather(phase_angle, AXES, axis=0, tiled=True),
        )
    )
    inputs = hidden.astype(jnp.float32)
    normed_float, pull_first = jax.vjp(rms_scale, inputs, params[7])
    normed_one = normed_float.astype(jnp.bfloat16)
    drive_pre = product(normed_one, params[0])
    forget_pre = product(normed_one, params[1])
    outgate_pre = product(normed_one, params[2])
    mixed_float, pull_mixer = jax.vjp(
        mixer_core, drive_pre, forget_pre, outgate_pre, params[11], params[10], params[9]
    )
    mixed = mixed_float.astype(jnp.bfloat16)
    middle = inputs + product(mixed, params[3])
    second_float, pull_second = jax.vjp(rms_scale, middle, params[8])
    normed_two = second_float.astype(jnp.bfloat16)
    gate_pre = product(normed_two, params[4])
    up_pre = product(normed_two, params[5])
    gate_sig = jax.nn.sigmoid(gate_pre)
    silu_gate = gate_pre * gate_sig
    hidden_units = (silu_gate * up_pre).astype(jnp.bfloat16)
    layer_out = (middle + product(hidden_units, params[6])).astype(jnp.bfloat16)
    back_params = unpack(
        (
            lax.all_gather(drive_weight, AXES, axis=0, tiled=True),
            lax.all_gather(forget_weight, AXES, axis=0, tiled=True),
            lax.all_gather(outgate_weight, AXES, axis=0, tiled=True),
            lax.all_gather(mixout_weight, AXES, axis=0, tiled=True),
            lax.all_gather(gate_weight, AXES, axis=0, tiled=True),
            lax.all_gather(up_weight, AXES, axis=0, tiled=True),
            lax.all_gather(down_weight, AXES, axis=0, tiled=True),
            lax.all_gather(first_gain, AXES, axis=0, tiled=True),
            lax.all_gather(second_gain, AXES, axis=0, tiled=True),
            lax.all_gather(group_gain, AXES, axis=0, tiled=True),
            lax.all_gather(forget_bias, AXES, axis=0, tiled=True),
            lax.all_gather(phase_angle, AXES, axis=0, tiled=True),
        )
    )
    units_back = back_product(cotangent, back_params[6])
    down_grad = outer_sum(hidden_units, cotangent)
    slope = gate_sig * (1.0 + gate_pre * (1.0 - gate_sig))
    gate_back = (units_back * up_pre * slope).astype(jnp.bfloat16)
    up_back = (units_back * silu_gate).astype(jnp.bfloat16)
    gate_grad = outer_sum(normed_two, gate_back)
    up_grad = outer_sum(normed_two, up_back)
    second_back = back_product(gate_back, back_params[4]) + back_product(up_back, back_params[5])
    middle_part, secondgain_grad = pull_second(second_back)
    middle_back = cotangent.astype(jnp.float32) + middle_part
    middle_low = middle_back.astype(jnp.bfloat16)
    mixout_grad = outer_sum(mixed, middle_low)
    mixed_back = back_product(middle_low, back_params[3])
    drive_back, forget_back, outgate_back, phase_grad, bias_grad, groupgain_grad = pull_mixer(
        mixed_back
    )
    drive_low = drive_back.astype(jnp.bfloat16)
    forget_low = forget_back.astype(jnp.bfloat16)
    outgate_low = outgate_back.astype(jnp.bfloat16)
    drive_grad = outer_sum(normed_one, drive_low)
    forget_grad = outer_sum(normed_one, forget_low)
    outgate_grad = outer_sum(normed_one, outgate_low)
    first_back = (
        back_product(drive_low, back_params[0])
        + back_product(forget_low, back_params[1])
        + back_product(outgate_low, back_params[2])
    )
    input_part, firstgain_grad = pull_first(first_back)
    hidden_grad = middle_back + input_part
    all_terms = (
        drive_grad.reshape(-1, 128),
        forget_grad.reshape(-1, 128),
        outgate_grad.reshape(-1, 128),
        mixout_grad.reshape(-1, 128),
        gate_grad.reshape(-1, 128),
        up_grad.reshape(-1, 128),
        down_grad.reshape(-1, 128),
        firstgain_grad,
        secondgain_grad,
        groupgain_grad,
        bias_grad,
        phase_grad,
    )
    sums = (
        lax.psum_scatter(all_terms[0], AXES, scatter_dimension=0, tiled=True),
        lax.psum_scatter(all_terms[1], AXES, scatter_dimension=0, tiled=True),
        lax.psum_scatter(all_terms[2], AXES, scatter_dimension=0, tiled=True),
        lax.psum_scatter(all_terms[3], AXES, scatter_dimension=0, tiled=True),
        lax.psum_scatter(all_terms[4], AXES, scatter_dimension=0, tiled=True),
        lax.psum_scatter(all_terms[5], AXES, scatter_dimension=0, tiled=True),
        lax.psum_scatter(all_terms[6], AXES, scatter_dimension=0, tiled=True),
        lax.psum_scatter(all_terms[7], AXES, scatter_dimension=0, tiled=True),
        lax.psum_scatter(all_terms[8], AXES, scatter_dimension=0, tiled=True),
        lax.psum_scatter(all_terms[9], AXES, scatter_dimension=0, tiled=True),
        lax.psum_scatter(all_terms[10], AXES, scatter_dimension=0, tiled=True),
        lax.psum_scatter(all_terms[11], AXES, scatter_dimension=0, tiled=True),
    )
    return (
        layer_out,
        hidden_grad,
        sums[0],
        sums[1],
        sums[2],
        sums[3],
        sums[4],
        sums[5],
        sums[6],
        sums[7],
        sums[8],
        sums[9],
        sums[10],
        sums[11],
    )


def solution(mesh):
    rows, flat = P(AXES, None), P(AXES)
    step = fast if tuple(mesh.shape[a] for a in AXES) == (4, 8) else local
    return jax.shard_map(
        step, mesh=mesh, in_specs=(rows,) * 9 + (flat,) * 5, out_specs=(rows,) * 9 + (flat,) * 5, check_vma=False
    )
```

```python
import functools

import jax
import jax.numpy as jnp
from jax import lax
from jax.experimental import pallas as pl
from jax.experimental.pallas import tpu as pltpu
from jax.sharding import PartitionSpec as P

D = 768
C = 384
FF = 1536
GROUPS = 8
NB = D // 128
CB = C // 128

lower_bound = 0.25
norm_eps = 1e-06
group_eps = 1e-05

F32 = jnp.float32
BF16 = jnp.bfloat16
MESH = pl.DeviceIdType.MESH
MIB = 2**20
AXES = "dp", "fsdp"

DRIVE = (0, 24, 6)
OUTGATE = (144, 24, 6)
FORGET = (288, 24, 3)
VECTORS = 360
MIXOUT = (368, 24, 6)
GATE = (512, 24, 12)
UP = (800, 24, 12)
DOWN = (1088, 48, 6)
ROWS = 1376
VECTOR_PARTS = ((0, 24), (24, 24), (48, 24), (72, 12), (84, 12))
WDFG = 2 * D + C

TILE = 224
SEGMENTS = 16


def sigmoid(t):
    return 0.5 * jnp.tanh(0.5 * t) + 0.5


def product(left, right):
    return jnp.dot(left, right, preferred_element_type=F32)


def back_product(left, right):
    return lax.dot_general(left, right, (((1,), (1,)), ((), ())), preferred_element_type=F32)


def outer_sum(left, right):
    return lax.dot_general(left, right, (((0,), (0,)), ((), ())), preferred_element_type=F32)


def coords():
    dp = lax.axis_index(AXES[0])
    fsdp = lax.axis_index(AXES[1])
    return dp // 2, dp % 2, fsdp // 2, fsdp % 2


def device(y, x, z, core):
    return (y * 2 + x, z * 2 + core)


CORE_LINK = 550e3
CORE_HOP = 1.5
GATHER_RATES = 75e3, 8.0
SCATTER_RATES = 92e3, 2.5
WINDOW = 4


Z_LINK, MID_LINK, PLANE_LINK, CORE_LINKS = range(4)


class Steps:
    def __init__(self):
        self.steps = []

    def add(self, run, needs, cost, transfers=(), rank=None):
        number = len(self.steps)
        self.steps.append((run, needs, cost, transfers, rank or (1, number)))
        return number

    def run(self, width, link_rate, hop):
        ready_at, free, now = {}, {}, 0.0
        pending = list(range(len(self.steps)))
        while pending:
            at = {n: max([ready_at[d] for d in self.steps[n][1]], default=0.0) for n in pending if all(d in ready_at for d in self.steps[n][1])}
            able = [n for n, t in at.items() if t <= now]
            if not able:
                now = min(at.values())
                continue
            chosen = min(able, key=lambda n: self.steps[n][4])
            pending.remove(chosen)
            run, _, cost, transfers, _ = self.steps[chosen]
            run()
            now += cost
            for index, (link, size) in enumerate(transfers):
                rate, wait = (CORE_LINK, CORE_HOP) if link == CORE_LINKS else (link_rate, hop)
                free[link] = max(now, free.get(link, 0.0)) + size * width / rate
                ready_at[chosen, index] = free[link] + wait
            ready_at[chosen] = now


class Places:
    def __init__(self):
        y, x, z, c = coords()
        self.z, self.core = z, c
        fy = jnp.where(c == 0, 1 - y, y)
        fx = jnp.where(c == 0, x, 1 - x)
        sy = jnp.where(c == 0, y, 1 - y)
        sx = jnp.where(c == 0, 1 - x, x)
        self.first = device(fy, fx, z, c)
        self.second = device(sy, sx, z, c)
        self.sibling = device(y, x, z, 1 - c)
        self.mate = device(y, x, z ^ 1, c)
        self.other = device(y, x, 3 - z, c)
        self.inner = jnp.logical_or(z == 1, z == 2)
        self.outer = jnp.logical_not(self.inner)
        self.along = [device(y, x, (z + d) % 4, c) for d in (1, 2, 3)]
        self.col = (y * 2 + x) * 4
        self.fcol = (fy * 2 + fx) * 4
        self.scol = (sy * 2 + sx) * 4
        self.dcol = ((1 - y) * 2 + (1 - x)) * 4
        self.half = (z % 2) * 2
        self.chip = self.col + z
        self.near = self.col + (z // 2) * 2
        self.far = self.col + 2 - (z // 2) * 2

    def barrier(self):
        bar = pltpu.get_barrier_semaphore()
        for partner in [self.first, self.second, self.sibling] + self.along:
            pl.semaphore_signal(bar, inc=1, device_id=partner, device_id_type=MESH)
        pl.semaphore_wait(bar, 6)


class Sends:
    def __init__(self, names, send_sems, recv_sems):
        self.index = {name: i for i, name in enumerate(names)}
        self.send_sems, self.recv_sems, self.copies = send_sems, recv_sems, {}

    def start(self, name, k, source, target, partner, when=None, lands=None):
        copy = pltpu.make_async_remote_copy(
            src_ref=source, dst_ref=target, send_sem=self.send_sems.at[k, self.index[name]],
            recv_sem=self.recv_sems.at[k, self.index[lands or name]], device_id=partner, device_id_type=MESH,
        )
        if when is None:
            copy.start()
        else:
            pl.when(when)(copy.start)
        self.copies[name, k] = copy, when

    def arrived(self, name, k):
        self.copies[name, k][0].wait_recv()

    def finish(self):
        for copy, when in self.copies.values():
            if when is None:
                copy.wait_send()
            else:
                pl.when(when)(copy.wait_send)


GATHER_NAMES = ("z1", "z2", "z3", "f0", "f1", "s0", "s1", "s2", "p", "c0", "c1", "c2", "c3", "c4")


class Gather:
    def __init__(self, places, raw, cuts, send_sems, recv_sems):
        self.at, self.raw, self.cuts = places, raw, cuts
        self.sends = Sends(GATHER_NAMES, send_sems, recv_sems)

    def send(self, name, first, count, k, partner, when=None, lands=None):
        low, high = self.cuts[k]
        ref = self.raw.at[self.at.core, pl.ds(first, count), low:high]
        self.sends.start(name, k, ref, ref, partner, when, lands)

    def own(self, k):
        self.send("z1", self.at.chip, 1, k, self.at.mate)

    def near(self, k):
        at = self.at
        self.sends.arrived("z1", k)
        self.send("z2", at.near, 2, k, at.other, at.inner)
        self.send("f0", at.near, 2, k, at.first)
        self.send("s0", at.near, 2, k, at.second)

    def far(self, k):
        at = self.at
        self.sends.arrived("z2", k)
        self.send("z3", at.far, 2, k, at.mate, at.inner, "z2")
        self.send("f1", at.far, 2, k, at.first)
        self.send("s1", at.far, 2, k, at.second)
        self.send("c0", at.col, 4, k, at.sibling)

    def first(self, k):
        at = self.at
        self.sends.arrived("f0", k)
        self.sends.arrived("f1", k)
        self.send("s2", at.fcol + at.half, 2, k, at.second)
        self.send("c1", at.fcol, 4, k, at.sibling)

    def second(self, k):
        at = self.at
        self.sends.arrived("s0", k)
        self.sends.arrived("s1", k)
        self.send("c2", at.scol, 4, k, at.sibling)

    def diagonal(self, k):
        at = self.at
        self.sends.arrived("s2", k)
        self.send("p", at.dcol + at.half, 2, k, at.mate)
        self.send("c3", at.dcol + at.half, 2, k, at.sibling)

    def rest(self, k):
        at = self.at
        self.sends.arrived("p", k)
        self.send("c4", at.dcol + 2 - at.half, 2, k, at.sibling)

    def whole(self, k):
        for name in ("c0", "c1", "c2", "c3", "c4"):
            self.sends.arrived(name, k)

    def schedule(self, steps, cost=0.3):
        done, far = [], []
        for k, (low, high) in enumerate(self.cuts):
            n = 2 * (high - low)

            def step(run, needs, transfers, stage):
                return steps.add(functools.partial(run, k), needs, cost, transfers, (0, k, -stage))

            own = step(self.own, far[k - WINDOW : k - WINDOW + 1] if k >= WINDOW else [], [(Z_LINK, n)], 0)
            near = step(self.near, [(own, 0)], [(MID_LINK, 2 * n), (PLANE_LINK, 2 * n)], 1)
            far.append(step(self.far, [(near, 0)], [(Z_LINK, 2 * n), (PLANE_LINK, 2 * n), (CORE_LINKS, 2 * n)], 2))
            first = step(self.first, [(near, 1), (far[k], 0), (far[k], 1)], [(PLANE_LINK, n), (CORE_LINKS, 2 * n)], 3)
            second = step(self.second, [first], [(CORE_LINKS, 2 * n)], 4)
            diagonal = step(self.diagonal, [second, (first, 0)], [(Z_LINK, 2 * n), (CORE_LINKS, n)], 5)
            rest = step(self.rest, [(diagonal, 0)], [(CORE_LINKS, n)], 6)
            done.append(step(self.whole, [(rest, 0), (diagonal, 1), (second, 0), (first, 1), (far[k], 2)], [], 7))
        return done


GATHER_SIZES = (144, 144, 80, 144, 288, 288, 288)


def cuts_of(sizes):
    cuts, start = [], 0
    for size in sizes:
        cuts.append((start, start + size))
        start += size
    return cuts


def pack(weight_ref, stage, blocks):
    rows = weight_ref.shape[0]
    stage[0:rows] = weight_ref[...].astype(F32)
    each = rows // blocks
    return jnp.concatenate([stage[pl.ds(j, each, stride=blocks)] for j in range(blocks)], axis=0)


def assemble(raw, part, target, column):
    first, rows, blocks = part
    total = -(-rows * blocks // 16) * 16

    def one(chip, _):
        pair = [raw[core, chip, first : first + total].astype(F32) for core in (0, 1)]
        for j in range(blocks):
            block = jnp.concatenate([member[j * rows : (j + 1) * rows] for member in pair], axis=0)
            target[pl.ds(pl.multiple_of(chip * (2 * rows), 16), 2 * rows), column + j * 128 : column + (j + 1) * 128] = (
                block.astype(BF16)
            )
        return 0

    lax.fori_loop(0, 16, one, 0)


def spread(lane, width, total, by_row):
    col = lax.broadcasted_iota(jnp.int32, (128, total), 1).astype(F32)
    row = lax.broadcasted_iota(jnp.int32, (128, total), 0).astype(F32)
    within = col - width * jnp.floor((col + 0.5) * (1.0 / width))
    return jnp.where(row == within + lane, 1.0, 0.0).astype(BF16)


def own_columns(width, total):
    col = lax.broadcasted_iota(jnp.int32, (32, total), 1)
    low = lax.broadcasted_iota(jnp.int32, (32, total), 0) * width
    return jnp.logical_and(col >= low, col < low + width)


def vector_of(rows, lane, width):
    total = 32 * width
    placed = product(rows, spread(lane, width, total, True))
    return jnp.sum(jnp.where(own_columns(width, total), placed, 0.0), axis=0, keepdims=True)


def col(c):
    return slice(c * 128, (c + 1) * 128)


def scan_forward(length, lam, src, out, cos, sin, carry):
    steps = length // SEGMENTS
    zero = jnp.zeros((SEGMENTS, 128), F32)

    def rows(j):
        return pl.ds(j, SEGMENTS, stride=steps)

    def first(j, kept):
        prod, re, im = kept
        new_p, new_re, new_im = [], [], []
        for c in range(CB):
            gate = lam[c, rows(j)]
            a, b = gate * cos[:, col(c)], gate * sin[:, col(c)]
            new_p.append(prod[c] * gate)
            new_re.append(a * re[c] - b * im[c] + src[c, rows(j)])
            new_im.append(a * im[c] + b * re[c] + src[CB + c, rows(j)])
        return tuple(new_p), tuple(new_re), tuple(new_im)

    ones = (jnp.ones((SEGMENTS, 128), F32),) * CB
    prod, re, im = lax.fori_loop(0, steps, first, (ones, (zero,) * CB, (zero,) * CB))
    turn_re, turn_im = turned(cos, sin, steps)
    for c in range(CB):
        p_re, p_im = prod[c] * turn_re[:, col(c)], prod[c] * turn_im[:, col(c)]
        at_re = at_im = jnp.zeros((1, 128), F32)
        for k in range(SEGMENTS):
            carry[c, k : k + 1] = at_re
            carry[CB + c, k : k + 1] = at_im
            row = slice(k, k + 1)
            at_re, at_im = (
                p_re[row] * at_re - p_im[row] * at_im + re[c][row],
                p_re[row] * at_im + p_im[row] * at_re + im[c][row],
            )

    def second(j, kept):
        re, im = kept
        new_re, new_im = [], []
        for c in range(CB):
            gate = lam[c, rows(j)]
            a, b = gate * cos[:, col(c)], gate * sin[:, col(c)]
            new_re.append(a * re[c] - b * im[c] + src[c, rows(j)])
            new_im.append(a * im[c] + b * re[c] + src[CB + c, rows(j)])
            out[c, rows(j)] = new_re[c]
            out[CB + c, rows(j)] = new_im[c]
        return tuple(new_re), tuple(new_im)

    start = tuple(carry[c] for c in range(CB)), tuple(carry[CB + c] for c in range(CB))
    lax.fori_loop(0, steps, second, start)


def turned(cos, sin, power):
    re, im = jnp.ones_like(cos), jnp.zeros_like(sin)
    base_re, base_im = cos, sin
    while power:
        if power % 2:
            re, im = re * base_re - im * base_im, re * base_im + im * base_re
        power //= 2
        if power:
            base_re, base_im = base_re * base_re - base_im * base_im, 2.0 * base_re * base_im
    return re, im


def group_sum(values, ones, exact):
    high = values.astype(BF16)
    total = product(high, ones)
    if exact:
        total += product((values - high.astype(F32)).astype(BF16), ones)
    return total


def split(values):
    high = values.astype(BF16)
    return jnp.concatenate([high, (values - high.astype(F32)).astype(BF16)], axis=1)


def group_spread(values, wide):
    return product(split(values), wide)


def group_matrices():
    feature = lax.broadcasted_iota(jnp.int32, (D, 128), 0)
    group = lax.broadcasted_iota(jnp.int32, (D, 128), 1) * (D // GROUPS)
    ones = jnp.where(jnp.logical_and(feature >= group, feature < group + D // GROUPS), 1.0, 0.0)
    feature = lax.broadcasted_iota(jnp.int32, (256, D), 1)
    row = lax.broadcasted_iota(jnp.int32, (256, D), 0)
    group = jnp.where(row >= 128, row - 128, row) * (D // GROUPS)
    wide = jnp.where(jnp.logical_and(feature >= group, feature < group + D // GROUPS), 1.0, 0.0)
    return ones.astype(BF16), wide.astype(BF16)


SHARE = 1.0 / (D // GROUPS)


def opening_kernel(
    length, cuts,
    hidden_in, drive, forget, outgate, mixout, gate, up, down, part0, part1, part2, part3, part4,
    n1_out, pd_out, pg_out, lam_out, s_out, mixed_out, normed_out, rstd_out, middle_out, n2_out, wdfg_out, wo_out, wau_out, wb_out, vec_out,
    raw, stage, wdfg, wo, wau, wb, vec_rows, vec, n1, pd_low, pg_low, lam, src, states, carry, mixed, normed, rstd, n2,
    ones_ref, wide_ref, hidden, out_sems, in_sem, send_sems, recv_sems,
):
    at = Places()
    coming = pltpu.make_async_copy(hidden_in, hidden, in_sem)
    coming.start()
    gather = Gather(at, raw, cuts, send_sems, recv_sems)
    own = raw.at[at.core, at.chip]
    vec_rows[0:8] = jnp.zeros((8, 128), F32)
    for ref, (lane, width) in zip((part0, part1, part2, part3, part4), VECTOR_PARTS):
        vec_rows[0:1, lane : lane + width] = ref[...].astype(F32)
    for ref, part in ((drive, DRIVE), (outgate, OUTGATE), (mixout, MIXOUT), (gate, GATE), (up, UP), (down, DOWN)):
        own[part[0] : part[0] + ref.shape[0]] = pack(ref, stage, part[2]).astype(BF16)
    own[FORGET[0] : FORGET[0] + 80] = jnp.concatenate([pack(forget, stage, 3), vec_rows[0:8]], axis=0).astype(BF16)
    at.barrier()

    copies = []

    def give(index, source, target):
        copy = pltpu.make_async_copy(source, target, out_sems.at[index])
        copy.start()
        copies.append(copy)

    def prepare():
        ones_ref[...], wide_ref[...] = group_matrices()

    def vectors():
        for chip in range(16):
            for core in range(2):
                block = raw[core, chip, FORGET[0] + 64 : FORGET[0] + 80].astype(F32)
                vec_rows[2 * chip + core : 2 * chip + core + 1] = block[8:9]
        rows = vec_rows[...].astype(BF16)
        for index, (lane, width) in enumerate(VECTOR_PARTS):
            vec[index : index + 1, 0 : 32 * width] = vector_of(rows, lane, width)
        phase = vec[4:5, 0:C]
        vec[5:6, 0:C] = jnp.cos(phase)
        vec[6:7, 0:C] = jnp.sin(phase)
        vec[7:8] = jnp.zeros((1, D), F32)
        give(0, vec, vec_out)
        give(1, wdfg, wdfg_out)
        coming.wait()

    def project(t):
        rows = slice(t * TILE, (t + 1) * TILE)
        x = hidden[rows].astype(F32)
        unit = (x * lax.rsqrt(jnp.mean(x * x, axis=1, keepdims=True) + norm_eps) * vec[0:1]).astype(BF16)
        n1[rows] = unit
        pre = product(unit, wdfg[...])
        pd, pf, pg = pre[:, :D], pre[:, D : D + C], pre[:, D + C :]
        pd_low[rows] = pd.astype(BF16)
        pg_low[rows] = pg.astype(BF16)
        keep = lower_bound + (1.0 - lower_bound) * sigmoid(pf + vec[3:4, 0:C])
        driven = pd * sigmoid(pd)
        inflow = 1.0 - keep
        for c in range(CB):
            lam[c, rows] = keep[:, col(c)]
            src[c, rows] = inflow[:, col(c)] * driven[:, col(c)]
            src[CB + c, rows] = inflow[:, col(c)] * driven[:, col(CB + c)]

    def projected():
        give(2, n1, n1_out)
        give(3, pd_low, pd_out)
        give(4, pg_low, pg_out)
        give(5, lam, lam_out)

    def scan():
        scan_forward(length, lam, src, states, vec[5:6, 0:C], vec[6:7, 0:C], carry)
        give(6, states, s_out)

    def mix(t):
        rows = slice(t * TILE, (t + 1) * TILE)
        ones, wide = ones_ref[...], wide_ref[...]
        y = jnp.concatenate([states[c, rows] for c in range(NB)], axis=1)
        centered = y - group_spread(group_sum(y, ones, True) * SHARE, wide)
        scale = split(lax.rsqrt(group_sum(centered * centered, ones, False) * SHARE + group_eps))
        rstd[rows] = scale
        unit = centered * product(scale, wide)
        normed[rows] = unit.astype(BF16)
        low = (unit * vec[2:3] * sigmoid(pg_low[rows].astype(F32))).astype(BF16)
        mixed[rows] = low
        middle = hidden[rows].astype(F32) + product(low, wo[...])
        for c in range(NB):
            src[c, rows] = middle[:, col(c)]
        q = lax.rsqrt(jnp.mean(middle * middle, axis=1, keepdims=True) + norm_eps)
        n2[rows] = (middle * q * vec[1:2]).astype(BF16)

    def mixed_rows(low, high, index):
        rows = pl.ds(low * TILE, (high - low) * TILE)
        for source, target in ((mixed, mixed_out), (normed, normed_out), (rstd, rstd_out), (n2, n2_out)):
            give(index, source.at[rows], target.at[rows])
            index += 1
        give(index, src.at[:, rows], middle_out.at[:, rows])

    tiles = length // TILE
    steps = Steps()
    whole = gather.schedule(steps)

    def place(k, part, target, column, cost):
        return steps.add(lambda: assemble(raw, part, target, column), whole[k : k + 1], cost)

    ready = steps.add(prepare, [], 0.3)
    first = [place(0, DRIVE, wdfg, 0, 0.4), place(1, OUTGATE, wdfg, D + C, 0.4), place(2, FORGET, wdfg, D, 0.3)]
    last = steps.add(vectors, first, 1.0)
    for t in range(tiles):
        last = steps.add(functools.partial(project, t), [last], 0.9)
    steps.add(projected, [last], 0.2)
    last = steps.add(scan, [last], 3.4)
    wo_ready = place(3, MIXOUT, wo, 0, 0.4)
    for t in range(tiles):
        last = steps.add(functools.partial(mix, t), [last, wo_ready, ready], 1.1)
        if t == tiles // 2:
            steps.add(functools.partial(mixed_rows, 0, t + 1, 7), [last], 0.3)
    steps.add(functools.partial(mixed_rows, tiles // 2 + 1, tiles, 12), [last], 0.3)
    wa_ready, wu_ready, wb_ready = place(4, GATE, wau, 0, 0.8), place(5, UP, wau, FF, 0.8), place(6, DOWN, wb, 0, 0.8)
    for index, source, target, needs in ((17, wo, wo_out, [wo_ready]), (18, wau, wau_out, [wa_ready, wu_ready]), (19, wb, wb_out, [wb_ready])):
        steps.add(functools.partial(give, index, source, target), needs, 0.1)
    steps.run(256, *GATHER_RATES)
    gather.sends.finish()
    for copy in copies:
        copy.wait()


def opening(hidden, weights, parts):
    length = hidden.shape[0]
    cuts = cuts_of(GATHER_SIZES)
    vmem = pl.BlockSpec(memory_space=pltpu.VMEM)
    hbm = pl.BlockSpec(memory_space=pl.ANY)
    low, wide = ((length, D), BF16), ((NB, length, 128), F32)
    shapes = [
        low, low, low, ((CB, length, 128), F32), wide, low, low, ((length, 256), BF16), wide, low,
        ((D, WDFG), BF16), ((D, D), BF16), ((D, 2 * FF), BF16), ((FF, D), BF16), ((8, D), F32),
    ]
    scratch = [
        ((2, 16, ROWS, 128), BF16), ((288, 128), F32), ((D, WDFG), BF16), ((D, D), BF16), ((D, 2 * FF), BF16), ((FF, D), BF16),
        ((32, 128), F32), ((8, D), F32), low, low, low, ((CB, length, 128), F32), wide, wide, ((NB, SEGMENTS, 128), F32),
        low, low, ((length, 256), BF16), low, ((D, 128), BF16), ((256, D), BF16), low,
    ]
    dma = pltpu.SemaphoreType.DMA
    count = len(cuts), len(GATHER_NAMES)
    return pl.pallas_call(
        functools.partial(opening_kernel, length, cuts),
        out_shape=[jax.ShapeDtypeStruct(*s) for s in shapes],
        in_specs=[hbm] + [vmem] * 12,
        out_specs=[hbm] * len(shapes),
        scratch_shapes=[pltpu.VMEM(*s) for s in scratch] + [dma((20,)), dma, dma(count), dma(count)],
        compiler_params=pltpu.CompilerParams(collective_id=0, has_side_effects=True, vmem_limit_bytes=63 * MIB),
    )(hidden, *weights, *(part[None] for part in parts))


MID = 224


def feed_kernel(g_ref, n2_ref, middle_ref, wau, wb, vec, out_ref, units_ref, dpau_ref, dm_ref, dmiddle_ref, sums_ref):
    @pl.when(pl.program_id(0) == 0)
    def _():
        sums_ref[...] = jnp.zeros_like(sums_ref)

    second_gain = vec[1:2]
    g = g_ref[...]
    middle = jnp.concatenate([middle_ref[c] for c in range(NB)], axis=1)
    pre = product(n2_ref[...], wau[...])
    pa, pu = pre[:, :FF], pre[:, FF:]
    sa = sigmoid(pa)
    silu = pa * sa
    units = (silu * pu).astype(BF16)
    units_ref[...] = units
    out_ref[...] = (middle + product(units, wb[...])).astype(BF16)
    dunits = back_product(g, wb[...])
    dpa = (dunits * pu * (sa * (1.0 + pa * (1.0 - sa)))).astype(BF16)
    dpu = (dunits * silu).astype(BF16)
    dpau = jnp.concatenate([dpa, dpu], axis=1)
    dpau_ref[...] = dpau
    dn2 = back_product(dpau, wau[...])
    q = lax.rsqrt(jnp.mean(middle * middle, axis=1, keepdims=True) + norm_eps)
    scaled = middle * q
    along = dn2 * scaled
    mean = jnp.mean(along * second_gain, axis=1, keepdims=True)
    dmiddle = g.astype(F32) + q * (second_gain * dn2 - scaled * mean)
    dmiddle_ref[...] = dmiddle
    dm_ref[...] = dmiddle.astype(BF16)
    sums_ref[0:1] += jnp.sum(along, axis=0, keepdims=True)


def feed(cotangent, n2, middle, wau, wb, vec):
    length = n2.shape[0]
    rows = lambda width: pl.BlockSpec((MID, width), lambda t: (t, 0))
    cols = pl.BlockSpec((NB, MID, 128), lambda t: (0, t, 0))
    whole = lambda a: pl.BlockSpec(a.shape, lambda t: (0, 0), pipeline_mode=pl.Buffered(1))
    outs = [(D, BF16), (FF, BF16), (2 * FF, BF16), (D, BF16), (D, F32)]
    return pl.pallas_call(
        feed_kernel,
        grid=(length // MID,),
        out_shape=[jax.ShapeDtypeStruct((length, w), t) for w, t in outs] + [jax.ShapeDtypeStruct((8, D), F32)],
        in_specs=[rows(D), rows(D), cols, whole(wau), whole(wb), whole(vec)],
        out_specs=[rows(w) for w, _ in outs] + [pl.BlockSpec((8, D), lambda t: (0, 0))],
        compiler_params=pltpu.CompilerParams(vmem_limit_bytes=63 * MIB),
    )(cotangent, n2, middle, wau, wb, vec)


CHUNKS = ((1088, 144), (1232, 144), (512, 144), (656, 144), (800, 144), (944, 144), (368, 144), (0, 144), (144, 144), (288, 80))
PARTS = tuple(part + (part[2] // split, i * (part[2] // split)) for part, split in ((DOWN, 2), (GATE, 2), (UP, 2)) for i in range(2)) + tuple(
    part + (part[2], 0) for part in (MIXOUT, DRIVE, OUTGATE, FORGET)
)
SCATTER_NAMES = ("c", "p", "s", "t", "f", "z3", "z2", "z1", "d1", "d2", "d3")
DIRECT = 7


class Scatter:
    SLOTS = {"p": 0, "t": 2, "s": 4, "f": 8, "z3": 12, "z2": 14, "z1": 16, "d1": 12, "d2": 13, "d3": 14}

    def __init__(self, places, stage, wide, narrow, deliver, send_sems, recv_sems):
        self.at, self.stage, self.wide, self.narrow, self.deliver = places, stage, wide, narrow, deliver
        self.sends = Sends(SCATTER_NAMES, send_sems, recv_sems)

    def rows(self, k):
        return slice(CHUNKS[k][0], CHUNKS[k][0] + CHUNKS[k][1])

    def add(self, k, first, count, received, slot):
        rows, core = self.rows(k), self.at.core

        def one(i, _):
            self.stage[core, first + i, rows] += received[slot + i, rows]
            return 0

        lax.fori_loop(0, count, one, 0, unroll=2)

    def slot(self, name, k):
        return 0 if name == "t" and k >= DIRECT else self.SLOTS[name]

    def send(self, name, k, first, count, partner, when=None):
        rows = self.rows(k)
        slot = self.slot(name, k)
        self.sends.start(
            name, k, self.stage.at[self.at.core, pl.ds(first, count), rows], self.narrow.at[slot : slot + count, rows], partner, when
        )

    def merge(self, name, k, first, count):
        self.sends.arrived(name, k)
        self.add(k, first, count, self.narrow, self.slot(name, k))

    def cores(self, k):
        rows = self.rows(k)
        self.sends.start("c", k, self.stage.at[1 - self.at.core, :, rows], self.wide.at[:, rows], self.at.sibling)

    def pair(self, k):
        at = self.at
        self.sends.arrived("c", k)
        if k < DIRECT:
            away = at.dcol + 2 - at.half
            self.add(k, away, 2, self.wide, away)
            self.send("p", k, away, 2, at.mate)
        else:
            self.add(k, at.dcol, 4, self.wide, at.dcol)
            self.send("t", k, at.dcol, 4, at.second)
        self.add(k, at.scol, 4, self.wide, at.scol)
        self.send("s", k, at.scol, 4, at.second)
        if k < DIRECT:
            self.add(k, at.dcol + at.half, 2, self.wide, at.dcol + at.half)
        self.add(k, at.fcol, 4, self.wide, at.fcol)
        self.add(k, at.col, 4, self.wide, at.col)

    def diagonal(self, k):
        at = self.at
        self.merge("p", k, at.dcol + at.half, 2)
        self.send("t", k, at.dcol + at.half, 2, at.second)

    def second(self, k):
        at = self.at
        if k < DIRECT:
            self.merge("t", k, at.fcol + at.half, 2)
        else:
            self.merge("t", k, at.fcol, 4)
        self.send("f", k, at.fcol, 4, at.first)
        self.merge("s", k, at.col, 4)

    def first(self, k):
        at = self.at
        self.merge("f", k, at.col, 4)
        if k < DIRECT:
            self.send("z3", k, at.far, 2, at.mate, at.outer)
        else:
            for d, name in enumerate(("d1", "d2", "d3")):
                self.send(name, k, at.col + (at.z + d + 1) % 4, 1, at.along[d])

    def relay(self, k):
        at = self.at

        @pl.when(at.inner)
        def _():
            self.merge("z3", k, at.far, 2)

        self.send("z2", k, at.far, 2, at.other, at.inner)

    def near(self, k):
        at = self.at

        @pl.when(at.inner)
        def _():
            self.merge("z2", k, at.near, 2)

        self.send("z1", k, at.col + (at.z ^ 1), 1, at.mate)

    def last(self, k):
        rows, at = self.rows(k), self.at
        total = self.stage[at.core, at.chip, rows].astype(F32)
        for name in ("z1",) if k < DIRECT else ("d1", "d2", "d3"):
            self.sends.arrived(name, k)
            total += self.narrow[self.SLOTS[name], rows].astype(F32)
        self.deliver(k, total)

    def schedule(self, steps, k, made):
        n = 2 * CHUNKS[k][1]

        def step(run, needs, cost, transfers, stage):
            return steps.add(functools.partial(run, k), needs, cost, transfers, (0, k, -stage))

        cores = step(self.cores, [made], 0.2, [(CORE_LINKS, 8 * n)], 0)
        if k < DIRECT:
            pair = step(self.pair, [(cores, 0)], 0.8, [(Z_LINK, 2 * n), (PLANE_LINK, 4 * n)], 1)
            diagonal = step(self.diagonal, [(pair, 0)], 0.3, [(PLANE_LINK, 2 * n)], 2)
            second = step(self.second, [(diagonal, 0), (pair, 1)], 0.4, [(PLANE_LINK, 4 * n)], 3)
            first = step(self.first, [(second, 0)], 0.4, [(Z_LINK, 2 * n)], 4)
            relay = step(self.relay, [(first, 0)], 0.3, [(MID_LINK, 2 * n)], 5)
            near = step(self.near, [(relay, 0)], 0.3, [(Z_LINK, n)], 6)
            step(self.last, [(near, 0)], 0.3, [], 7)
        else:
            pair = step(self.pair, [(cores, 0)], 0.8, [(PLANE_LINK, 4 * n), (PLANE_LINK, 4 * n)], 1)
            second = step(self.second, [(pair, 0), (pair, 1)], 0.4, [(PLANE_LINK, 4 * n)], 3)
            first = step(self.first, [(second, 0)], 0.4, [(MID_LINK, 4 * n)], 4)
            step(self.last, [(first, 0)], 0.3, [], 7)


def closing_kernel(
    length,
    units, g, n2, dpau, mixed, dm, n1, pg, normed, rstd, states, lam, pd, hidden, dmiddle, wdfg, wo, vec, sums,
    hidden_grad, packed_out,
    left, right, left2, right2, s_buf, ds_buf, lam_buf, wdfg_buf, wo_buf, x_tile, dm_tile, carry, vec_rows, vec_sums, gain_rows, wide_ref, ones_ref,
    stage, from_core, from_links, load_sems, tile_sems, send_sems, recv_sems,
):
    at = Places()

    def unpack(total, start, rows, blocks, here, first):
        for j in range(here):
            packed_out[pl.ds(start + first + j, rows, stride=blocks)] = total[j * rows : (j + 1) * rows]

    def deliver(k, total):
        unpack(total, *PARTS[k])
        if k == 9:
            packed_out[VECTORS : VECTORS + 8] = total[72:80]

    scatter = Scatter(at, stage, from_core, from_links, deliver, send_sems, recv_sems)
    loads = {}

    def load(key, source, target):
        copy = pltpu.make_async_copy(source, target, load_sems.at[len(loads)])
        copy.start()
        loads[key] = copy

    def need(*keys):
        for key in keys:
            loads[key].wait()

    load("units", units, left)
    load("g", g, right)
    load("n2", n2, left2)
    load("dpau", dpau, right2)
    load("s", states, s_buf.at[:, pl.ds(8, length)])
    load("lam", lam, lam_buf)
    load("wo", wo, wo_buf)
    load("wdfg", wdfg, wdfg_buf)
    at.barrier()

    def weight_chunk(source, source_col, rows, per, other, other_col, blocks, start, tail=None, by=None):
        for m in range(rows // 384):
            value = outer_sum(
                source[:, source_col + 384 * m : source_col + 384 * (m + 1)], other[:, other_col : other_col + 128 * blocks]
            )
            if by is not None:
                own = slice(384 * m, 384 * (m + 1))
                total = value[:, col(0)] * by[own, other_col : other_col + 128].astype(F32)
                for j in range(1, blocks):
                    total += value[:, col(j)] * by[own, other_col + 128 * j : other_col + 128 * (j + 1)].astype(F32)
                if other_col == 0:
                    gain_rows[own] = total
                else:
                    gain_rows[own] += total
            for i in range(384 // per):
                index = m * (384 // per) + i
                core, chip = index % 2, index // 2
                parts = [value[i * per : (i + 1) * per, col(j)] for j in range(blocks)]
                if tail is not None:
                    parts += [tail[index : index + 1], jnp.zeros((7, 128), F32)]
                block = jnp.concatenate(parts, axis=0)
                stage[core, chip, start : start + block.shape[0]] = block.astype(BF16)

    def down(i):
        if i == 0:
            need("units", "g")
        weight_chunk(left, 0, FF, 48, right, 384 * i, 3, DOWN[0] + 144 * i)
        if i == 1:
            load("mixed", mixed, left.at[:, 0:D])
            load("n1", n1, left.at[:, D : 2 * D])
            load("dm", dm, right)

    def gate_up(i):
        if i == 0:
            need("n2", "dpau")
        weight_chunk(left2, 0, D, 24, right2, D * i, 6, GATE[0] + 144 * i)
        if i == 3:
            load("pg", pg, right2.at[:, D + C : WDFG])
            load("normed", normed, right2.at[:, WDFG : WDFG + D])
            load("rstd", rstd, right2.at[:, WDFG + D : WDFG + D + 256])
            load("pd", pd, left2)
            ones_ref[...], wide_ref[...] = group_matrices()
            vec_sums[...] = jnp.zeros_like(vec_sums)

    def mixout():
        need("mixed", "dm")
        weight_chunk(left, 0, D, 24, right, 0, 6, MIXOUT[0])

    def unmix(t):
        if t == 0:
            need("pg", "normed", "rstd", "wo")
        rows = slice(t * TILE, (t + 1) * TILE)
        ones, wide = ones_ref[...], wide_ref[...]
        group_gain = vec[2:3]
        unit = right2[rows, WDFG : WDFG + D].astype(F32)
        scale = product(right2[rows, WDFG + D : WDFG + D + 256], wide)
        sg = sigmoid(right2[rows, D + C : WDFG].astype(F32))
        dmixed = back_product(right[rows], wo_buf[...])
        both = dmixed * sg
        dunit = both * group_gain
        both = both * unit
        right2[rows, D + C : WDFG] = (both * group_gain * (1.0 - sg)).astype(BF16)
        mean_one = group_spread(group_sum(dunit, ones, False) * SHARE, wide)
        mean_two = group_spread(group_sum(dunit * unit, ones, False) * SHARE, wide)
        ds = scale * (dunit - mean_one - unit * mean_two)
        for c in range(NB):
            ds_buf[c, rows] = ds[:, col(c)]
        vec_sums[3:4] += jnp.sum(both, axis=0, keepdims=True)

    def reverse():
        need("s", "lam")
        scan_backward(length, lam_buf, s_buf, ds_buf, vec[5:6, 0:C], vec[6:7, 0:C], carry, vec_sums)

    def gates(t):
        if t == 0:
            need("pd")
        rows = slice(t * TILE, (t + 1) * TILE)
        pre = left2[rows].astype(F32)
        sig = sigmoid(pre)
        driven = pre * sig
        slope = sig * (1.0 + pre * (1.0 - sig))
        for c in range(CB):
            gate = lam_buf[c, rows]
            inflow = 1.0 - gate
            dgate = s_buf[c, t * TILE + 8 : (t + 1) * TILE + 8]
            for half in (c, CB + c):
                grad = ds_buf[half, rows]
                dgate -= grad * driven[:, col(half)]
                right2[rows, col(half)] = (inflow * grad * slope[:, col(half)]).astype(BF16)
            dpf = dgate * ((gate - lower_bound) * inflow * (1.0 / (1.0 - lower_bound)))
            vec_sums[0:1, col(c)] += jnp.sum(dpf, axis=0, keepdims=True)
            right2[rows, col(NB + c)] = dpf.astype(BF16)

    def drive():
        need("n1", "wdfg")
        weight_chunk(left, D, D, 24, right2, 0, 6, DRIVE[0], None, wdfg_buf)

    def outgate():
        weight_chunk(left, D, D, 24, right2, D + C, 6, OUTGATE[0], None, wdfg_buf)

    def forget():
        value = outer_sum(left[:, D : 2 * D], right2[:, D : D + C])
        for c in range(CB):
            gain_rows[...] += value[:, col(c)] * wdfg_buf[:, col(NB + c)].astype(F32)
        high = gain_rows[...].astype(BF16)
        low = (gain_rows[...] - high.astype(F32)).astype(BF16)
        ones = jnp.ones((8, 128), BF16)
        vec_sums[2:3] = (back_product(ones, high) + back_product(ones, low))[0:1] / vec[0:1]
        rows = jnp.zeros((32, 128), F32)
        sources = (vec_sums[2:3], sums[0:1], vec_sums[3:4], vec_sums[0:1, 0:C], vec_sums[1:2, 0:C])
        for (lane, width), source in zip(VECTOR_PARTS, sources):
            total = 32 * width
            mine = jnp.where(own_columns(width, total), jnp.broadcast_to(source, (32, total)), 0.0).astype(BF16)
            rows += back_product(mine, spread(lane, width, total, True))
        vec_rows[...] = rows
        for index in range(32):
            parts = [value[index * 24 : (index + 1) * 24, col(j)] for j in range(3)]
            parts += [vec_rows[index : index + 1], jnp.zeros((7, 128), F32)]
            stage[index % 2, index // 2, FORGET[0] : FORGET[0] + 80] = jnp.concatenate(parts, axis=0).astype(BF16)

    count = length // TILE
    fetched, outgoing = {}, {}

    def fetch(t):
        rows = slice(t * TILE, (t + 1) * TILE)
        a = pltpu.make_async_copy(hidden.at[rows], x_tile.at[t % 2], tile_sems.at[0, t % 2])
        b = pltpu.make_async_copy(dmiddle.at[rows], dm_tile.at[t % 3], tile_sems.at[1, t % 3])
        a.start()
        b.start()
        fetched[t] = (a, b)

    def inputs(t):
        if t == 0:
            fetch(0)
        if t >= 2:
            outgoing[t - 2].wait()
        if t + 1 < count:
            fetch(t + 1)
        for copy in fetched[t]:
            copy.wait()
        rows = slice(t * TILE, (t + 1) * TILE)
        first_gain = vec[0:1]
        x = x_tile[t % 2].astype(F32)
        dn1 = back_product(right2[rows, 0:WDFG], wdfg_buf[...])
        p = lax.rsqrt(jnp.mean(x * x, axis=1, keepdims=True) + norm_eps)
        scaled = x * p
        mean = jnp.mean(dn1 * scaled * first_gain, axis=1, keepdims=True)
        dm_tile[t % 3] += p * (first_gain * dn1 - scaled * mean)
        copy = pltpu.make_async_copy(dm_tile.at[t % 3], hidden_grad.at[rows], tile_sems.at[2, t % 3])
        copy.start()
        outgoing[t] = copy

    steps = Steps()
    last = None

    def job(run, cost, k=None):
        nonlocal last
        last = steps.add(run, [] if last is None else [last], cost)
        if k is not None:
            scatter.schedule(steps, k, last)

    def tiled(run, cost):
        for t in range(count):
            job(functools.partial(run, t), cost)

    for i in range(2):
        job(functools.partial(down, i), 2.5, i)
    for i in range(4):
        job(functools.partial(gate_up, i), 2.5, 2 + i)
    job(mixout, 2.5, 6)
    tiled(unmix, 1.1)
    job(reverse, 4.5)
    tiled(gates, 0.4)
    job(drive, 2.5, 7)
    job(outgate, 2.5, 8)
    job(forget, 2.5, 9)
    tiled(inputs, 1.1)
    steps.run(256, *SCATTER_RATES)
    for t in (count - 2, count - 1):
        outgoing[t].wait()
    scatter.sends.finish()


def scan_backward(length, lam, states, ds, cos, sin, carry, vec_sums):
    steps = length // SEGMENTS
    zero = jnp.zeros((SEGMENTS, 128), F32)

    def rows(j):
        return pl.ds(j, SEGMENTS, stride=steps)

    def first(i, kept):
        j = steps - 1 - i
        prod, re, im = kept
        new_p, new_re, new_im = [], [], []
        for c in range(CB):
            gate = lam[c, rows(j)]
            g_re, g_im = ds[c, rows(j)] + re[c], ds[CB + c, rows(j)] + im[c]
            new_p.append(prod[c] * gate)
            new_re.append(gate * (cos[:, col(c)] * g_re + sin[:, col(c)] * g_im))
            new_im.append(gate * (cos[:, col(c)] * g_im - sin[:, col(c)] * g_re))
        return tuple(new_p), tuple(new_re), tuple(new_im)

    ones = (jnp.ones((SEGMENTS, 128), F32),) * CB
    prod, re, im = lax.fori_loop(0, steps, first, (ones, (zero,) * CB, (zero,) * CB))
    turn_re, turn_im = turned(cos, -sin, steps)
    for c in range(CB):
        p_re, p_im = prod[c] * turn_re[:, col(c)], prod[c] * turn_im[:, col(c)]
        at_re = at_im = jnp.zeros((1, 128), F32)
        for k in reversed(range(SEGMENTS)):
            carry[c, k : k + 1] = at_re
            carry[CB + c, k : k + 1] = at_im
            row = slice(k, k + 1)
            at_re, at_im = (
                p_re[row] * at_re - p_im[row] * at_im + re[c][row],
                p_re[row] * at_im + p_im[row] * at_re + im[c][row],
            )
    for c in range(NB):
        states[c, 0:8] = jnp.zeros((8, 128), F32)

    def step(at_rows, before, kept):
        re, im, phase = kept
        new_re, new_im, new_phase = [], [], []
        for c in range(CB):
            gate = lam[c, at_rows]
            g_re, g_im = ds[c, at_rows] + re[c], ds[CB + c, at_rows] + im[c]
            w_re = cos[:, col(c)] * g_re + sin[:, col(c)] * g_im
            w_im = cos[:, col(c)] * g_im - sin[:, col(c)] * g_re
            new_re.append(gate * w_re)
            new_im.append(gate * w_im)
            s_re, s_im = before(c), before(CB + c)
            new_phase.append(phase[c] + gate * (w_im * s_re - w_re * s_im))
            ds[c, at_rows] = g_re
            ds[CB + c, at_rows] = g_im
            yield c, w_re * s_re + w_im * s_im
        kept[:] = [tuple(new_re), tuple(new_im), tuple(new_phase)]

    opening_rows = [states[c, pl.ds(7, SEGMENTS, stride=steps)] for c in range(NB)]

    def second(i, kept):
        j = steps - 1 - i
        kept = list(kept)
        for c, dgate in step(rows(j), lambda c: states[c, pl.ds(j + 7, SEGMENTS, stride=steps)], kept):
            states[c, pl.ds(j + 8, SEGMENTS, stride=steps)] = dgate
        return tuple(kept)

    start = (tuple(carry[c] for c in range(CB)), tuple(carry[CB + c] for c in range(CB)), (zero,) * CB)
    kept = list(lax.fori_loop(0, steps - 1, second, start))
    for c, dgate in step(rows(0), lambda c: opening_rows[c], kept):
        states[c, pl.ds(8, SEGMENTS, stride=steps)] = dgate
    for c in range(CB):
        vec_sums[1:2, col(c)] = jnp.sum(kept[2][c], axis=0, keepdims=True)


def closing(length, arrays, hidden, dmiddle, wdfg, wo, vec, sums):
    vmem = pl.BlockSpec(memory_space=pltpu.VMEM)
    hbm = pl.BlockSpec(memory_space=pl.ANY)
    dma = pltpu.SemaphoreType.DMA
    scratch = [
        ((length, FF), BF16), ((length, D), BF16), ((length, D), BF16), ((length, 2 * FF), BF16),
        ((NB, length + 8, 128), F32), ((NB, length, 128), F32), ((CB, length, 128), F32), ((D, WDFG), BF16), ((D, D), BF16),
        ((2, TILE, D), BF16), ((3, TILE, D), F32), ((NB, SEGMENTS, 128), F32), ((32, 128), F32), ((8, D), F32),
        ((D, 128), F32), ((256, D), BF16), ((D, 128), BF16),
        ((2, 16, ROWS, 128), BF16), ((16, ROWS, 128), BF16), ((17, ROWS, 128), BF16),
    ]
    sems = len(CHUNKS), len(SCATTER_NAMES)
    return pl.pallas_call(
        functools.partial(closing_kernel, length),
        out_shape=[jax.ShapeDtypeStruct((length, D), F32), jax.ShapeDtypeStruct((ROWS, 128), F32)],
        in_specs=[hbm] * 17 + [vmem] * 2,
        out_specs=[hbm, vmem],
        scratch_shapes=[pltpu.VMEM(*s) for s in scratch] + [dma((17,)), dma((3, 3)), dma(sems), dma(sems)],
        compiler_params=pltpu.CompilerParams(collective_id=1, has_side_effects=True, vmem_limit_bytes=63 * MIB),
    )(*arrays, hidden, dmiddle, wdfg, wo, vec, sums)


PIECES = 7


def handing_kernel(grad, packed, grad_out, drive_out, forget_out, outgate_out, mixout_out, gate_out, up_out, down_out, *rest):
    *vector_outs, held, sems = rest
    rows = grad.shape[0] // PIECES
    part = lambda ref, i: ref.at[pl.ds(i * rows, rows)]
    copies = [pltpu.make_async_copy(part(grad, i), part(held, i), sems.at[0, i]) for i in range(PIECES)]
    for copy in copies:
        copy.start()
    for ref, place in (
        (drive_out, DRIVE), (forget_out, FORGET), (outgate_out, OUTGATE), (mixout_out, MIXOUT), (gate_out, GATE), (up_out, UP), (down_out, DOWN)
    ):
        ref[...] = packed[place[0] : place[0] + ref.shape[0]]
    row = packed[VECTORS : VECTORS + 1]
    for ref, (lane, width) in zip(vector_outs, VECTOR_PARTS):
        ref[...] = row[0, lane : lane + width]
    away = [pltpu.make_async_copy(part(held, i), part(grad_out, i), sems.at[1, i]) for i in range(PIECES)]
    for copy, out in zip(copies, away):
        copy.wait()
        out.start()
    for out in away:
        out.wait()


def handing(grad, packed, shards):
    vmem = pl.BlockSpec(memory_space=pltpu.VMEM)
    hbm = pl.BlockSpec(memory_space=pl.ANY)
    shapes = [grad.shape] + [w.shape for w in shards] + [(width,) for _, width in VECTOR_PARTS]
    return pl.pallas_call(
        handing_kernel,
        out_shape=[jax.ShapeDtypeStruct(s, F32) for s in shapes],
        in_specs=[hbm, vmem],
        out_specs=[hbm] + [vmem] * 12,
        scratch_shapes=[pltpu.VMEM(grad.shape, F32), pltpu.SemaphoreType.DMA((2, PIECES))],
        compiler_params=pltpu.CompilerParams(vmem_limit_bytes=63 * MIB),
    )(grad, packed)


def fast(hidden, cotangent, *params):
    weights, parts = params[:7], params[7:]
    n1, pd, pg, lam, states, mixed, normed, rstd, middle, n2, wdfg, wo, wau, wb, vec = opening(hidden, weights, parts)
    out, units, dpau, dm, dmiddle, sums = feed(cotangent, n2, middle, wau, wb, vec)
    arrays = (units, cotangent, n2, dpau, mixed, dm, n1, pg, normed, rstd, states, lam, pd)
    grad, packed = closing(hidden.shape[0], arrays, hidden, dmiddle, wdfg, wo, vec, sums)
    return (out, *handing(grad, packed, weights))


SPAN = 56


def rms_scale(values, gain_vec):
    return (
        values * lax.rsqrt(jnp.mean(values * values, axis=1, keepdims=True) + norm_eps) * gain_vec
    )


def combine(earlier, later_term):
    return (
        later_term[0] * earlier[0] - later_term[1] * earlier[1],
        later_term[0] * earlier[1] + later_term[1] * earlier[0],
        later_term[0] * earlier[2] - later_term[1] * earlier[3] + later_term[2],
        later_term[0] * earlier[3] + later_term[1] * earlier[2] + later_term[3],
    )


def block_prefix(block_terms):
    length = block_terms[0].shape[0]
    width = block_terms[0].shape[1]
    current = block_terms
    offset = 1
    while offset < length:
        filler = (
            jnp.ones((offset, width), jnp.float32),
            jnp.zeros((offset, width), jnp.float32),
            jnp.zeros((offset, width), jnp.float32),
            jnp.zeros((offset, width), jnp.float32),
        )
        earlier = tuple(
            (
                jnp.concatenate([front, member[: length - offset]], axis=0)
                for front, member in zip(filler, current)
            )
        )
        current = combine(earlier, current)
        offset = offset * 2
    return current


def mixer_core(drive_pre, forget_pre, outgate_pre, phase_angle, forget_bias, group_gain):
    length = drive_pre.shape[0]
    features = drive_pre.shape[1]
    channels = features // 2
    blocks = length // SPAN
    driven = jax.nn.silu(drive_pre)
    retain = lower_bound + (1.0 - lower_bound) * jax.nn.sigmoid(forget_pre + forget_bias)
    rotate_re = retain * jnp.cos(phase_angle)
    rotate_im = retain * jnp.sin(phase_angle)
    inflow = 1.0 - retain
    source_re = inflow * driven[:, :channels]
    source_im = inflow * driven[:, channels:]
    pieces = tuple(
        (
            member.reshape(blocks, SPAN, channels)
            for member in (rotate_re, rotate_im, source_re, source_im)
        )
    )

    def advance(carried, block_terms):
        summed = block_prefix(block_terms)
        state_re = summed[0] * carried[0] - summed[1] * carried[1] + summed[2]
        state_im = summed[0] * carried[1] + summed[1] * carried[0] + summed[3]
        return ((state_re[-1], state_im[-1]), (state_re, state_im))

    initial = (jnp.zeros((channels,), jnp.float32), jnp.zeros((channels,), jnp.float32))
    _, (states_re, states_im) = lax.scan(jax.checkpoint(advance), initial, pieces)
    joined = jnp.concatenate(
        [states_re.reshape(length, channels), states_im.reshape(length, channels)], axis=1
    )
    grouped = joined.reshape(length, GROUPS, features // GROUPS)
    centered = grouped - jnp.mean(grouped, axis=2, keepdims=True)
    normed = centered * lax.rsqrt(jnp.mean(centered * centered, axis=2, keepdims=True) + group_eps)
    return normed.reshape(length, features) * group_gain * jax.nn.sigmoid(outgate_pre)


def unpack(gathered):
    targets = ((D, D), (D, C), (D, D), (D, D), (D, FF), (D, FF), (FF, D))
    matrices = tuple(
        (gathered[position].reshape(target) for position, target in enumerate(targets))
    )
    vectors = tuple((member.astype(jnp.float32) for member in gathered[7:]))
    return matrices + vectors


def local(
    hidden,
    cotangent,
    drive_weight,
    forget_weight,
    outgate_weight,
    mixout_weight,
    gate_weight,
    up_weight,
    down_weight,
    first_gain,
    second_gain,
    group_gain,
    forget_bias,
    phase_angle,
):
    params = unpack(
        (
            lax.all_gather(drive_weight, AXES, axis=0, tiled=True),
            lax.all_gather(forget_weight, AXES, axis=0, tiled=True),
            lax.all_gather(outgate_weight, AXES, axis=0, tiled=True),
            lax.all_gather(mixout_weight, AXES, axis=0, tiled=True),
            lax.all_gather(gate_weight, AXES, axis=0, tiled=True),
            lax.all_gather(up_weight, AXES, axis=0, tiled=True),
            lax.all_gather(down_weight, AXES, axis=0, tiled=True),
            lax.all_gather(first_gain, AXES, axis=0, tiled=True),
            lax.all_gather(second_gain, AXES, axis=0, tiled=True),
            lax.all_gather(group_gain, AXES, axis=0, tiled=True),
            lax.all_gather(forget_bias, AXES, axis=0, tiled=True),
            lax.all_gather(phase_angle, AXES, axis=0, tiled=True),
        )
    )
    inputs = hidden.astype(jnp.float32)
    normed_float, pull_first = jax.vjp(rms_scale, inputs, params[7])
    normed_one = normed_float.astype(jnp.bfloat16)
    drive_pre = product(normed_one, params[0])
    forget_pre = product(normed_one, params[1])
    outgate_pre = product(normed_one, params[2])
    mixed_float, pull_mixer = jax.vjp(
        mixer_core, drive_pre, forget_pre, outgate_pre, params[11], params[10], params[9]
    )
    mixed = mixed_float.astype(jnp.bfloat16)
    middle = inputs + product(mixed, params[3])
    second_float, pull_second = jax.vjp(rms_scale, middle, params[8])
    normed_two = second_float.astype(jnp.bfloat16)
    gate_pre = product(normed_two, params[4])
    up_pre = product(normed_two, params[5])
    gate_sig = jax.nn.sigmoid(gate_pre)
    silu_gate = gate_pre * gate_sig
    hidden_units = (silu_gate * up_pre).astype(jnp.bfloat16)
    layer_out = (middle + product(hidden_units, params[6])).astype(jnp.bfloat16)
    back_params = unpack(
        (
            lax.all_gather(drive_weight, AXES, axis=0, tiled=True),
            lax.all_gather(forget_weight, AXES, axis=0, tiled=True),
            lax.all_gather(outgate_weight, AXES, axis=0, tiled=True),
            lax.all_gather(mixout_weight, AXES, axis=0, tiled=True),
            lax.all_gather(gate_weight, AXES, axis=0, tiled=True),
            lax.all_gather(up_weight, AXES, axis=0, tiled=True),
            lax.all_gather(down_weight, AXES, axis=0, tiled=True),
            lax.all_gather(first_gain, AXES, axis=0, tiled=True),
            lax.all_gather(second_gain, AXES, axis=0, tiled=True),
            lax.all_gather(group_gain, AXES, axis=0, tiled=True),
            lax.all_gather(forget_bias, AXES, axis=0, tiled=True),
            lax.all_gather(phase_angle, AXES, axis=0, tiled=True),
        )
    )
    units_back = back_product(cotangent, back_params[6])
    down_grad = outer_sum(hidden_units, cotangent)
    slope = gate_sig * (1.0 + gate_pre * (1.0 - gate_sig))
    gate_back = (units_back * up_pre * slope).astype(jnp.bfloat16)
    up_back = (units_back * silu_gate).astype(jnp.bfloat16)
    gate_grad = outer_sum(normed_two, gate_back)
    up_grad = outer_sum(normed_two, up_back)
    second_back = back_product(gate_back, back_params[4]) + back_product(up_back, back_params[5])
    middle_part, secondgain_grad = pull_second(second_back)
    middle_back = cotangent.astype(jnp.float32) + middle_part
    middle_low = middle_back.astype(jnp.bfloat16)
    mixout_grad = outer_sum(mixed, middle_low)
    mixed_back = back_product(middle_low, back_params[3])
    drive_back, forget_back, outgate_back, phase_grad, bias_grad, groupgain_grad = pull_mixer(
        mixed_back
    )
    drive_low = drive_back.astype(jnp.bfloat16)
    forget_low = forget_back.astype(jnp.bfloat16)
    outgate_low = outgate_back.astype(jnp.bfloat16)
    drive_grad = outer_sum(normed_one, drive_low)
    forget_grad = outer_sum(normed_one, forget_low)
    outgate_grad = outer_sum(normed_one, outgate_low)
    first_back = (
        back_product(drive_low, back_params[0])
        + back_product(forget_low, back_params[1])
        + back_product(outgate_low, back_params[2])
    )
    input_part, firstgain_grad = pull_first(first_back)
    hidden_grad = middle_back + input_part
    all_terms = (
        drive_grad.reshape(-1, 128),
        forget_grad.reshape(-1, 128),
        outgate_grad.reshape(-1, 128),
        mixout_grad.reshape(-1, 128),
        gate_grad.reshape(-1, 128),
        up_grad.reshape(-1, 128),
        down_grad.reshape(-1, 128),
        firstgain_grad,
        secondgain_grad,
        groupgain_grad,
        bias_grad,
        phase_grad,
    )
    sums = (
        lax.psum_scatter(all_terms[0], AXES, scatter_dimension=0, tiled=True),
        lax.psum_scatter(all_terms[1], AXES, scatter_dimension=0, tiled=True),
        lax.psum_scatter(all_terms[2], AXES, scatter_dimension=0, tiled=True),
        lax.psum_scatter(all_terms[3], AXES, scatter_dimension=0, tiled=True),
        lax.psum_scatter(all_terms[4], AXES, scatter_dimension=0, tiled=True),
        lax.psum_scatter(all_terms[5], AXES, scatter_dimension=0, tiled=True),
        lax.psum_scatter(all_terms[6], AXES, scatter_dimension=0, tiled=True),
        lax.psum_scatter(all_terms[7], AXES, scatter_dimension=0, tiled=True),
        lax.psum_scatter(all_terms[8], AXES, scatter_dimension=0, tiled=True),
        lax.psum_scatter(all_terms[9], AXES, scatter_dimension=0, tiled=True),
        lax.psum_scatter(all_terms[10], AXES, scatter_dimension=0, tiled=True),
        lax.psum_scatter(all_terms[11], AXES, scatter_dimension=0, tiled=True),
    )
    return (
        layer_out,
        hidden_grad,
        sums[0],
        sums[1],
        sums[2],
        sums[3],
        sums[4],
        sums[5],
        sums[6],
        sums[7],
        sums[8],
        sums[9],
        sums[10],
        sums[11],
    )


def solution(mesh):
    rows, flat = P(AXES, None), P(AXES)
    step = fast if tuple(mesh.shape[a] for a in AXES) == (4, 8) else local
    return jax.shard_map(
        step, mesh=mesh, in_specs=(rows,) * 9 + (flat,) * 5, out_specs=(rows,) * 9 + (flat,) * 5, check_vma=False
    )
```

```python
import functools

import jax
import jax.numpy as jnp
from jax import lax
from jax.experimental import pallas as pl
from jax.experimental.pallas import tpu as pltpu
from jax.sharding import PartitionSpec as P

D = 768
C = 384
FF = 1536
GROUPS = 8
NB = D // 128
CB = C // 128

lower_bound = 0.25
norm_eps = 1e-06
group_eps = 1e-05

F32 = jnp.float32
BF16 = jnp.bfloat16
MESH = pl.DeviceIdType.MESH
MIB = 2**20
AXES = "dp", "fsdp"

DRIVE = (0, 24, 6)
OUTGATE = (144, 24, 6)
FORGET = (288, 24, 3)
VECTORS = 360
MIXOUT = (368, 24, 6)
GATE = (512, 24, 12)
UP = (800, 24, 12)
DOWN = (1088, 48, 6)
ROWS = 1376
VECTOR_PARTS = ((0, 24), (24, 24), (48, 24), (72, 12), (84, 12))
WDFG = 2 * D + C

TILE = 224
SEGMENTS = 16


def sigmoid(t):
    return 0.5 * jnp.tanh(0.5 * t) + 0.5


def product(left, right):
    return jnp.dot(left, right, preferred_element_type=F32)


def back_product(left, right):
    return lax.dot_general(left, right, (((1,), (1,)), ((), ())), preferred_element_type=F32)


def outer_sum(left, right):
    return lax.dot_general(left, right, (((0,), (0,)), ((), ())), preferred_element_type=F32)


def coords():
    dp = lax.axis_index(AXES[0])
    fsdp = lax.axis_index(AXES[1])
    return dp // 2, dp % 2, fsdp // 2, fsdp % 2


def device(y, x, z, core):
    return (y * 2 + x, z * 2 + core)


CORE_LINK = 550e3
CORE_HOP = 1.5
GATHER_RATES = 75e3, 8.0
SCATTER_RATES = 92e3, 2.5
WINDOW = 4


Z_LINK, MID_LINK, PLANE_LINK, CORE_LINKS = range(4)


class Steps:
    def __init__(self):
        self.steps = []

    def add(self, run, needs, cost, transfers=(), rank=None):
        number = len(self.steps)
        self.steps.append((run, needs, cost, transfers, rank or (1, number)))
        return number

    def run(self, width, link_rate, hop):
        ready_at, free, now = {}, {}, 0.0
        pending = list(range(len(self.steps)))
        while pending:
            at = {n: max([ready_at[d] for d in self.steps[n][1]], default=0.0) for n in pending if all(d in ready_at for d in self.steps[n][1])}
            able = [n for n, t in at.items() if t <= now]
            if not able:
                now = min(at.values())
                continue
            chosen = min(able, key=lambda n: self.steps[n][4])
            pending.remove(chosen)
            run, _, cost, transfers, _ = self.steps[chosen]
            run()
            now += cost
            for index, (link, size) in enumerate(transfers):
                rate, wait = (CORE_LINK, CORE_HOP) if link == CORE_LINKS else (link_rate, hop)
                free[link] = max(now, free.get(link, 0.0)) + size * width / rate
                ready_at[chosen, index] = free[link] + wait
            ready_at[chosen] = now


class Places:
    def __init__(self):
        y, x, z, c = coords()
        self.z, self.core = z, c
        fy = jnp.where(c == 0, 1 - y, y)
        fx = jnp.where(c == 0, x, 1 - x)
        sy = jnp.where(c == 0, y, 1 - y)
        sx = jnp.where(c == 0, 1 - x, x)
        self.first = device(fy, fx, z, c)
        self.second = device(sy, sx, z, c)
        self.sibling = device(y, x, z, 1 - c)
        self.mate = device(y, x, z ^ 1, c)
        self.other = device(y, x, 3 - z, c)
        self.inner = jnp.logical_or(z == 1, z == 2)
        self.outer = jnp.logical_not(self.inner)
        self.along = [device(y, x, (z + d) % 4, c) for d in (1, 2, 3)]
        self.col = (y * 2 + x) * 4
        self.fcol = (fy * 2 + fx) * 4
        self.scol = (sy * 2 + sx) * 4
        self.dcol = ((1 - y) * 2 + (1 - x)) * 4
        self.half = (z % 2) * 2
        self.chip = self.col + z
        self.near = self.col + (z // 2) * 2
        self.far = self.col + 2 - (z // 2) * 2

    def barrier(self):
        bar = pltpu.get_barrier_semaphore()
        for partner in [self.first, self.second, self.sibling] + self.along:
            pl.semaphore_signal(bar, inc=1, device_id=partner, device_id_type=MESH)
        pl.semaphore_wait(bar, 6)


class Sends:
    def __init__(self, names, send_sems, recv_sems):
        self.index = {name: i for i, name in enumerate(names)}
        self.send_sems, self.recv_sems, self.copies = send_sems, recv_sems, {}

    def start(self, name, k, source, target, partner, when=None, lands=None):
        copy = pltpu.make_async_remote_copy(
            src_ref=source, dst_ref=target, send_sem=self.send_sems.at[k, self.index[name]],
            recv_sem=self.recv_sems.at[k, self.index[lands or name]], device_id=partner, device_id_type=MESH,
        )
        if when is None:
            copy.start()
        else:
            pl.when(when)(copy.start)
        self.copies[name, k] = copy, when

    def arrived(self, name, k):
        self.copies[name, k][0].wait_recv()

    def finish(self):
        for copy, when in self.copies.values():
            if when is None:
                copy.wait_send()
            else:
                pl.when(when)(copy.wait_send)


GATHER_NAMES = ("z1", "z2", "z3", "f0", "f1", "s0", "s1", "s2", "p", "c0", "c1", "c2", "c3", "c4")


class Gather:
    def __init__(self, places, raw, cuts, send_sems, recv_sems):
        self.at, self.raw, self.cuts = places, raw, cuts
        self.sends = Sends(GATHER_NAMES, send_sems, recv_sems)

    def send(self, name, first, count, k, partner, when=None, lands=None):
        low, high = self.cuts[k]
        ref = self.raw.at[self.at.core, pl.ds(first, count), low:high]
        self.sends.start(name, k, ref, ref, partner, when, lands)

    def own(self, k):
        self.send("z1", self.at.chip, 1, k, self.at.mate)

    def near(self, k):
        at = self.at
        self.sends.arrived("z1", k)
        self.send("z2", at.near, 2, k, at.other, at.inner)
        self.send("f0", at.near, 2, k, at.first)
        self.send("s0", at.near, 2, k, at.second)

    def far(self, k):
        at = self.at
        self.sends.arrived("z2", k)
        self.send("z3", at.far, 2, k, at.mate, at.inner, "z2")
        self.send("f1", at.far, 2, k, at.first)
        self.send("s1", at.far, 2, k, at.second)
        self.send("c0", at.col, 4, k, at.sibling)

    def first(self, k):
        at = self.at
        self.sends.arrived("f0", k)
        self.sends.arrived("f1", k)
        self.send("s2", at.fcol + at.half, 2, k, at.second)
        self.send("c1", at.fcol, 4, k, at.sibling)

    def second(self, k):
        at = self.at
        self.sends.arrived("s0", k)
        self.sends.arrived("s1", k)
        self.send("c2", at.scol, 4, k, at.sibling)

    def diagonal(self, k):
        at = self.at
        self.sends.arrived("s2", k)
        self.send("p", at.dcol + at.half, 2, k, at.mate)
        self.send("c3", at.dcol + at.half, 2, k, at.sibling)

    def rest(self, k):
        at = self.at
        self.sends.arrived("p", k)
        self.send("c4", at.dcol + 2 - at.half, 2, k, at.sibling)

    def whole(self, k):
        for name in ("c0", "c1", "c2", "c3", "c4"):
            self.sends.arrived(name, k)

    def schedule(self, steps, cost=0.3):
        done, far = [], []
        for k, (low, high) in enumerate(self.cuts):
            n = 2 * (high - low)

            def step(run, needs, transfers, stage):
                return steps.add(functools.partial(run, k), needs, cost, transfers, (0, k, -stage))

            own = step(self.own, far[k - WINDOW : k - WINDOW + 1] if k >= WINDOW else [], [(Z_LINK, n)], 0)
            near = step(self.near, [(own, 0)], [(MID_LINK, 2 * n), (PLANE_LINK, 2 * n)], 1)
            far.append(step(self.far, [(near, 0)], [(Z_LINK, 2 * n), (PLANE_LINK, 2 * n), (CORE_LINKS, 2 * n)], 2))
            first = step(self.first, [(near, 1), (far[k], 0), (far[k], 1)], [(PLANE_LINK, n), (CORE_LINKS, 2 * n)], 3)
            second = step(self.second, [first], [(CORE_LINKS, 2 * n)], 4)
            diagonal = step(self.diagonal, [second, (first, 0)], [(Z_LINK, 2 * n), (CORE_LINKS, n)], 5)
            rest = step(self.rest, [(diagonal, 0)], [(CORE_LINKS, n)], 6)
            done.append(step(self.whole, [(rest, 0), (diagonal, 1), (second, 0), (first, 1), (far[k], 2)], [], 7))
        return done


GATHER_SIZES = (144, 144, 80, 144, 288, 288, 288)


def cuts_of(sizes):
    cuts, start = [], 0
    for size in sizes:
        cuts.append((start, start + size))
        start += size
    return cuts


def pack(weight_ref, stage, blocks):
    rows = weight_ref.shape[0]
    stage[0:rows] = weight_ref[...].astype(F32)
    each = rows // blocks
    return jnp.concatenate([stage[pl.ds(j, each, stride=blocks)] for j in range(blocks)], axis=0)


def assemble(raw, part, target, column):
    first, rows, blocks = part
    total = -(-rows * blocks // 16) * 16

    def one(chip, _):
        pair = [raw[core, chip, first : first + total].astype(F32) for core in (0, 1)]
        for j in range(blocks):
            block = jnp.concatenate([member[j * rows : (j + 1) * rows] for member in pair], axis=0)
            target[pl.ds(pl.multiple_of(chip * (2 * rows), 16), 2 * rows), column + j * 128 : column + (j + 1) * 128] = (
                block.astype(BF16)
            )
        return 0

    lax.fori_loop(0, 16, one, 0)


def spread(lane, width, total, by_row):
    col = lax.broadcasted_iota(jnp.int32, (128, total), 1).astype(F32)
    row = lax.broadcasted_iota(jnp.int32, (128, total), 0).astype(F32)
    within = col - width * jnp.floor((col + 0.5) * (1.0 / width))
    return jnp.where(row == within + lane, 1.0, 0.0).astype(BF16)


def own_columns(width, total):
    col = lax.broadcasted_iota(jnp.int32, (32, total), 1)
    low = lax.broadcasted_iota(jnp.int32, (32, total), 0) * width
    return jnp.logical_and(col >= low, col < low + width)


def vector_of(rows, lane, width):
    total = 32 * width
    placed = product(rows, spread(lane, width, total, True))
    return jnp.sum(jnp.where(own_columns(width, total), placed, 0.0), axis=0, keepdims=True)


def col(c):
    return slice(c * 128, (c + 1) * 128)


def scan_forward(length, lam, src, out, cos, sin, carry):
    steps = length // SEGMENTS
    zero = jnp.zeros((SEGMENTS, 128), F32)

    def rows(j):
        return pl.ds(j, SEGMENTS, stride=steps)

    def first(j, kept):
        prod, re, im = kept
        new_p, new_re, new_im = [], [], []
        for c in range(CB):
            gate = lam[c, rows(j)]
            a, b = gate * cos[:, col(c)], gate * sin[:, col(c)]
            new_p.append(prod[c] * gate)
            new_re.append(a * re[c] - b * im[c] + src[c, rows(j)])
            new_im.append(a * im[c] + b * re[c] + src[CB + c, rows(j)])
        return tuple(new_p), tuple(new_re), tuple(new_im)

    ones = (jnp.ones((SEGMENTS, 128), F32),) * CB
    prod, re, im = lax.fori_loop(0, steps, first, (ones, (zero,) * CB, (zero,) * CB))
    turn_re, turn_im = turned(cos, sin, steps)
    for c in range(CB):
        p_re, p_im = prod[c] * turn_re[:, col(c)], prod[c] * turn_im[:, col(c)]
        at_re = at_im = jnp.zeros((1, 128), F32)
        for k in range(SEGMENTS):
            carry[c, k : k + 1] = at_re
            carry[CB + c, k : k + 1] = at_im
            row = slice(k, k + 1)
            at_re, at_im = (
                p_re[row] * at_re - p_im[row] * at_im + re[c][row],
                p_re[row] * at_im + p_im[row] * at_re + im[c][row],
            )

    def second(j, kept):
        re, im = kept
        new_re, new_im = [], []
        for c in range(CB):
            gate = lam[c, rows(j)]
            a, b = gate * cos[:, col(c)], gate * sin[:, col(c)]
            new_re.append(a * re[c] - b * im[c] + src[c, rows(j)])
            new_im.append(a * im[c] + b * re[c] + src[CB + c, rows(j)])
            out[c, rows(j)] = new_re[c]
            out[CB + c, rows(j)] = new_im[c]
        return tuple(new_re), tuple(new_im)

    start = tuple(carry[c] for c in range(CB)), tuple(carry[CB + c] for c in range(CB))
    lax.fori_loop(0, steps, second, start)


def turned(cos, sin, power):
    re, im = jnp.ones_like(cos), jnp.zeros_like(sin)
    base_re, base_im = cos, sin
    while power:
        if power % 2:
            re, im = re * base_re - im * base_im, re * base_im + im * base_re
        power //= 2
        if power:
            base_re, base_im = base_re * base_re - base_im * base_im, 2.0 * base_re * base_im
    return re, im


def group_sum(values, ones, exact):
    high = values.astype(BF16)
    total = product(high, ones)
    if exact:
        total += product((values - high.astype(F32)).astype(BF16), ones)
    return total


def split(values):
    high = values.astype(BF16)
    return jnp.concatenate([high, (values - high.astype(F32)).astype(BF16)], axis=1)


def group_spread(values, wide):
    return product(split(values), wide)


def group_matrices():
    feature = lax.broadcasted_iota(jnp.int32, (D, 128), 0)
    group = lax.broadcasted_iota(jnp.int32, (D, 128), 1) * (D // GROUPS)
    ones = jnp.where(jnp.logical_and(feature >= group, feature < group + D // GROUPS), 1.0, 0.0)
    feature = lax.broadcasted_iota(jnp.int32, (256, D), 1)
    row = lax.broadcasted_iota(jnp.int32, (256, D), 0)
    group = jnp.where(row >= 128, row - 128, row) * (D // GROUPS)
    wide = jnp.where(jnp.logical_and(feature >= group, feature < group + D // GROUPS), 1.0, 0.0)
    return ones.astype(BF16), wide.astype(BF16)


SHARE = 1.0 / (D // GROUPS)


def opening_kernel(
    length, cuts,
    hidden_in, drive, forget, outgate, mixout, gate, up, down, part0, part1, part2, part3, part4,
    n1_out, pd_out, pg_out, lam_out, s_out, mixed_out, normed_out, rstd_out, middle_out, n2_out, wdfg_out, wo_out, wau_out, wb_out, vec_out,
    raw, stage, wdfg, wo, wau, wb, vec_rows, vec, n1, pd_low, pg_low, lam, src, states, carry, mixed, normed, rstd, n2,
    ones_ref, wide_ref, hidden, out_sems, in_sem, send_sems, recv_sems,
):
    at = Places()
    coming = pltpu.make_async_copy(hidden_in, hidden, in_sem)
    coming.start()
    gather = Gather(at, raw, cuts, send_sems, recv_sems)
    own = raw.at[at.core, at.chip]
    vec_rows[0:8] = jnp.zeros((8, 128), F32)
    for ref, (lane, width) in zip((part0, part1, part2, part3, part4), VECTOR_PARTS):
        vec_rows[0:1, lane : lane + width] = ref[...].astype(F32)
    for ref, part in ((drive, DRIVE), (outgate, OUTGATE), (mixout, MIXOUT), (gate, GATE), (up, UP), (down, DOWN)):
        own[part[0] : part[0] + ref.shape[0]] = pack(ref, stage, part[2]).astype(BF16)
    own[FORGET[0] : FORGET[0] + 80] = jnp.concatenate([pack(forget, stage, 3), vec_rows[0:8]], axis=0).astype(BF16)
    at.barrier()

    copies = []

    def give(index, source, target):
        copy = pltpu.make_async_copy(source, target, out_sems.at[index])
        copy.start()
        copies.append(copy)

    def prepare():
        ones_ref[...], wide_ref[...] = group_matrices()

    def vectors():
        for chip in range(16):
            for core in range(2):
                block = raw[core, chip, FORGET[0] + 64 : FORGET[0] + 80].astype(F32)
                vec_rows[2 * chip + core : 2 * chip + core + 1] = block[8:9]
        rows = vec_rows[...].astype(BF16)
        for index, (lane, width) in enumerate(VECTOR_PARTS):
            vec[index : index + 1, 0 : 32 * width] = vector_of(rows, lane, width)
        phase = vec[4:5, 0:C]
        vec[5:6, 0:C] = jnp.cos(phase)
        vec[6:7, 0:C] = jnp.sin(phase)
        vec[7:8] = jnp.zeros((1, D), F32)
        give(0, vec, vec_out)
        give(1, wdfg, wdfg_out)
        coming.wait()

    def project(t):
        rows = slice(t * TILE, (t + 1) * TILE)
        x = hidden[rows].astype(F32)
        unit = (x * lax.rsqrt(jnp.mean(x * x, axis=1, keepdims=True) + norm_eps) * vec[0:1]).astype(BF16)
        n1[rows] = unit
        pre = product(unit, wdfg[...])
        pd, pf, pg = pre[:, :D], pre[:, D : D + C], pre[:, D + C :]
        pd_low[rows] = pd.astype(BF16)
        pg_low[rows] = pg.astype(BF16)
        keep = lower_bound + (1.0 - lower_bound) * sigmoid(pf + vec[3:4, 0:C])
        driven = pd * sigmoid(pd)
        inflow = 1.0 - keep
        for c in range(CB):
            lam[c, rows] = keep[:, col(c)]
            src[c, rows] = inflow[:, col(c)] * driven[:, col(c)]
            src[CB + c, rows] = inflow[:, col(c)] * driven[:, col(CB + c)]

    def projected():
        give(2, n1, n1_out)
        give(3, pd_low, pd_out)
        give(4, pg_low, pg_out)
        give(5, lam, lam_out)

    def scan():
        scan_forward(length, lam, src, states, vec[5:6, 0:C], vec[6:7, 0:C], carry)
        give(6, states, s_out)

    def mix(t):
        rows = slice(t * TILE, (t + 1) * TILE)
        ones, wide = ones_ref[...], wide_ref[...]
        y = jnp.concatenate([states[c, rows] for c in range(NB)], axis=1)
        centered = y - group_spread(group_sum(y, ones, True) * SHARE, wide)
        scale = split(lax.rsqrt(group_sum(centered * centered, ones, False) * SHARE + group_eps))
        rstd[rows] = scale
        unit = centered * product(scale, wide)
        normed[rows] = unit.astype(BF16)
        low = (unit * vec[2:3] * sigmoid(pg_low[rows].astype(F32))).astype(BF16)
        mixed[rows] = low
        middle = hidden[rows].astype(F32) + product(low, wo[...])
        for c in range(NB):
            src[c, rows] = middle[:, col(c)]
        q = lax.rsqrt(jnp.mean(middle * middle, axis=1, keepdims=True) + norm_eps)
        n2[rows] = (middle * q * vec[1:2]).astype(BF16)

    def mixed_rows(low, high, index):
        rows = pl.ds(low * TILE, (high - low) * TILE)
        for source, target in ((mixed, mixed_out), (normed, normed_out), (rstd, rstd_out), (n2, n2_out)):
            give(index, source.at[rows], target.at[rows])
            index += 1
        give(index, src.at[:, rows], middle_out.at[:, rows])

    tiles = length // TILE
    steps = Steps()
    whole = gather.schedule(steps)

    def place(k, part, target, column, cost):
        return steps.add(lambda: assemble(raw, part, target, column), whole[k : k + 1], cost)

    ready = steps.add(prepare, [], 0.3)
    first = [place(0, DRIVE, wdfg, 0, 0.4), place(1, OUTGATE, wdfg, D + C, 0.4), place(2, FORGET, wdfg, D, 0.3)]
    last = steps.add(vectors, first, 1.0)
    for t in range(tiles):
        last = steps.add(functools.partial(project, t), [last], 0.9)
    steps.add(projected, [last], 0.2)
    last = steps.add(scan, [last], 3.4)
    wo_ready = place(3, MIXOUT, wo, 0, 0.4)
    for t in range(tiles):
        last = steps.add(functools.partial(mix, t), [last, wo_ready, ready], 1.1)
        if t == tiles // 2:
            steps.add(functools.partial(mixed_rows, 0, t + 1, 7), [last], 0.3)
    steps.add(functools.partial(mixed_rows, tiles // 2 + 1, tiles, 12), [last], 0.3)
    wa_ready, wu_ready, wb_ready = place(4, GATE, wau, 0, 0.8), place(5, UP, wau, FF, 0.8), place(6, DOWN, wb, 0, 0.8)
    for index, source, target, needs in ((17, wo, wo_out, [wo_ready]), (18, wau, wau_out, [wa_ready, wu_ready]), (19, wb, wb_out, [wb_ready])):
        steps.add(functools.partial(give, index, source, target), needs, 0.1)
    steps.run(256, *GATHER_RATES)
    gather.sends.finish()
    for copy in copies:
        copy.wait()


def opening(hidden, weights, parts):
    length = hidden.shape[0]
    cuts = cuts_of(GATHER_SIZES)
    vmem = pl.BlockSpec(memory_space=pltpu.VMEM)
    hbm = pl.BlockSpec(memory_space=pl.ANY)
    low, wide = ((length, D), BF16), ((NB, length, 128), F32)
    shapes = [
        low, low, low, ((CB, length, 128), F32), wide, low, low, ((length, 256), BF16), wide, low,
        ((D, WDFG), BF16), ((D, D), BF16), ((D, 2 * FF), BF16), ((FF, D), BF16), ((8, D), F32),
    ]
    scratch = [
        ((2, 16, ROWS, 128), BF16), ((288, 128), F32), ((D, WDFG), BF16), ((D, D), BF16), ((D, 2 * FF), BF16), ((FF, D), BF16),
        ((32, 128), F32), ((8, D), F32), low, low, low, ((CB, length, 128), F32), wide, wide, ((NB, SEGMENTS, 128), F32),
        low, low, ((length, 256), BF16), low, ((D, 128), BF16), ((256, D), BF16), low,
    ]
    dma = pltpu.SemaphoreType.DMA
    count = len(cuts), len(GATHER_NAMES)
    return pl.pallas_call(
        functools.partial(opening_kernel, length, cuts),
        out_shape=[jax.ShapeDtypeStruct(*s) for s in shapes],
        in_specs=[hbm] + [vmem] * 12,
        out_specs=[hbm] * len(shapes),
        scratch_shapes=[pltpu.VMEM(*s) for s in scratch] + [dma((20,)), dma, dma(count), dma(count)],
        compiler_params=pltpu.CompilerParams(collective_id=0, has_side_effects=True, vmem_limit_bytes=63 * MIB),
    )(hidden, *weights, *(part[None] for part in parts))


MID = 224


def feed_kernel(g_ref, n2_ref, middle_ref, wau, wb, vec, out_ref, units_ref, dpau_ref, dm_ref, dmiddle_ref, sums_ref):
    @pl.when(pl.program_id(0) == 0)
    def _():
        sums_ref[...] = jnp.zeros_like(sums_ref)

    second_gain = vec[1:2]
    g = g_ref[...]
    middle = jnp.concatenate([middle_ref[c] for c in range(NB)], axis=1)
    pre = product(n2_ref[...], wau[...])
    pa, pu = pre[:, :FF], pre[:, FF:]
    sa = sigmoid(pa)
    silu = pa * sa
    units = (silu * pu).astype(BF16)
    units_ref[...] = units
    out_ref[...] = (middle + product(units, wb[...])).astype(BF16)
    dunits = back_product(g, wb[...])
    dpa = (dunits * pu * (sa * (1.0 + pa * (1.0 - sa)))).astype(BF16)
    dpu = (dunits * silu).astype(BF16)
    dpau = jnp.concatenate([dpa, dpu], axis=1)
    dpau_ref[...] = dpau
    dn2 = back_product(dpau, wau[...])
    q = lax.rsqrt(jnp.mean(middle * middle, axis=1, keepdims=True) + norm_eps)
    scaled = middle * q
    along = dn2 * scaled
    mean = jnp.mean(along * second_gain, axis=1, keepdims=True)
    dmiddle = g.astype(F32) + q * (second_gain * dn2 - scaled * mean)
    dmiddle_ref[...] = dmiddle
    dm_ref[...] = dmiddle.astype(BF16)
    sums_ref[0:1] += jnp.sum(along, axis=0, keepdims=True)


def feed(cotangent, n2, middle, wau, wb, vec):
    length = n2.shape[0]
    rows = lambda width: pl.BlockSpec((MID, width), lambda t: (t, 0))
    cols = pl.BlockSpec((NB, MID, 128), lambda t: (0, t, 0))
    whole = lambda a: pl.BlockSpec(a.shape, lambda t: (0, 0), pipeline_mode=pl.Buffered(1))
    outs = [(D, BF16), (FF, BF16), (2 * FF, BF16), (D, BF16), (D, F32)]
    return pl.pallas_call(
        feed_kernel,
        grid=(length // MID,),
        out_shape=[jax.ShapeDtypeStruct((length, w), t) for w, t in outs] + [jax.ShapeDtypeStruct((8, D), F32)],
        in_specs=[rows(D), rows(D), cols, whole(wau), whole(wb), whole(vec)],
        out_specs=[rows(w) for w, _ in outs] + [pl.BlockSpec((8, D), lambda t: (0, 0))],
        compiler_params=pltpu.CompilerParams(vmem_limit_bytes=63 * MIB),
    )(cotangent, n2, middle, wau, wb, vec)


CHUNKS = ((1088, 144), (1232, 144), (512, 144), (656, 144), (800, 144), (944, 144), (368, 144), (0, 144), (144, 144), (288, 80))
PARTS = tuple(part + (part[2] // split, i * (part[2] // split)) for part, split in ((DOWN, 2), (GATE, 2), (UP, 2)) for i in range(2)) + tuple(
    part + (part[2], 0) for part in (MIXOUT, DRIVE, OUTGATE, FORGET)
)
SCATTER_NAMES = ("c", "p", "s", "t", "f", "z3", "z2", "z1", "d1", "d2", "d3")
DIRECT = 7


class Scatter:
    SLOTS = {"p": 0, "t": 2, "s": 4, "f": 8, "z3": 12, "z2": 14, "z1": 16, "d1": 12, "d2": 13, "d3": 14}

    def __init__(self, places, stage, wide, narrow, deliver, send_sems, recv_sems):
        self.at, self.stage, self.wide, self.narrow, self.deliver = places, stage, wide, narrow, deliver
        self.sends = Sends(SCATTER_NAMES, send_sems, recv_sems)

    def rows(self, k):
        return slice(CHUNKS[k][0], CHUNKS[k][0] + CHUNKS[k][1])

    def add(self, k, first, count, received, slot):
        rows, core = self.rows(k), self.at.core

        def one(i, _):
            self.stage[core, first + i, rows] += received[slot + i, rows]
            return 0

        lax.fori_loop(0, count, one, 0, unroll=2)

    def slot(self, name, k):
        return 0 if name == "t" and k >= DIRECT else self.SLOTS[name]

    def send(self, name, k, first, count, partner, when=None):
        rows = self.rows(k)
        slot = self.slot(name, k)
        self.sends.start(
            name, k, self.stage.at[self.at.core, pl.ds(first, count), rows], self.narrow.at[slot : slot + count, rows], partner, when
        )

    def merge(self, name, k, first, count):
        self.sends.arrived(name, k)
        self.add(k, first, count, self.narrow, self.slot(name, k))

    def cores(self, k):
        rows = self.rows(k)
        self.sends.start("c", k, self.stage.at[1 - self.at.core, :, rows], self.wide.at[:, rows], self.at.sibling)

    def pair(self, k):
        at = self.at
        self.sends.arrived("c", k)
        if k < DIRECT:
            away = at.dcol + 2 - at.half
            self.add(k, away, 2, self.wide, away)
            self.send("p", k, away, 2, at.mate)
        else:
            self.add(k, at.dcol, 4, self.wide, at.dcol)
            self.send("t", k, at.dcol, 4, at.second)
        self.add(k, at.scol, 4, self.wide, at.scol)
        self.send("s", k, at.scol, 4, at.second)
        if k < DIRECT:
            self.add(k, at.dcol + at.half, 2, self.wide, at.dcol + at.half)
        self.add(k, at.fcol, 4, self.wide, at.fcol)
        self.add(k, at.col, 4, self.wide, at.col)

    def diagonal(self, k):
        at = self.at
        self.merge("p", k, at.dcol + at.half, 2)
        self.send("t", k, at.dcol + at.half, 2, at.second)

    def second(self, k):
        at = self.at
        if k < DIRECT:
            self.merge("t", k, at.fcol + at.half, 2)
        else:
            self.merge("t", k, at.fcol, 4)
        self.send("f", k, at.fcol, 4, at.first)
        self.merge("s", k, at.col, 4)

    def first(self, k):
        at = self.at
        self.merge("f", k, at.col, 4)
        if k < DIRECT:
            self.send("z3", k, at.far, 2, at.mate, at.outer)
        else:
            for d, name in enumerate(("d1", "d2", "d3")):
                self.send(name, k, at.col + (at.z + d + 1) % 4, 1, at.along[d])

    def relay(self, k):
        at = self.at

        @pl.when(at.inner)
        def _():
            self.merge("z3", k, at.far, 2)

        self.send("z2", k, at.far, 2, at.other, at.inner)

    def near(self, k):
        at = self.at

        @pl.when(at.inner)
        def _():
            self.merge("z2", k, at.near, 2)

        self.send("z1", k, at.col + (at.z ^ 1), 1, at.mate)

    def last(self, k):
        rows, at = self.rows(k), self.at
        total = self.stage[at.core, at.chip, rows].astype(F32)
        for name in ("z1",) if k < DIRECT else ("d1", "d2", "d3"):
            self.sends.arrived(name, k)
            total += self.narrow[self.SLOTS[name], rows].astype(F32)
        self.deliver(k, total)

    def schedule(self, steps, k, made):
        n = 2 * CHUNKS[k][1]

        def step(run, needs, cost, transfers, stage):
            return steps.add(functools.partial(run, k), needs, cost, transfers, (0, k, -stage))

        cores = step(self.cores, [made], 0.2, [(CORE_LINKS, 8 * n)], 0)
        if k < DIRECT:
            pair = step(self.pair, [(cores, 0)], 0.8, [(Z_LINK, 2 * n), (PLANE_LINK, 4 * n)], 1)
            diagonal = step(self.diagonal, [(pair, 0)], 0.3, [(PLANE_LINK, 2 * n)], 2)
            second = step(self.second, [(diagonal, 0), (pair, 1)], 0.4, [(PLANE_LINK, 4 * n)], 3)
            first = step(self.first, [(second, 0)], 0.4, [(Z_LINK, 2 * n)], 4)
            relay = step(self.relay, [(first, 0)], 0.3, [(MID_LINK, 2 * n)], 5)
            near = step(self.near, [(relay, 0)], 0.3, [(Z_LINK, n)], 6)
            step(self.last, [(near, 0)], 0.3, [], 7)
        else:
            pair = step(self.pair, [(cores, 0)], 0.8, [(PLANE_LINK, 4 * n), (PLANE_LINK, 4 * n)], 1)
            second = step(self.second, [(pair, 0), (pair, 1)], 0.4, [(PLANE_LINK, 4 * n)], 3)
            first = step(self.first, [(second, 0)], 0.4, [(MID_LINK, 4 * n)], 4)
            step(self.last, [(first, 0)], 0.3, [], 7)


def closing_kernel(
    length,
    units, g, n2, dpau, mixed, dm, n1, pg, normed, rstd, states, lam, pd, hidden, dmiddle, wdfg, wo, vec, sums,
    hidden_grad, packed_out,
    left, right, left2, right2, s_buf, ds_buf, lam_buf, wdfg_buf, wo_buf, x_tile, dm_tile, carry, vec_rows, vec_sums, gain_rows, wide_ref, ones_ref,
    stage, from_core, from_links, load_sems, tile_sems, send_sems, recv_sems,
):
    at = Places()

    def unpack(total, start, rows, blocks, here, first):
        for j in range(here):
            packed_out[pl.ds(start + first + j, rows, stride=blocks)] = total[j * rows : (j + 1) * rows]

    def deliver(k, total):
        unpack(total, *PARTS[k])
        if k == 9:
            packed_out[VECTORS : VECTORS + 8] = total[72:80]

    scatter = Scatter(at, stage, from_core, from_links, deliver, send_sems, recv_sems)
    loads = {}

    def load(key, source, target):
        copy = pltpu.make_async_copy(source, target, load_sems.at[len(loads)])
        copy.start()
        loads[key] = copy

    def need(*keys):
        for key in keys:
            loads[key].wait()

    load("units", units, left)
    load("g", g, right)
    at.barrier()

    def weight_chunk(source, source_col, rows, per, other, other_col, blocks, start, tail=None, by=None):
        for m in range(rows // 384):
            value = outer_sum(
                source[:, source_col + 384 * m : source_col + 384 * (m + 1)], other[:, other_col : other_col + 128 * blocks]
            )
            if by is not None:
                own = slice(384 * m, 384 * (m + 1))
                total = value[:, col(0)] * by[own, other_col : other_col + 128].astype(F32)
                for j in range(1, blocks):
                    total += value[:, col(j)] * by[own, other_col + 128 * j : other_col + 128 * (j + 1)].astype(F32)
                if other_col == 0:
                    gain_rows[own] = total
                else:
                    gain_rows[own] += total
            for i in range(384 // per):
                index = m * (384 // per) + i
                core, chip = index % 2, index // 2
                parts = [value[i * per : (i + 1) * per, col(j)] for j in range(blocks)]
                if tail is not None:
                    parts += [tail[index : index + 1], jnp.zeros((7, 128), F32)]
                block = jnp.concatenate(parts, axis=0)
                stage[core, chip, start : start + block.shape[0]] = block.astype(BF16)

    def down(i):
        if i == 0:
            need("units", "g")
            load("n2", n2, left2)
            load("dpau", dpau, right2)
        weight_chunk(left, 0, FF, 48, right, 384 * i, 3, DOWN[0] + 144 * i)
        if i == 1:
            load("mixed", mixed, left.at[:, 0:D])
            load("n1", n1, left.at[:, D : 2 * D])
            load("dm", dm, right)

    def gate_up(i):
        if i == 0:
            need("n2", "dpau")
            load("s", states, s_buf.at[:, pl.ds(8, length)])
            load("lam", lam, lam_buf)
            load("wo", wo, wo_buf)
            load("wdfg", wdfg, wdfg_buf)
        weight_chunk(left2, 0, D, 24, right2, D * i, 6, GATE[0] + 144 * i)
        if i == 3:
            load("pg", pg, right2.at[:, D + C : WDFG])
            load("normed", normed, right2.at[:, WDFG : WDFG + D])
            load("rstd", rstd, right2.at[:, WDFG + D : WDFG + D + 256])
            load("pd", pd, left2)
            ones_ref[...], wide_ref[...] = group_matrices()
            vec_sums[...] = jnp.zeros_like(vec_sums)

    def mixout():
        need("mixed", "dm")
        weight_chunk(left, 0, D, 24, right, 0, 6, MIXOUT[0])

    def unmix(t):
        if t == 0:
            need("pg", "normed", "rstd", "wo")
        rows = slice(t * TILE, (t + 1) * TILE)
        ones, wide = ones_ref[...], wide_ref[...]
        group_gain = vec[2:3]
        unit = right2[rows, WDFG : WDFG + D].astype(F32)
        scale = product(right2[rows, WDFG + D : WDFG + D + 256], wide)
        sg = sigmoid(right2[rows, D + C : WDFG].astype(F32))
        dmixed = back_product(right[rows], wo_buf[...])
        both = dmixed * sg
        dunit = both * group_gain
        both = both * unit
        right2[rows, D + C : WDFG] = (both * group_gain * (1.0 - sg)).astype(BF16)
        mean_one = group_spread(group_sum(dunit, ones, False) * SHARE, wide)
        mean_two = group_spread(group_sum(dunit * unit, ones, False) * SHARE, wide)
        ds = scale * (dunit - mean_one - unit * mean_two)
        for c in range(NB):
            ds_buf[c, rows] = ds[:, col(c)]
        vec_sums[3:4] += jnp.sum(both, axis=0, keepdims=True)

    def reverse():
        need("s", "lam")
        scan_backward(length, lam_buf, s_buf, ds_buf, vec[5:6, 0:C], vec[6:7, 0:C], carry, vec_sums)

    def gates(t):
        if t == 0:
            need("pd")
        rows = slice(t * TILE, (t + 1) * TILE)
        pre = left2[rows].astype(F32)
        sig = sigmoid(pre)
        driven = pre * sig
        slope = sig * (1.0 + pre * (1.0 - sig))
        for c in range(CB):
            gate = lam_buf[c, rows]
            inflow = 1.0 - gate
            dgate = s_buf[c, t * TILE + 8 : (t + 1) * TILE + 8]
            for half in (c, CB + c):
                grad = ds_buf[half, rows]
                dgate -= grad * driven[:, col(half)]
                right2[rows, col(half)] = (inflow * grad * slope[:, col(half)]).astype(BF16)
            dpf = dgate * ((gate - lower_bound) * inflow * (1.0 / (1.0 - lower_bound)))
            vec_sums[0:1, col(c)] += jnp.sum(dpf, axis=0, keepdims=True)
            right2[rows, col(NB + c)] = dpf.astype(BF16)

    def drive():
        need("n1", "wdfg")
        weight_chunk(left, D, D, 24, right2, 0, 6, DRIVE[0], None, wdfg_buf)

    def outgate():
        weight_chunk(left, D, D, 24, right2, D + C, 6, OUTGATE[0], None, wdfg_buf)

    def forget():
        value = outer_sum(left[:, D : 2 * D], right2[:, D : D + C])
        for c in range(CB):
            gain_rows[...] += value[:, col(c)] * wdfg_buf[:, col(NB + c)].astype(F32)
        high = gain_rows[...].astype(BF16)
        low = (gain_rows[...] - high.astype(F32)).astype(BF16)
        ones = jnp.ones((8, 128), BF16)
        vec_sums[2:3] = (back_product(ones, high) + back_product(ones, low))[0:1] / vec[0:1]
        rows = jnp.zeros((32, 128), F32)
        sources = (vec_sums[2:3], sums[0:1], vec_sums[3:4], vec_sums[0:1, 0:C], vec_sums[1:2, 0:C])
        for (lane, width), source in zip(VECTOR_PARTS, sources):
            total = 32 * width
            mine = jnp.where(own_columns(width, total), jnp.broadcast_to(source, (32, total)), 0.0).astype(BF16)
            rows += back_product(mine, spread(lane, width, total, True))
        vec_rows[...] = rows
        for index in range(32):
            parts = [value[index * 24 : (index + 1) * 24, col(j)] for j in range(3)]
            parts += [vec_rows[index : index + 1], jnp.zeros((7, 128), F32)]
            stage[index % 2, index // 2, FORGET[0] : FORGET[0] + 80] = jnp.concatenate(parts, axis=0).astype(BF16)

    count = length // TILE
    fetched, outgoing = {}, {}

    def fetch(t):
        rows = slice(t * TILE, (t + 1) * TILE)
        a = pltpu.make_async_copy(hidden.at[rows], x_tile.at[t % 2], tile_sems.at[0, t % 2])
        b = pltpu.make_async_copy(dmiddle.at[rows], dm_tile.at[t % 3], tile_sems.at[1, t % 3])
        a.start()
        b.start()
        fetched[t] = (a, b)

    def inputs(t):
        if t == 0:
            fetch(0)
        if t >= 2:
            outgoing[t - 2].wait()
        if t + 1 < count:
            fetch(t + 1)
        for copy in fetched[t]:
            copy.wait()
        rows = slice(t * TILE, (t + 1) * TILE)
        first_gain = vec[0:1]
        x = x_tile[t % 2].astype(F32)
        dn1 = back_product(right2[rows, 0:WDFG], wdfg_buf[...])
        p = lax.rsqrt(jnp.mean(x * x, axis=1, keepdims=True) + norm_eps)
        scaled = x * p
        mean = jnp.mean(dn1 * scaled * first_gain, axis=1, keepdims=True)
        dm_tile[t % 3] += p * (first_gain * dn1 - scaled * mean)
        copy = pltpu.make_async_copy(dm_tile.at[t % 3], hidden_grad.at[rows], tile_sems.at[2, t % 3])
        copy.start()
        outgoing[t] = copy

    steps = Steps()
    last = None

    def job(run, cost, k=None):
        nonlocal last
        last = steps.add(run, [] if last is None else [last], cost)
        if k is not None:
            scatter.schedule(steps, k, last)

    def tiled(run, cost):
        for t in range(count):
            job(functools.partial(run, t), cost)

    for i in range(2):
        job(functools.partial(down, i), 2.5, i)
    for i in range(4):
        job(functools.partial(gate_up, i), 2.5, 2 + i)
    job(mixout, 2.5, 6)
    tiled(unmix, 1.1)
    job(reverse, 4.5)
    tiled(gates, 0.4)
    job(drive, 2.5, 7)
    job(outgate, 2.5, 8)
    job(forget, 2.5, 9)
    tiled(inputs, 1.1)
    steps.run(256, *SCATTER_RATES)
    for t in (count - 2, count - 1):
        outgoing[t].wait()
    scatter.sends.finish()


def scan_backward(length, lam, states, ds, cos, sin, carry, vec_sums):
    steps = length // SEGMENTS
    zero = jnp.zeros((SEGMENTS, 128), F32)

    def rows(j):
        return pl.ds(j, SEGMENTS, stride=steps)

    def first(i, kept):
        j = steps - 1 - i
        prod, re, im = kept
        new_p, new_re, new_im = [], [], []
        for c in range(CB):
            gate = lam[c, rows(j)]
            g_re, g_im = ds[c, rows(j)] + re[c], ds[CB + c, rows(j)] + im[c]
            new_p.append(prod[c] * gate)
            new_re.append(gate * (cos[:, col(c)] * g_re + sin[:, col(c)] * g_im))
            new_im.append(gate * (cos[:, col(c)] * g_im - sin[:, col(c)] * g_re))
        return tuple(new_p), tuple(new_re), tuple(new_im)

    ones = (jnp.ones((SEGMENTS, 128), F32),) * CB
    prod, re, im = lax.fori_loop(0, steps, first, (ones, (zero,) * CB, (zero,) * CB))
    turn_re, turn_im = turned(cos, -sin, steps)
    for c in range(CB):
        p_re, p_im = prod[c] * turn_re[:, col(c)], prod[c] * turn_im[:, col(c)]
        at_re = at_im = jnp.zeros((1, 128), F32)
        for k in reversed(range(SEGMENTS)):
            carry[c, k : k + 1] = at_re
            carry[CB + c, k : k + 1] = at_im
            row = slice(k, k + 1)
            at_re, at_im = (
                p_re[row] * at_re - p_im[row] * at_im + re[c][row],
                p_re[row] * at_im + p_im[row] * at_re + im[c][row],
            )
    for c in range(NB):
        states[c, 0:8] = jnp.zeros((8, 128), F32)

    def step(at_rows, before, kept):
        re, im, phase = kept
        new_re, new_im, new_phase = [], [], []
        for c in range(CB):
            gate = lam[c, at_rows]
            g_re, g_im = ds[c, at_rows] + re[c], ds[CB + c, at_rows] + im[c]
            w_re = cos[:, col(c)] * g_re + sin[:, col(c)] * g_im
            w_im = cos[:, col(c)] * g_im - sin[:, col(c)] * g_re
            new_re.append(gate * w_re)
            new_im.append(gate * w_im)
            s_re, s_im = before(c), before(CB + c)
            new_phase.append(phase[c] + gate * (w_im * s_re - w_re * s_im))
            ds[c, at_rows] = g_re
            ds[CB + c, at_rows] = g_im
            yield c, w_re * s_re + w_im * s_im
        kept[:] = [tuple(new_re), tuple(new_im), tuple(new_phase)]

    opening_rows = [states[c, pl.ds(7, SEGMENTS, stride=steps)] for c in range(NB)]

    def second(i, kept):
        j = steps - 1 - i
        kept = list(kept)
        for c, dgate in step(rows(j), lambda c: states[c, pl.ds(j + 7, SEGMENTS, stride=steps)], kept):
            states[c, pl.ds(j + 8, SEGMENTS, stride=steps)] = dgate
        return tuple(kept)

    start = (tuple(carry[c] for c in range(CB)), tuple(carry[CB + c] for c in range(CB)), (zero,) * CB)
    kept = list(lax.fori_loop(0, steps - 1, second, start))
    for c, dgate in step(rows(0), lambda c: opening_rows[c], kept):
        states[c, pl.ds(8, SEGMENTS, stride=steps)] = dgate
    for c in range(CB):
        vec_sums[1:2, col(c)] = jnp.sum(kept[2][c], axis=0, keepdims=True)


def closing(length, arrays, hidden, dmiddle, wdfg, wo, vec, sums):
    vmem = pl.BlockSpec(memory_space=pltpu.VMEM)
    hbm = pl.BlockSpec(memory_space=pl.ANY)
    dma = pltpu.SemaphoreType.DMA
    scratch = [
        ((length, FF), BF16), ((length, D), BF16), ((length, D), BF16), ((length, 2 * FF), BF16),
        ((NB, length + 8, 128), F32), ((NB, length, 128), F32), ((CB, length, 128), F32), ((D, WDFG), BF16), ((D, D), BF16),
        ((2, TILE, D), BF16), ((3, TILE, D), F32), ((NB, SEGMENTS, 128), F32), ((32, 128), F32), ((8, D), F32),
        ((D, 128), F32), ((256, D), BF16), ((D, 128), BF16),
        ((2, 16, ROWS, 128), BF16), ((16, ROWS, 128), BF16), ((17, ROWS, 128), BF16),
    ]
    sems = len(CHUNKS), len(SCATTER_NAMES)
    return pl.pallas_call(
        functools.partial(closing_kernel, length),
        out_shape=[jax.ShapeDtypeStruct((length, D), F32), jax.ShapeDtypeStruct((ROWS, 128), F32)],
        in_specs=[hbm] * 17 + [vmem] * 2,
        out_specs=[hbm, vmem],
        scratch_shapes=[pltpu.VMEM(*s) for s in scratch] + [dma((17,)), dma((3, 3)), dma(sems), dma(sems)],
        compiler_params=pltpu.CompilerParams(collective_id=1, has_side_effects=True, vmem_limit_bytes=63 * MIB),
    )(*arrays, hidden, dmiddle, wdfg, wo, vec, sums)


PIECES = 7


def handing_kernel(grad, packed, grad_out, drive_out, forget_out, outgate_out, mixout_out, gate_out, up_out, down_out, *rest):
    *vector_outs, held, sems = rest
    rows = grad.shape[0] // PIECES
    part = lambda ref, i: ref.at[pl.ds(i * rows, rows)]
    copies = [pltpu.make_async_copy(part(grad, i), part(held, i), sems.at[0, i]) for i in range(PIECES)]
    for copy in copies:
        copy.start()
    for ref, place in (
        (drive_out, DRIVE), (forget_out, FORGET), (outgate_out, OUTGATE), (mixout_out, MIXOUT), (gate_out, GATE), (up_out, UP), (down_out, DOWN)
    ):
        ref[...] = packed[place[0] : place[0] + ref.shape[0]]
    row = packed[VECTORS : VECTORS + 1]
    for ref, (lane, width) in zip(vector_outs, VECTOR_PARTS):
        ref[...] = row[0, lane : lane + width]
    away = [pltpu.make_async_copy(part(held, i), part(grad_out, i), sems.at[1, i]) for i in range(PIECES)]
    for copy, out in zip(copies, away):
        copy.wait()
        out.start()
    for out in away:
        out.wait()


def handing(grad, packed, shards):
    vmem = pl.BlockSpec(memory_space=pltpu.VMEM)
    hbm = pl.BlockSpec(memory_space=pl.ANY)
    shapes = [grad.shape] + [w.shape for w in shards] + [(width,) for _, width in VECTOR_PARTS]
    return pl.pallas_call(
        handing_kernel,
        out_shape=[jax.ShapeDtypeStruct(s, F32) for s in shapes],
        in_specs=[hbm, vmem],
        out_specs=[hbm] + [vmem] * 12,
        scratch_shapes=[pltpu.VMEM(grad.shape, F32), pltpu.SemaphoreType.DMA((2, PIECES))],
        compiler_params=pltpu.CompilerParams(vmem_limit_bytes=63 * MIB),
    )(grad, packed)


def fast(hidden, cotangent, *params):
    weights, parts = params[:7], params[7:]
    n1, pd, pg, lam, states, mixed, normed, rstd, middle, n2, wdfg, wo, wau, wb, vec = opening(hidden, weights, parts)
    out, units, dpau, dm, dmiddle, sums = feed(cotangent, n2, middle, wau, wb, vec)
    arrays = (units, cotangent, n2, dpau, mixed, dm, n1, pg, normed, rstd, states, lam, pd)
    grad, packed = closing(hidden.shape[0], arrays, hidden, dmiddle, wdfg, wo, vec, sums)
    return (out, *handing(grad, packed, weights))


SPAN = 56


def rms_scale(values, gain_vec):
    return (
        values * lax.rsqrt(jnp.mean(values * values, axis=1, keepdims=True) + norm_eps) * gain_vec
    )


def combine(earlier, later_term):
    return (
        later_term[0] * earlier[0] - later_term[1] * earlier[1],
        later_term[0] * earlier[1] + later_term[1] * earlier[0],
        later_term[0] * earlier[2] - later_term[1] * earlier[3] + later_term[2],
        later_term[0] * earlier[3] + later_term[1] * earlier[2] + later_term[3],
    )


def block_prefix(block_terms):
    length = block_terms[0].shape[0]
    width = block_terms[0].shape[1]
    current = block_terms
    offset = 1
    while offset < length:
        filler = (
            jnp.ones((offset, width), jnp.float32),
            jnp.zeros((offset, width), jnp.float32),
            jnp.zeros((offset, width), jnp.float32),
            jnp.zeros((offset, width), jnp.float32),
        )
        earlier = tuple(
            (
                jnp.concatenate([front, member[: length - offset]], axis=0)
                for front, member in zip(filler, current)
            )
        )
        current = combine(earlier, current)
        offset = offset * 2
    return current


def mixer_core(drive_pre, forget_pre, outgate_pre, phase_angle, forget_bias, group_gain):
    length = drive_pre.shape[0]
    features = drive_pre.shape[1]
    channels = features // 2
    blocks = length // SPAN
    driven = jax.nn.silu(drive_pre)
    retain = lower_bound + (1.0 - lower_bound) * jax.nn.sigmoid(forget_pre + forget_bias)
    rotate_re = retain * jnp.cos(phase_angle)
    rotate_im = retain * jnp.sin(phase_angle)
    inflow = 1.0 - retain
    source_re = inflow * driven[:, :channels]
    source_im = inflow * driven[:, channels:]
    pieces = tuple(
        (
            member.reshape(blocks, SPAN, channels)
            for member in (rotate_re, rotate_im, source_re, source_im)
        )
    )

    def advance(carried, block_terms):
        summed = block_prefix(block_terms)
        state_re = summed[0] * carried[0] - summed[1] * carried[1] + summed[2]
        state_im = summed[0] * carried[1] + summed[1] * carried[0] + summed[3]
        return ((state_re[-1], state_im[-1]), (state_re, state_im))

    initial = (jnp.zeros((channels,), jnp.float32), jnp.zeros((channels,), jnp.float32))
    _, (states_re, states_im) = lax.scan(jax.checkpoint(advance), initial, pieces)
    joined = jnp.concatenate(
        [states_re.reshape(length, channels), states_im.reshape(length, channels)], axis=1
    )
    grouped = joined.reshape(length, GROUPS, features // GROUPS)
    centered = grouped - jnp.mean(grouped, axis=2, keepdims=True)
    normed = centered * lax.rsqrt(jnp.mean(centered * centered, axis=2, keepdims=True) + group_eps)
    return normed.reshape(length, features) * group_gain * jax.nn.sigmoid(outgate_pre)


def unpack(gathered):
    targets = ((D, D), (D, C), (D, D), (D, D), (D, FF), (D, FF), (FF, D))
    matrices = tuple(
        (gathered[position].reshape(target) for position, target in enumerate(targets))
    )
    vectors = tuple((member.astype(jnp.float32) for member in gathered[7:]))
    return matrices + vectors


def local(
    hidden,
    cotangent,
    drive_weight,
    forget_weight,
    outgate_weight,
    mixout_weight,
    gate_weight,
    up_weight,
    down_weight,
    first_gain,
    second_gain,
    group_gain,
    forget_bias,
    phase_angle,
):
    params = unpack(
        (
            lax.all_gather(drive_weight, AXES, axis=0, tiled=True),
            lax.all_gather(forget_weight, AXES, axis=0, tiled=True),
            lax.all_gather(outgate_weight, AXES, axis=0, tiled=True),
            lax.all_gather(mixout_weight, AXES, axis=0, tiled=True),
            lax.all_gather(gate_weight, AXES, axis=0, tiled=True),
            lax.all_gather(up_weight, AXES, axis=0, tiled=True),
            lax.all_gather(down_weight, AXES, axis=0, tiled=True),
            lax.all_gather(first_gain, AXES, axis=0, tiled=True),
            lax.all_gather(second_gain, AXES, axis=0, tiled=True),
            lax.all_gather(group_gain, AXES, axis=0, tiled=True),
            lax.all_gather(forget_bias, AXES, axis=0, tiled=True),
            lax.all_gather(phase_angle, AXES, axis=0, tiled=True),
        )
    )
    inputs = hidden.astype(jnp.float32)
    normed_float, pull_first = jax.vjp(rms_scale, inputs, params[7])
    normed_one = normed_float.astype(jnp.bfloat16)
    drive_pre = product(normed_one, params[0])
    forget_pre = product(normed_one, params[1])
    outgate_pre = product(normed_one, params[2])
    mixed_float, pull_mixer = jax.vjp(
        mixer_core, drive_pre, forget_pre, outgate_pre, params[11], params[10], params[9]
    )
    mixed = mixed_float.astype(jnp.bfloat16)
    middle = inputs + product(mixed, params[3])
    second_float, pull_second = jax.vjp(rms_scale, middle, params[8])
    normed_two = second_float.astype(jnp.bfloat16)
    gate_pre = product(normed_two, params[4])
    up_pre = product(normed_two, params[5])
    gate_sig = jax.nn.sigmoid(gate_pre)
    silu_gate = gate_pre * gate_sig
    hidden_units = (silu_gate * up_pre).astype(jnp.bfloat16)
    layer_out = (middle + product(hidden_units, params[6])).astype(jnp.bfloat16)
    back_params = unpack(
        (
            lax.all_gather(drive_weight, AXES, axis=0, tiled=True),
            lax.all_gather(forget_weight, AXES, axis=0, tiled=True),
            lax.all_gather(outgate_weight, AXES, axis=0, tiled=True),
            lax.all_gather(mixout_weight, AXES, axis=0, tiled=True),
            lax.all_gather(gate_weight, AXES, axis=0, tiled=True),
            lax.all_gather(up_weight, AXES, axis=0, tiled=True),
            lax.all_gather(down_weight, AXES, axis=0, tiled=True),
            lax.all_gather(first_gain, AXES, axis=0, tiled=True),
            lax.all_gather(second_gain, AXES, axis=0, tiled=True),
            lax.all_gather(group_gain, AXES, axis=0, tiled=True),
            lax.all_gather(forget_bias, AXES, axis=0, tiled=True),
            lax.all_gather(phase_angle, AXES, axis=0, tiled=True),
        )
    )
    units_back = back_product(cotangent, back_params[6])
    down_grad = outer_sum(hidden_units, cotangent)
    slope = gate_sig * (1.0 + gate_pre * (1.0 - gate_sig))
    gate_back = (units_back * up_pre * slope).astype(jnp.bfloat16)
    up_back = (units_back * silu_gate).astype(jnp.bfloat16)
    gate_grad = outer_sum(normed_two, gate_back)
    up_grad = outer_sum(normed_two, up_back)
    second_back = back_product(gate_back, back_params[4]) + back_product(up_back, back_params[5])
    middle_part, secondgain_grad = pull_second(second_back)
    middle_back = cotangent.astype(jnp.float32) + middle_part
    middle_low = middle_back.astype(jnp.bfloat16)
    mixout_grad = outer_sum(mixed, middle_low)
    mixed_back = back_product(middle_low, back_params[3])
    drive_back, forget_back, outgate_back, phase_grad, bias_grad, groupgain_grad = pull_mixer(
        mixed_back
    )
    drive_low = drive_back.astype(jnp.bfloat16)
    forget_low = forget_back.astype(jnp.bfloat16)
    outgate_low = outgate_back.astype(jnp.bfloat16)
    drive_grad = outer_sum(normed_one, drive_low)
    forget_grad = outer_sum(normed_one, forget_low)
    outgate_grad = outer_sum(normed_one, outgate_low)
    first_back = (
        back_product(drive_low, back_params[0])
        + back_product(forget_low, back_params[1])
        + back_product(outgate_low, back_params[2])
    )
    input_part, firstgain_grad = pull_first(first_back)
    hidden_grad = middle_back + input_part
    all_terms = (
        drive_grad.reshape(-1, 128),
        forget_grad.reshape(-1, 128),
        outgate_grad.reshape(-1, 128),
        mixout_grad.reshape(-1, 128),
        gate_grad.reshape(-1, 128),
        up_grad.reshape(-1, 128),
        down_grad.reshape(-1, 128),
        firstgain_grad,
        secondgain_grad,
        groupgain_grad,
        bias_grad,
        phase_grad,
    )
    sums = (
        lax.psum_scatter(all_terms[0], AXES, scatter_dimension=0, tiled=True),
        lax.psum_scatter(all_terms[1], AXES, scatter_dimension=0, tiled=True),
        lax.psum_scatter(all_terms[2], AXES, scatter_dimension=0, tiled=True),
        lax.psum_scatter(all_terms[3], AXES, scatter_dimension=0, tiled=True),
        lax.psum_scatter(all_terms[4], AXES, scatter_dimension=0, tiled=True),
        lax.psum_scatter(all_terms[5], AXES, scatter_dimension=0, tiled=True),
        lax.psum_scatter(all_terms[6], AXES, scatter_dimension=0, tiled=True),
        lax.psum_scatter(all_terms[7], AXES, scatter_dimension=0, tiled=True),
        lax.psum_scatter(all_terms[8], AXES, scatter_dimension=0, tiled=True),
        lax.psum_scatter(all_terms[9], AXES, scatter_dimension=0, tiled=True),
        lax.psum_scatter(all_terms[10], AXES, scatter_dimension=0, tiled=True),
        lax.psum_scatter(all_terms[11], AXES, scatter_dimension=0, tiled=True),
    )
    return (
        layer_out,
        hidden_grad,
        sums[0],
        sums[1],
        sums[2],
        sums[3],
        sums[4],
        sums[5],
        sums[6],
        sums[7],
        sums[8],
        sums[9],
        sums[10],
        sums[11],
    )


def solution(mesh):
    rows, flat = P(AXES, None), P(AXES)
    step = fast if tuple(mesh.shape[a] for a in AXES) == (4, 8) else local
    return jax.shard_map(
        step, mesh=mesh, in_specs=(rows,) * 9 + (flat,) * 5, out_specs=(rows,) * 9 + (flat,) * 5, check_vma=False
    )
```
